32 devices in a mesh: groups: 2 (over y), batch: 4 (over z), pair: 2 (over x), orb: 2 (over core).
Axes of the slice: x: 2, y: 2, z: 4, core: 2. Of those that a mesh axis runs over, the one named last changes fastest.
Arguments:
- basis_values: bfloat16 [64, 256, 512], P(('groups', 'batch', 'pair')), parts along dimension 0, may hold values from -6 to 6
- point_weights: float32 [64, 256], P(('groups', 'batch', 'pair')), parts along dimension 0, may hold values from 0.005 to 0.05
- slot_ids: int32 [64, 8, 8], P(('groups', 'batch', 'pair'), None, 'orb'), parts along dimension 0, may hold values from 0 to 63, as said below
- fetch_rows: int32 [16, 2, 8, 8], P(('groups', 'batch', 'pair'), 'orb'), parts along dimension 0, may hold values from 0 to 15, as said below
- density_blocks: bfloat16 [256, 4096], P(('groups', 'batch', 'pair')), parts along dimension 0, may hold values from -0.01171875 to 0.01171875
- core_blocks: bfloat16 [256, 4096], P(('groups', 'batch', 'pair')), parts along dimension 0, may hold values from -3 to 3
Outputs:
- kohn_sham: float32 [256, 4096], P(('groups', 'batch', 'pair')), parts along dimension 0
The draws below stay inside these ranges and needn't reach their ends.
There are 2 independent parts, one for each index of `groups`. The reference program is written for one: setup_inputs(seed, part) draws one part's arguments, and reference() takes and returns one part's arrays. A program takes and returns all parts, laid end to end along the dimension named above; each array names one. Nothing has to cross between parts.
Inputs may be any that keep to these rules, and one draw needn't show every extreme that they name: `fetch_rows`: within one share the 32 slots named by slot_ids name distinct stored rows; the 8 rows of one owner in one share's table are distinct. `slot_ids`: each share's entries name exactly 32 distinct slots of its table; one owner has all 8 of its slots named in every share.
All inputs are finite; a program needn't handle non-finite values.
Results may differ from the reference program's by a relative error of at most 0.004.
Values may be sent and summed in bfloat16 or wider, within the bound.
No kernel may reach another device: no remote copies, remote signals or barrier semaphores. Data moves between devices by JAX's collectives and lax.ppermute only.
A program may use at most 64 MiB of HBM per device.

```python
import math
import jax
import jax.numpy as jnp
from jax import lax

PTS = 256
GO = 64
K = 8
BATCH_DEV = 4
PB_DEV = 16
OWNERS = 8
BATCHES = 32
BLOCKS = 128
CAP = 8
POOL = 32
N_ORB = 2


def draw_fetch_rows(key, part):
    key = jax.random.fold_in(key, 11)
    base = jax.random.randint(key, (OWNERS, N_ORB, OWNERS, 1), 0, PB_DEV).astype(jnp.int32)
    steps = jnp.arange(CAP, dtype=jnp.int32)[None, None, None, :]
    return ((base + steps) % PB_DEV).astype(jnp.int32)


def draw_slot_ids(key, part):
    key = jax.random.fold_in(key, 7)
    own_cols = K // N_ORB
    entries = BATCH_DEV * K * own_cols
    shares = OWNERS * N_ORB
    hot_key, order_key = jax.random.split(key)
    hottest = jax.random.randint(hot_key, (), 0, OWNERS).astype(jnp.int32)
    slot_index = jnp.arange(OWNERS * CAP, dtype=jnp.int32)
    slot_owner = slot_index // CAP

    def one_share(share_key):
        first_key, second_key, third_key = jax.random.split(share_key, 3)
        ranks = jax.random.permutation(first_key, OWNERS * CAP).astype(jnp.int32)
        ranks = jnp.where(slot_owner == hottest, -1, ranks)
        ranks = jnp.where(slot_index == OWNERS * CAP - 1, -2, ranks)
        picked = jnp.argsort(ranks, stable=True)[:POOL].astype(jnp.int32)
        cover = jnp.arange(entries, dtype=jnp.int32) % POOL
        extra = jax.random.randint(second_key, (entries,), 0, POOL).astype(jnp.int32)
        choose = jnp.where(jnp.arange(entries, dtype=jnp.int32) < POOL, cover, extra)
        chosen = picked[choose]
        return chosen[jax.random.permutation(third_key, entries)]
    chosen = jax.vmap(one_share)(jax.random.split(order_key, shares))
    ids = chosen.reshape(OWNERS, N_ORB, BATCH_DEV, K, own_cols).transpose(0, 2, 3, 1, 4)
    return ids.reshape(OWNERS * BATCH_DEV, K, K).astype(jnp.int32)


def level_of(rng, shape, cuts, least, top_value):
    level, own = 1.0, jax.random.fold_in(rng, 6)
    for axis_at, blocks in cuts:
        steps = jnp.exp(jax.random.uniform(jax.random.fold_in(own, axis_at), (blocks,), jnp.float32, least / len(cuts), top_value / len(cuts)))
        level = level * jnp.repeat(steps, shape[axis_at] // blocks).reshape([-1 if axis == axis_at else 1 for axis in range(len(shape))])
    return level


def bell_draw(stream_key, dims, spread, bound, cuts=(), kind=jnp.bfloat16):
    factor_of = level_of(stream_key, dims, cuts, -0.22, 0.18) if cuts else 1.0
    array = jax.random.normal(stream_key, dims, jnp.float32) * spread * factor_of
    return jnp.minimum(jnp.maximum(array, -bound), bound).astype(kind)


def setup_inputs(seed: int = 0, part: int = 0) -> dict:
    streams_of = jax.random.split(jax.random.key(seed), 7)
    part_splits = jax.random.split(jax.random.fold_in(streams_of[6], part), 7)
    return {
        "basis_values": bell_draw(part_splits[0], (BATCHES, PTS, K * GO), 1.0, 6.0, ((0, 8),)),
        "point_weights": jnp.clip(jnp.exp(math.log(0.05) - 2.3025851 * jax.random.uniform(part_splits[1], (BATCHES, PTS), jnp.float32) ** level_of(part_splits[1], (BATCHES, PTS), ((0, 8),), -0.2, 0.2)), 0.005, 0.05),
        "slot_ids": draw_slot_ids(jax.random.fold_in(jax.random.fold_in(streams_of[6], part), 71), part),
        "fetch_rows": draw_fetch_rows(jax.random.fold_in(jax.random.fold_in(streams_of[6], part), 71), part),
        "density_blocks": bell_draw(part_splits[4], (BLOCKS, GO * GO), ((K * GO) ** 2) ** -0.5, 0.01171875, ((0, 8),)),
        "core_blocks": bell_draw(part_splits[5], (BLOCKS, GO * GO), 0.5, 3.0, ((0, 8),)),
    }


def reference(basis_values, point_weights, slot_ids, fetch_rows, density_blocks, core_blocks):
    own = K // N_ORB
    owner_base = (jnp.arange(OWNERS, dtype=jnp.int32) * PB_DEV)[:, None]
    half = (jnp.arange(K, dtype=jnp.int32) // own).astype(jnp.int32)
    half_grid = jnp.broadcast_to(half[None, :], (K, K))

    def device_step(total, inputs):
        values_g, weight_g, slots_g, fetch_g = inputs
        rows_g = (fetch_g + owner_base[None, :, :]).reshape(N_ORB, OWNERS * CAP).astype(jnp.int32)

        def batch_step(acc, inner):
            values_bf, weight, slots = inner
            rows = rows_g[half_grid, slots].astype(jnp.int32)
            dense = density_blocks[rows.reshape(-1)].astype(jnp.float32).reshape(K, K, GO, GO)
            dense = dense.transpose(0, 2, 1, 3).reshape(K * GO, K * GO)
            values = values_bf.astype(jnp.float32)
            product = jnp.dot(values, dense, precision=lax.Precision.HIGHEST)
            density = jnp.sum(product * values, axis=1)
            potential = weight * jnp.tanh(density)
            weighted = lax.optimization_barrier((values * potential[:, None]).astype(jnp.bfloat16))
            hamil = jnp.dot(values.T, weighted.astype(jnp.float32), precision=lax.Precision.HIGHEST)
            pieces = hamil.reshape(K, GO, K, GO).transpose(0, 2, 1, 3)
            acc = acc.at[half_grid, slots].add(pieces.reshape(K, K, GO * GO))
            return acc, None

        start = jnp.zeros((N_ORB, OWNERS * CAP, GO * GO), jnp.float32)
        acc, _ = lax.scan(batch_step, start, (values_g, weight_g, slots_g))
        sent = lax.optimization_barrier(acc.astype(jnp.bfloat16)).astype(jnp.float32)
        total = total.at[rows_g.reshape(-1)].add(sent.reshape(N_ORB * OWNERS * CAP, GO * GO))
        return total, None

    inputs = (basis_values.reshape(OWNERS, BATCH_DEV, PTS, K * GO),
              point_weights.reshape(OWNERS, BATCH_DEV, PTS),
              slot_ids.reshape(OWNERS, BATCH_DEV, K, K),
              fetch_rows)
    start = jnp.zeros((BLOCKS, GO * GO), jnp.float32)
    total, _ = lax.scan(device_step, start, inputs)
    return core_blocks.astype(jnp.float32) + total
```

```python
import functools

import jax
import jax.numpy as jnp
from jax import lax
from jax.experimental import pallas as pl
from jax.experimental.pallas import tpu as pltpu
from jax.sharding import PartitionSpec as P

GO = 64
VMEM_LIMIT = 50 * 1024 * 1024
NT = (((1,), (1,)), ((), ()))


def split_dot(left, right, dims=None):
    if dims is None:
        return jnp.dot(left, right, preferred_element_type=jnp.float32)
    return lax.dot_general(left, right, dims, preferred_element_type=jnp.float32)


def prepare_kernel(half_ref, rows_ref, values_ref, left_ref, left_t_ref, pick_ref, put_ref):
    batches, points, columns = values_ref.shape
    groups = columns // GO
    kept = left_ref.shape[2]
    per_half = kept // groups
    first = half_ref[0] * per_half
    at = lax.broadcasted_iota(jnp.int32, (kept, columns), 0)
    lane = lax.broadcasted_iota(jnp.int32, (kept, columns), 1)
    wanted = (at % groups) * GO + first + at // groups
    select = jnp.where(lane == wanted, 1.0, 0.0).astype(jnp.bfloat16)
    for t in range(batches):
        left_ref[t] = split_dot(values_ref[t], select, NT).astype(jnp.bfloat16)
        left_t_ref[t] = split_dot(select, values_ref[t], NT).astype(jnp.bfloat16)
    table_rows, entries = put_ref.shape
    row = lax.broadcasted_iota(jnp.int32, (table_rows, entries), 0)
    hot = jnp.where(row == rows_ref[...], 1.0, 0.0)
    put_ref[...] = hot.astype(jnp.bfloat16)
    pick_ref[...] = hot.T.astype(jnp.bfloat16)


def density_kernel(pieces, *refs):
    piece_refs = refs[:pieces]
    pick_ref, left_ref, values_ref, out_ref, table, dense = refs[pieces:]
    held = piece_refs[0].shape[0]
    batches, points, columns = values_ref.shape
    groups = columns // GO
    for k in range(pieces):
        table[k * held:(k + 1) * held, :] = piece_refs[k][...]
    low = lax.broadcasted_iota(jnp.int32, (1, 1, groups, 128), 3) < GO
    for j in range(table.shape[1] // 128):
        lanes = slice(j * 128, (j + 1) * 128)
        got = split_dot(pick_ref[...], table[:, lanes])
        got = got.reshape(batches, groups // 2, 2, groups, 128)
        even, odd = got[:, :, 0], got[:, :, 1]
        first = jnp.where(low, even, pltpu.roll(odd, GO, 3))
        second = jnp.where(low, pltpu.roll(even, GO, 3), odd)
        for t in range(batches):
            for q in range(groups // 2):
                both = jnp.concatenate([first[t, q], second[t, q]], axis=0)
                dense[t, j * 2 * groups:(j + 1) * 2 * groups, q * 128:(q + 1) * 128] = both.astype(jnp.bfloat16)
    for t in range(batches):
        product = split_dot(left_ref[t], dense[t]) * values_ref[t].astype(jnp.float32)
        folded = product[:, :128]
        for q in range(1, columns // 128):
            folded = folded + product[:, q * 128:(q + 1) * 128]
        out_ref[t:t + 1, :] = jnp.sum(folded.T, axis=0, keepdims=True)


def scatter_kernel(pieces, *refs):
    mine_ref, other_ref, weight_ref, values_ref, left_t_ref, put_ref = refs[:6]
    out_refs = refs[6:6 + pieces]
    high, rest = refs[6 + pieces:]
    held = out_refs[0].shape[0]
    batches, points, columns = values_ref.shape
    groups = columns // GO
    kept = left_t_ref.shape[1]
    steps = kept // (2 * groups)
    potential = weight_ref[...] * jnp.tanh(mine_ref[...] + other_ref[...])
    low = lax.broadcasted_iota(jnp.int32, (1, groups, 128), 2) < GO
    for t in range(batches):
        factor = jnp.broadcast_to(potential[t:t + 1, :], (128, points)).T
        factor = jnp.concatenate([factor] * (columns // 128), axis=1)
        weighted = (values_ref[t].astype(jnp.float32) * factor).astype(jnp.bfloat16)
        part = split_dot(left_t_ref[t], weighted)
        for q in range(groups // 2):
            cut = part[:, q * 128:(q + 1) * 128].reshape(steps, 2, groups, 128)
            first, second = cut[:, 0], cut[:, 1]
            even = jnp.where(low, first, pltpu.roll(second, GO, 2))
            odd = jnp.where(low, pltpu.roll(first, GO, 2), second)
            at = (t * groups + 2 * q) * groups
            for j in range(steps):
                both = jnp.concatenate([even[j], odd[j]], axis=0)
                top = both.astype(jnp.bfloat16)
                high[at:at + 2 * groups, j * 128:(j + 1) * 128] = top
                rest[at:at + 2 * groups, j * 128:(j + 1) * 128] = (both - top.astype(jnp.float32)).astype(jnp.bfloat16)
    step = max(1, min(pieces, 128 // held))
    for k in range(0, pieces, step):
        some = put_ref[k * held:(k + step) * held, :]
        total = split_dot(some, high[...]) + split_dot(some, rest[...])
        for i in range(step):
            out_refs[k + i][...] = total[i * held:(i + 1) * held, :].astype(jnp.bfloat16)


def sum_kernel(*refs):
    out_ref = refs[-1]
    total = refs[0][...].astype(jnp.float32)
    for ref in refs[1:-1]:
        total = total + ref[...].astype(jnp.float32)
    out_ref[...] = total.astype(out_ref.dtype)


def finish_kernel(half_ref, mine_ref, other_ref, core_ref, out_ref):
    wide = mine_ref.shape[1]
    own = pl.multiple_of(half_ref[0] * wide, wide)
    far = pl.multiple_of((1 - half_ref[0]) * wide, wide)
    out_ref[:, pl.ds(own, wide)] = core_ref[:, pl.ds(own, wide)].astype(jnp.float32) + mine_ref[...]
    out_ref[:, pl.ds(far, wide)] = core_ref[:, pl.ds(far, wide)].astype(jnp.float32) + other_ref[...]


def call(kernel, outs, count, scratch=(), scalar=False, flops=0, moved=0):
    specs = [pl.BlockSpec(memory_space=pltpu.VMEM)] * count
    if scalar:
        specs = [pl.BlockSpec(memory_space=pltpu.SMEM)] + specs
    out_specs = jax.tree.map(lambda _: pl.BlockSpec(memory_space=pltpu.VMEM), outs)
    return pl.pallas_call(
        kernel,
        out_shape=outs,
        in_specs=specs,
        out_specs=out_specs,
        scratch_shapes=list(scratch),
        compiler_params=pltpu.CompilerParams(vmem_limit_bytes=VMEM_LIMIT),
        cost_estimate=pl.CostEstimate(flops=flops, bytes_accessed=moved, transcendentals=0),
    )


def from_ahead(array, axis, count, step):
    return lax.ppermute(array, axis, [((i + step) % count, i) for i in range(count)])


def to_ahead(array, axis, count, step):
    return lax.ppermute(array, axis, [(i, (i + step) % count) for i in range(count)])


def per_device(basis_values, point_weights, slot_ids, fetch_rows, density_blocks, core_blocks):
    rows_z, rows_x = lax.axis_size("batch"), lax.axis_size("pair")
    z, x, half = lax.axis_index("batch"), lax.axis_index("pair"), lax.axis_index("orb")
    owners = rows_z * rows_x
    batches, points, columns = basis_values.shape
    groups, own_groups = slot_ids.shape[1], slot_ids.shape[2]
    held, square = density_blocks.shape
    capacity = fetch_rows.shape[3]
    wide = square // 2
    table_rows = owners * held
    entries = batches * groups * groups
    kept = columns // 2
    bf16, f32 = jnp.bfloat16, jnp.float32

    owner = jnp.arange(owners, dtype=jnp.int32)
    ahead = ((owner // rows_x - z) % rows_z) * rows_x + (owner % rows_x - x) % rows_x
    home = (ahead[:, None] * held + fetch_rows.reshape(owners, capacity)).reshape(-1)
    slots = jnp.arange(owners * capacity, dtype=jnp.int32)
    own_rows = jnp.sum(jnp.where(slot_ids[..., None] == slots, home, 0), axis=-1)
    own_rows = own_rows.transpose(0, 2, 1).astype(jnp.int32)
    other_rows = lax.ppermute(own_rows, "orb", [(0, 1), (1, 0)])
    rows = jnp.concatenate(
        [jnp.where(half == 0, own_rows, other_rows), jnp.where(half == 0, other_rows, own_rows)], axis=1
    ).reshape(1, entries)
    half_at = half.reshape(1).astype(jnp.int32)

    mine = lax.dynamic_slice_in_dim(density_blocks, half * wide, wide, 1)
    pieces = []
    for dz in range(rows_z):
        base = mine if dz == 0 else from_ahead(mine, "batch", rows_z, dz)
        pieces.append(base)
        for dx in range(1, rows_x):
            pieces.append(from_ahead(base, "pair", rows_x, dx))
    count = len(pieces)

    left, left_t, pick, put = call(
        prepare_kernel,
        (
            jax.ShapeDtypeStruct((batches, points, kept), bf16),
            jax.ShapeDtypeStruct((batches, kept, points), bf16),
            jax.ShapeDtypeStruct((entries, table_rows), bf16),
            jax.ShapeDtypeStruct((table_rows, entries), bf16),
        ),
        2,
        scalar=True,
        flops=4 * batches * points * columns * kept,
        moved=3 * batches * points * columns * 2,
    )(half_at, rows, basis_values)

    partial = call(
        functools.partial(density_kernel, count),
        jax.ShapeDtypeStruct((batches, points), f32),
        count + 3,
        scratch=(pltpu.VMEM((table_rows, wide), bf16), pltpu.VMEM((batches, kept, columns), bf16)),
        flops=2 * batches * points * columns * kept,
        moved=2 * batches * points * columns * 2,
    )(*pieces, pick, left, basis_values)
    partial_other = lax.ppermute(partial, "orb", [(0, 1), (1, 0)])

    sums = call(
        functools.partial(scatter_kernel, count),
        [jax.ShapeDtypeStruct((held, wide), bf16)] * count,
        6,
        scratch=(pltpu.VMEM((entries, wide), bf16), pltpu.VMEM((entries, wide), bf16)),
        flops=2 * batches * points * columns * kept,
        moved=2 * batches * points * columns * 2,
    )(partial, partial_other, point_weights, basis_values, left_t, put)

    landed = []
    for dz in range(rows_z - 1, -1, -1):
        terms = [sums[dz * rows_x]]
        for dx in range(1, rows_x):
            terms.append(to_ahead(sums[dz * rows_x + dx], "pair", rows_x, dx))
        if dz == 0:
            landed.extend(terms)
            continue
        joined = terms[0].astype(f32)
        for term in terms[1:]:
            joined = joined + term.astype(f32)
        landed.append(to_ahead(joined.astype(bf16), "batch", rows_z, dz))
    total = call(
        sum_kernel, jax.ShapeDtypeStruct((held, wide), f32), len(landed), moved=len(landed) * held * wide * 2
    )(*landed)
    total_other = lax.ppermute(total, "orb", [(0, 1), (1, 0)])
    return call(
        finish_kernel, jax.ShapeDtypeStruct((held, square), f32), 3, scalar=True, moved=held * square * 12
    )(half_at, total, total_other, core_blocks)


def solution(mesh):
    placed = (
        P(("groups", "batch", "pair"), None, None),
        P(("groups", "batch", "pair"), None),
        P(("groups", "batch", "pair"), None, "orb"),
        P(("groups", "batch", "pair"), "orb", None, None),
        P(("groups", "batch", "pair"), None),
        P(("groups", "batch", "pair"), None),
    )
    return jax.shard_map(
        per_device,
        mesh=mesh,
        in_specs=placed,
        out_specs=P(("groups", "batch", "pair"), None),
        check_vma=False,
    )
```

```python
import functools

import jax
import jax.numpy as jnp
from jax import lax
from jax.experimental import pallas as pl
from jax.experimental.pallas import tpu as pltpu
from jax.sharding import PartitionSpec as P

GO = 64
VMEM_LIMIT = 50 * 1024 * 1024
NT = (((1,), (1,)), ((), ()))


def split_dot(left, right, dims=None):
    if dims is None:
        return jnp.dot(left, right, preferred_element_type=jnp.float32)
    return lax.dot_general(left, right, dims, preferred_element_type=jnp.float32)


def prepare_kernel(half_ref, rows_ref, values_ref, left_ref, left_t_ref, pick_ref, put_ref):
    batches, points, columns = values_ref.shape
    groups = columns // GO
    kept = left_ref.shape[2]
    per_half = kept // groups
    first = half_ref[0] * per_half
    at = lax.broadcasted_iota(jnp.int32, (kept, columns), 0)
    lane = lax.broadcasted_iota(jnp.int32, (kept, columns), 1)
    wanted = (at % groups) * GO + first + at // groups
    select = jnp.where(lane == wanted, 1.0, 0.0).astype(jnp.bfloat16)
    for t in range(batches):
        left_ref[t] = split_dot(values_ref[t], select, NT).astype(jnp.bfloat16)
        left_t_ref[t] = split_dot(select, values_ref[t], NT).astype(jnp.bfloat16)
    table_rows, entries = put_ref.shape
    row = lax.broadcasted_iota(jnp.int32, (table_rows, entries), 0)
    hot = jnp.where(row == rows_ref[...], 1.0, 0.0)
    put_ref[...] = hot.astype(jnp.bfloat16)
    pick_ref[...] = hot.T.astype(jnp.bfloat16)


def density_kernel(places, *refs):
    piece_refs = refs[:len(places)]
    pick_ref, left_ref, values_ref, out_ref, table, dense = refs[len(places):]
    batches, points, columns = values_ref.shape
    groups = columns // GO
    for ref, blocks in zip(piece_refs, places):
        held = ref.shape[0] // len(blocks)
        for i, k in enumerate(blocks):
            table[k * held:(k + 1) * held, :] = ref[i * held:(i + 1) * held, :]
    low = lax.broadcasted_iota(jnp.int32, (1, 1, groups, 128), 3) < GO
    for j in range(table.shape[1] // 128):
        lanes = slice(j * 128, (j + 1) * 128)
        got = split_dot(pick_ref[...], table[:, lanes])
        got = got.reshape(batches, groups // 2, 2, groups, 128)
        even, odd = got[:, :, 0], got[:, :, 1]
        first = jnp.where(low, even, pltpu.roll(odd, GO, 3))
        second = jnp.where(low, pltpu.roll(even, GO, 3), odd)
        for t in range(batches):
            for q in range(groups // 2):
                both = jnp.concatenate([first[t, q], second[t, q]], axis=0)
                dense[t, j * 2 * groups:(j + 1) * 2 * groups, q * 128:(q + 1) * 128] = both.astype(jnp.bfloat16)
    for t in range(batches):
        product = split_dot(left_ref[t], dense[t]) * values_ref[t].astype(jnp.float32)
        folded = product[:, :128]
        for q in range(1, columns // 128):
            folded = folded + product[:, q * 128:(q + 1) * 128]
        out_ref[t:t + 1, :] = jnp.sum(folded.T, axis=0, keepdims=True)


def scatter_kernel(places, *refs):
    mine_ref, other_ref, weight_ref, values_ref, left_t_ref, put_ref = refs[:6]
    out_refs = refs[6:6 + len(places)]
    high, rest = refs[6 + len(places):]
    target = {}
    for ref, blocks in zip(out_refs, places):
        for i, k in enumerate(blocks):
            target[k] = (ref, i)
    pieces = len(target)
    held = put_ref.shape[0] // pieces
    batches, points, columns = values_ref.shape
    groups = columns // GO
    kept = left_t_ref.shape[1]
    steps = kept // (2 * groups)
    potential = weight_ref[...] * jnp.tanh(mine_ref[...] + other_ref[...])
    low = lax.broadcasted_iota(jnp.int32, (1, groups, 128), 2) < GO
    for t in range(batches):
        factor = jnp.broadcast_to(potential[t:t + 1, :], (128, points)).T
        factor = jnp.concatenate([factor] * (columns // 128), axis=1)
        weighted = (values_ref[t].astype(jnp.float32) * factor).astype(jnp.bfloat16)
        part = split_dot(left_t_ref[t], weighted)
        for q in range(groups // 2):
            cut = part[:, q * 128:(q + 1) * 128].reshape(steps, 2, groups, 128)
            first, second = cut[:, 0], cut[:, 1]
            even = jnp.where(low, first, pltpu.roll(second, GO, 2))
            odd = jnp.where(low, pltpu.roll(first, GO, 2), second)
            at = (t * groups + 2 * q) * groups
            for j in range(steps):
                both = jnp.concatenate([even[j], odd[j]], axis=0)
                top = both.astype(jnp.bfloat16)
                high[at:at + 2 * groups, j * 128:(j + 1) * 128] = top
                rest[at:at + 2 * groups, j * 128:(j + 1) * 128] = (both - top.astype(jnp.float32)).astype(jnp.bfloat16)
    step = max(1, min(pieces, 128 // held))
    for k in range(0, pieces, step):
        some = put_ref[k * held:(k + step) * held, :]
        total = split_dot(some, high[...]) + split_dot(some, rest[...])
        for i in range(step):
            ref, at = target[k + i]
            ref[at * held:(at + 1) * held, :] = total[i * held:(i + 1) * held, :].astype(jnp.bfloat16)


def sum_kernel(*refs):
    out_ref = refs[-1]
    total = refs[0][...].astype(jnp.float32)
    for ref in refs[1:-1]:
        total = total + ref[...].astype(jnp.float32)
    out_ref[...] = total.astype(out_ref.dtype)


def finish_kernel(half_ref, mine_ref, other_ref, core_ref, out_ref):
    wide = mine_ref.shape[1]
    own = pl.multiple_of(half_ref[0] * wide, wide)
    far = pl.multiple_of((1 - half_ref[0]) * wide, wide)
    out_ref[:, pl.ds(own, wide)] = core_ref[:, pl.ds(own, wide)].astype(jnp.float32) + mine_ref[...]
    out_ref[:, pl.ds(far, wide)] = core_ref[:, pl.ds(far, wide)].astype(jnp.float32) + other_ref[...]


def call(kernel, outs, count, scratch=(), scalar=False, flops=0, moved=0):
    specs = [pl.BlockSpec(memory_space=pltpu.VMEM)] * count
    if scalar:
        specs = [pl.BlockSpec(memory_space=pltpu.SMEM)] + specs
    out_specs = jax.tree.map(lambda _: pl.BlockSpec(memory_space=pltpu.VMEM), outs)
    return pl.pallas_call(
        kernel,
        out_shape=outs,
        in_specs=specs,
        out_specs=out_specs,
        scratch_shapes=list(scratch),
        compiler_params=pltpu.CompilerParams(vmem_limit_bytes=VMEM_LIMIT),
        cost_estimate=pl.CostEstimate(flops=flops, bytes_accessed=moved, transcendentals=0),
    )


def swap(array, axis, count, step):
    return lax.ppermute(array, axis, [(i, i ^ step) for i in range(count)])


def per_device(basis_values, point_weights, slot_ids, fetch_rows, density_blocks, core_blocks):
    rows_z, rows_x = lax.axis_size("batch"), lax.axis_size("pair")
    z, x, half = lax.axis_index("batch"), lax.axis_index("pair"), lax.axis_index("orb")
    owners = rows_z * rows_x
    batches, points, columns = basis_values.shape
    groups, own_groups = slot_ids.shape[1], slot_ids.shape[2]
    held, square = density_blocks.shape
    capacity = fetch_rows.shape[3]
    wide = square // 2
    table_rows = owners * held
    entries = batches * groups * groups
    kept = columns // 2
    bf16, f32 = jnp.bfloat16, jnp.float32

    upper = list(range(rows_z // 2, rows_z))
    lower = list(range(1, rows_z // 2))
    cut = (len(upper) + 1) // 2
    groups_in = [[0], upper[:cut] + lower, upper[cut:]]
    groups_in = [group for group in groups_in if group]

    mine = lax.dynamic_slice_in_dim(density_blocks, half * wide, wide, 1)
    held_z = {0: mine}
    for dz in upper + lower:
        held_z[dz] = swap(mine, "batch", rows_z, dz)
    arrays, places = [], []
    for dz in [0] + upper + lower:
        arrays.append(held_z[dz])
        places.append([dz * rows_x])
    for group in groups_in:
        sent = jnp.concatenate([held_z[dz] for dz in group], axis=0) if len(group) > 1 else held_z[group[0]]
        for dx in range(1, rows_x):
            arrays.append(swap(sent, "pair", rows_x, dx))
            places.append([dz * rows_x + dx for dz in group])

    slot_ids, fetch_rows, _ = lax.optimization_barrier((slot_ids, fetch_rows, held_z[upper[0]]))
    owner = jnp.arange(owners, dtype=jnp.int32)
    apart = ((owner // rows_x) ^ z) * rows_x + ((owner % rows_x) ^ x)
    home = (apart[:, None] * held + fetch_rows.reshape(owners, capacity)).reshape(-1)
    slots = jnp.arange(owners * capacity, dtype=jnp.int32)
    own_rows = jnp.sum(jnp.where(slot_ids[..., None] == slots, home, 0), axis=-1)
    own_rows = own_rows.transpose(0, 2, 1).astype(jnp.int32)
    other_rows = swap(own_rows, "orb", 2, 1)
    rows = jnp.concatenate(
        [jnp.where(half == 0, own_rows, other_rows), jnp.where(half == 0, other_rows, own_rows)], axis=1
    ).reshape(1, entries)
    half_at = half.reshape(1).astype(jnp.int32)

    left, left_t, pick, put = call(
        prepare_kernel,
        (
            jax.ShapeDtypeStruct((batches, points, kept), bf16),
            jax.ShapeDtypeStruct((batches, kept, points), bf16),
            jax.ShapeDtypeStruct((entries, table_rows), bf16),
            jax.ShapeDtypeStruct((table_rows, entries), bf16),
        ),
        2,
        scalar=True,
        flops=4 * batches * points * columns * kept,
        moved=3 * batches * points * columns * 2,
    )(half_at, rows, basis_values)

    partial = call(
        functools.partial(density_kernel, places),
        jax.ShapeDtypeStruct((batches, points), f32),
        len(arrays) + 3,
        scratch=(pltpu.VMEM((table_rows, wide), bf16), pltpu.VMEM((batches, kept, columns), bf16)),
        flops=2 * batches * points * columns * kept,
        moved=2 * batches * points * columns * 2,
    )(*arrays, pick, left, basis_values)
    partial_other = swap(partial, "orb", 2, 1)

    groups_out = [group for group in (upper[::-1], lower[::-1] + [0]) if group]
    kept_places = [[dz * rows_x] for dz in range(rows_z)]
    sent_places = [[dz * rows_x + dx for dz in group] for group in groups_out for dx in range(1, rows_x)]
    out_places = kept_places + sent_places
    sums = call(
        functools.partial(scatter_kernel, out_places),
        [jax.ShapeDtypeStruct((held * len(blocks), wide), bf16) for blocks in out_places],
        6,
        scratch=(pltpu.VMEM((entries, wide), bf16), pltpu.VMEM((entries, wide), bf16)),
        flops=2 * batches * points * columns * kept,
        moved=2 * batches * points * columns * 2,
    )(partial, partial_other, point_weights, basis_values, left_t, put)
    landed = []
    at = rows_z
    for group in groups_out:
        came = []
        for dx in range(1, rows_x):
            came.append(swap(sums[at], "pair", rows_x, dx))
            at += 1
        for i, dz in enumerate(group):
            terms = [sums[dz]] + [array[i * held:(i + 1) * held] for array in came]
            if dz == 0:
                landed.extend(terms)
                continue
            joined = terms[0].astype(f32)
            for term in terms[1:]:
                joined = joined + term.astype(f32)
            landed.append(swap(joined.astype(bf16), "batch", rows_z, dz))
    total = call(
        sum_kernel, jax.ShapeDtypeStruct((held, wide), f32), len(landed), moved=len(landed) * held * wide * 2
    )(*landed)
    total_other = swap(total, "orb", 2, 1)
    return call(
        finish_kernel, jax.ShapeDtypeStruct((held, square), f32), 3, scalar=True, moved=held * square * 12
    )(half_at, total, total_other, core_blocks)


def solution(mesh):
    placed = (
        P(("groups", "batch", "pair"), None, None),
        P(("groups", "batch", "pair"), None),
        P(("groups", "batch", "pair"), None, "orb"),
        P(("groups", "batch", "pair"), "orb", None, None),
        P(("groups", "batch", "pair"), None),
        P(("groups", "batch", "pair"), None),
    )
    return jax.shard_map(
        per_device,
        mesh=mesh,
        in_specs=placed,
        out_specs=P(("groups", "batch", "pair"), None),
        check_vma=False,
    )
```

```python
import functools

import jax
import jax.numpy as jnp
from jax import lax
from jax.experimental import pallas as pl
from jax.experimental.pallas import tpu as pltpu
from jax.sharding import PartitionSpec as P

GO = 64
VMEM_LIMIT = 50 * 1024 * 1024
NT = (((1,), (1,)), ((), ()))


def split_dot(left, right, dims=None):
    if dims is None:
        return jnp.dot(left, right, preferred_element_type=jnp.float32)
    return lax.dot_general(left, right, dims, preferred_element_type=jnp.float32)


def prepare_kernel(half_ref, values_hbm, left_ref, left_t_ref, values, arrived):
    batches, points, columns = values.shape
    copies = [pltpu.make_async_copy(values_hbm.at[t], values.at[t], arrived.at[t]) for t in range(batches)]
    for copy in copies:
        copy.start()
    groups = columns // GO
    kept = left_ref.shape[2]
    first = half_ref[0] * (kept // groups)
    at = lax.broadcasted_iota(jnp.int32, (kept, columns), 0)
    lane = lax.broadcasted_iota(jnp.int32, (kept, columns), 1)
    wanted = (at % groups) * GO + first + at // groups
    select = jnp.where(lane == wanted, 1.0, 0.0).astype(jnp.bfloat16)
    for t in range(batches):
        copies[t].wait()
        left_ref[t] = split_dot(values[t], select, NT).astype(jnp.bfloat16)
        left_t_ref[t] = split_dot(select, values[t], NT).astype(jnp.bfloat16)


def index_kernel(held, fetch_ref, slots_ref, rows_ref):
    owners, capacity = fetch_ref.shape
    slots = slots_ref[...]
    rows = jnp.zeros(slots.shape, jnp.int32)
    for owner in range(owners):
        for at in range(capacity):
            rows = jnp.where(slots == owner * capacity + at, fetch_ref[owner, at] + owner * held, rows)
    rows_ref[...] = rows


def row_table(place_ref, rows_ref, held, owners):
    rows = lax.bitwise_xor(rows_ref[...], place_ref[0] * held)
    row = lax.broadcasted_iota(jnp.int32, (owners * held, rows.shape[1]), 0)
    return jnp.where(row == rows, 1.0, 0.0)


def density_kernel(places, place_ref, *refs):
    piece_refs = refs[:len(places)]
    rows_ref, left_ref, values_ref, out_ref, table, dense = refs[len(places):]
    batches, points, columns = values_ref.shape
    groups = columns // GO
    held = piece_refs[0].shape[0]
    for ref, k in zip(piece_refs, places):
        table[k * held:(k + 1) * held, :] = ref[...]
    pick = row_table(place_ref, rows_ref, held, len(places)).T.astype(jnp.bfloat16)
    low = lax.broadcasted_iota(jnp.int32, (1, 1, groups, 128), 3) < GO
    for j in range(table.shape[1] // 128):
        lanes = slice(j * 128, (j + 1) * 128)
        got = split_dot(pick, table[:, lanes])
        got = got.reshape(batches, groups // 2, 2, groups, 128)
        even, odd = got[:, :, 0], got[:, :, 1]
        first = jnp.where(low, even, pltpu.roll(odd, GO, 3))
        second = jnp.where(low, pltpu.roll(even, GO, 3), odd)
        for t in range(batches):
            for q in range(groups // 2):
                both = jnp.concatenate([first[t, q], second[t, q]], axis=0)
                dense[t, j * 2 * groups:(j + 1) * 2 * groups, q * 128:(q + 1) * 128] = both.astype(jnp.bfloat16)
    for t in range(batches):
        product = split_dot(left_ref[t], dense[t]) * values_ref[t].astype(jnp.float32)
        folded = product[:, :128]
        for q in range(1, columns // 128):
            folded = folded + product[:, q * 128:(q + 1) * 128]
        out_ref[t:t + 1, :] = jnp.sum(folded.T, axis=0, keepdims=True)


def scatter_kernel(place_ref, *refs):
    mine_ref, other_ref, weight_ref, values_ref, left_t_ref, rows_ref = refs[:6]
    out_refs = refs[6:-2]
    high, rest = refs[-2:]
    pieces = len(out_refs)
    held = out_refs[0].shape[0]
    put = row_table(place_ref, rows_ref, held, pieces).astype(jnp.bfloat16)
    batches, points, columns = values_ref.shape
    groups = columns // GO
    kept = left_t_ref.shape[1]
    steps = kept // (2 * groups)
    potential = weight_ref[...] * jnp.tanh(mine_ref[...] + other_ref[...])
    low = lax.broadcasted_iota(jnp.int32, (1, groups, 128), 2) < GO
    for t in range(batches):
        factor = jnp.broadcast_to(potential[t:t + 1, :], (128, points)).T
        factor = jnp.concatenate([factor] * (columns // 128), axis=1)
        weighted = (values_ref[t].astype(jnp.float32) * factor).astype(jnp.bfloat16)
        part = split_dot(left_t_ref[t], weighted)
        for q in range(groups // 2):
            cut = part[:, q * 128:(q + 1) * 128].reshape(steps, 2, groups, 128)
            first, second = cut[:, 0], cut[:, 1]
            even = jnp.where(low, first, pltpu.roll(second, GO, 2))
            odd = jnp.where(low, pltpu.roll(first, GO, 2), second)
            at = (t * groups + 2 * q) * groups
            for j in range(steps):
                both = jnp.concatenate([even[j], odd[j]], axis=0)
                top = both.astype(jnp.bfloat16)
                high[at:at + 2 * groups, j * 128:(j + 1) * 128] = top
                rest[at:at + 2 * groups, j * 128:(j + 1) * 128] = (both - top.astype(jnp.float32)).astype(jnp.bfloat16)
    step = max(1, min(pieces, 128 // held))
    for k in range(0, pieces, step):
        some = put[k * held:(k + step) * held, :]
        total = split_dot(some, high[...]) + split_dot(some, rest[...])
        for i in range(step):
            out_refs[k + i][...] = total[i * held:(i + 1) * held, :].astype(jnp.bfloat16)


def sum_kernel(*refs):
    out_ref = refs[-1]
    total = refs[0][...].astype(jnp.float32)
    for ref in refs[1:-1]:
        total = total + ref[...].astype(jnp.float32)
    out_ref[...] = total.astype(out_ref.dtype)


def finish_kernel(half_ref, mine_ref, other_ref, core_ref, out_ref):
    wide = mine_ref.shape[1]
    own = pl.multiple_of(half_ref[0] * wide, wide)
    far = pl.multiple_of((1 - half_ref[0]) * wide, wide)
    out_ref[:, pl.ds(own, wide)] = core_ref[:, pl.ds(own, wide)].astype(jnp.float32) + mine_ref[...]
    out_ref[:, pl.ds(far, wide)] = core_ref[:, pl.ds(far, wide)].astype(jnp.float32) + other_ref[...]


def call(kernel, outs, count, scratch=(), scalar=False, flops=0, moved=0, space=pltpu.VMEM):
    specs = [pl.BlockSpec(memory_space=space)] * count
    if scalar:
        specs = [pl.BlockSpec(memory_space=pltpu.SMEM)] + specs
    out_specs = jax.tree.map(lambda _: pl.BlockSpec(memory_space=pltpu.VMEM), outs)
    return pl.pallas_call(
        kernel,
        out_shape=outs,
        in_specs=specs,
        out_specs=out_specs,
        scratch_shapes=list(scratch),
        compiler_params=pltpu.CompilerParams(vmem_limit_bytes=VMEM_LIMIT),
        cost_estimate=pl.CostEstimate(flops=flops, bytes_accessed=moved, transcendentals=0),
    )


def swap(array, axis, count, step):
    return lax.ppermute(array, axis, [(i, i ^ step) for i in range(count)])


def per_device(basis_values, point_weights, slot_ids, fetch_rows, density_blocks, core_blocks):
    rows_z, rows_x = lax.axis_size("batch"), lax.axis_size("pair")
    z, x, half = lax.axis_index("batch"), lax.axis_index("pair"), lax.axis_index("orb")
    owners = rows_z * rows_x
    batches, points, columns = basis_values.shape
    groups, own_groups = slot_ids.shape[1], slot_ids.shape[2]
    held, square = density_blocks.shape
    capacity = fetch_rows.shape[3]
    wide = square // 2
    table_rows = owners * held
    entries = batches * groups * groups
    kept = columns // 2
    bf16, f32 = jnp.bfloat16, jnp.float32

    far = rows_z // 2
    upper = [dz for dz in range(far + 1, rows_z)]
    lower = [dz for dz in range(1, far)]
    side = list(range(1, rows_x))
    direct = (
        [far * rows_x]
        + [dz * rows_x for dz in upper]
        + [dz * rows_x + dx for dz in upper for dx in side]
        + side
        + [dz * rows_x + dx for dz in lower for dx in [0] + side]
    )
    grid = ("batch", "pair")

    mine = lax.dynamic_slice_in_dim(density_blocks, half * wide, wide, 1)
    pieces = {0: mine}
    for k in reversed(direct):
        pieces[k] = swap(mine, grid, owners, k)
    for dx in side:
        pieces[far * rows_x + dx] = swap(pieces[far * rows_x], "pair", rows_x, dx)
    order = [0] + direct[::-1] + [far * rows_x + dx for dx in side]

    half_at = half.reshape(1).astype(jnp.int32)
    left, left_t = call(
        prepare_kernel,
        (
            jax.ShapeDtypeStruct((batches, points, kept), bf16),
            jax.ShapeDtypeStruct((batches, kept, points), bf16),
        ),
        1,
        scratch=(pltpu.VMEM(basis_values.shape, bf16), pltpu.SemaphoreType.DMA((batches,))),
        scalar=True,
        space=pl.ANY,
        flops=4 * batches * points * columns * kept,
        moved=3 * batches * points * columns * 2,
    )(half_at, basis_values)

    own_rows = pl.pallas_call(
        functools.partial(index_kernel, held),
        out_shape=jax.ShapeDtypeStruct((batches, own_groups, groups), jnp.int32),
        in_specs=[pl.BlockSpec(memory_space=pltpu.SMEM), pl.BlockSpec(memory_space=pltpu.VMEM)],
        out_specs=pl.BlockSpec(memory_space=pltpu.VMEM),
    )(fetch_rows.reshape(owners, capacity), slot_ids.transpose(0, 2, 1))
    other_rows = swap(own_rows, "orb", 2, 1)
    rows = jnp.concatenate(
        [jnp.where(half == 0, own_rows, other_rows), jnp.where(half == 0, other_rows, own_rows)], axis=1
    ).reshape(1, entries)
    place = (z * rows_x + x).reshape(1).astype(jnp.int32)

    partial = call(
        functools.partial(density_kernel, order),
        jax.ShapeDtypeStruct((batches, points), f32),
        owners + 3,
        scalar=True,
        scratch=(pltpu.VMEM((table_rows, wide), bf16), pltpu.VMEM((batches, kept, columns), bf16)),
        flops=2 * batches * points * columns * kept,
        moved=2 * batches * points * columns * 2,
    )(place, *[pieces[k] for k in order], rows, left, basis_values)
    partial_other = swap(partial, "orb", 2, 1)

    sums = call(
        scatter_kernel,
        [jax.ShapeDtypeStruct((held, wide), bf16)] * owners,
        6,
        scalar=True,
        scratch=(pltpu.VMEM((entries, wide), bf16), pltpu.VMEM((entries, wide), bf16)),
        flops=2 * batches * points * columns * kept,
        moved=2 * batches * points * columns * 2,
    )(place, partial, partial_other, point_weights, basis_values, left_t, rows)

    landed = []
    for k in direct[1:]:
        landed.append(swap(sums[k], grid, owners, k))
    joined = sums[far * rows_x].astype(f32)
    for dx in side:
        joined = joined + swap(sums[far * rows_x + dx], "pair", rows_x, dx).astype(f32)
    landed.append(swap(joined.astype(bf16), "batch", rows_z, far))
    landed.append(sums[0])
    total = call(
        sum_kernel, jax.ShapeDtypeStruct((held, wide), f32), len(landed), moved=len(landed) * held * wide * 2
    )(*landed)
    total_other = swap(total, "orb", 2, 1)
    return call(
        finish_kernel, jax.ShapeDtypeStruct((held, square), f32), 3, scalar=True, moved=held * square * 12
    )(half_at, total, total_other, core_blocks)


def solution(mesh):
    placed = (
        P(("groups", "batch", "pair"), None, None),
        P(("groups", "batch", "pair"), None),
        P(("groups", "batch", "pair"), None, "orb"),
        P(("groups", "batch", "pair"), "orb", None, None),
        P(("groups", "batch", "pair"), None),
        P(("groups", "batch", "pair"), None),
    )
    return jax.shard_map(
        per_device,
        mesh=mesh,
        in_specs=placed,
        out_specs=P(("groups", "batch", "pair"), None),
        check_vma=False,
    )
```

```python
import functools

import jax
import jax.numpy as jnp
from jax import lax
from jax.experimental import pallas as pl
from jax.experimental.pallas import tpu as pltpu
from jax.sharding import PartitionSpec as P

GO = 64
VMEM_LIMIT = 50 * 1024 * 1024
NT = (((1,), (1,)), ((), ()))


def split_dot(left, right, dims=None):
    if dims is None:
        return jnp.dot(left, right, preferred_element_type=jnp.float32)
    return lax.dot_general(left, right, dims, preferred_element_type=jnp.float32)


def prepare_kernel(half_ref, values_hbm, left_ref, left_t_ref, values, arrived):
    batches, points, columns = values.shape
    copies = [pltpu.make_async_copy(values_hbm.at[t], values.at[t], arrived.at[t]) for t in range(batches)]
    for copy in copies:
        copy.start()
    groups = columns // GO
    kept = left_ref.shape[2]
    first = half_ref[0] * (kept // groups)
    at = lax.broadcasted_iota(jnp.int32, (kept, columns), 0)
    lane = lax.broadcasted_iota(jnp.int32, (kept, columns), 1)
    wanted = (at % groups) * GO + first + at // groups
    select = jnp.where(lane == wanted, 1.0, 0.0).astype(jnp.bfloat16)
    for t in range(batches):
        copies[t].wait()
        left_ref[t] = split_dot(values[t], select, NT).astype(jnp.bfloat16)
        left_t_ref[t] = split_dot(select, values[t], NT).astype(jnp.bfloat16)


def index_kernel(held, fetch_ref, slots_ref, rows_ref):
    owners, capacity = fetch_ref.shape
    slots = slots_ref[...]
    rows = jnp.zeros(slots.shape, jnp.int32)
    stored = fetch_ref[...] + held * lax.broadcasted_iota(jnp.int32, (owners, capacity), 0)
    for owner in range(owners):
        for at in range(capacity):
            home = stored[owner:owner + 1, at:at + 1].reshape(1, 1, 1)
            rows = jnp.where(slots == owner * capacity + at, home, rows)
    rows_ref[...] = rows


def row_table(place_ref, rows_ref, held, owners):
    rows = lax.bitwise_xor(rows_ref[...], place_ref[0] * held)
    row = lax.broadcasted_iota(jnp.int32, (owners * held, rows.shape[1]), 0)
    return jnp.where(row == rows, 1.0, 0.0)


def density_kernel(places, place_ref, *refs):
    piece_refs = refs[:len(places)]
    rows_ref, left_ref, values_ref, out_ref, table, dense = refs[len(places):]
    batches, points, columns = values_ref.shape
    groups = columns // GO
    held = piece_refs[0].shape[0]
    for ref, k in zip(piece_refs, places):
        table[k * held:(k + 1) * held, :] = ref[...]
    pick = row_table(place_ref, rows_ref, held, len(places)).T.astype(jnp.bfloat16)
    low = lax.broadcasted_iota(jnp.int32, (1, 1, groups, 128), 3) < GO
    for j in range(table.shape[1] // 128):
        lanes = slice(j * 128, (j + 1) * 128)
        got = split_dot(pick, table[:, lanes])
        got = got.reshape(batches, groups // 2, 2, groups, 128)
        even, odd = got[:, :, 0], got[:, :, 1]
        first = jnp.where(low, even, pltpu.roll(odd, GO, 3))
        second = jnp.where(low, pltpu.roll(even, GO, 3), odd)
        for t in range(batches):
            for q in range(groups // 2):
                both = jnp.concatenate([first[t, q], second[t, q]], axis=0)
                dense[t, j * 2 * groups:(j + 1) * 2 * groups, q * 128:(q + 1) * 128] = both.astype(jnp.bfloat16)
    for t in range(batches):
        product = split_dot(left_ref[t], dense[t]) * values_ref[t].astype(jnp.float32)
        folded = product[:, :128]
        for q in range(1, columns // 128):
            folded = folded + product[:, q * 128:(q + 1) * 128]
        out_ref[t:t + 1, :] = jnp.sum(folded.T, axis=0, keepdims=True)


def scatter_kernel(place_ref, *refs):
    mine_ref, other_ref, weight_ref, values_ref, left_t_ref, rows_ref = refs[:6]
    out_refs = refs[6:-2]
    high, rest = refs[-2:]
    pieces = len(out_refs)
    held = out_refs[0].shape[0]
    put = row_table(place_ref, rows_ref, held, pieces).astype(jnp.bfloat16)
    batches, points, columns = values_ref.shape
    groups = columns // GO
    kept = left_t_ref.shape[1]
    steps = kept // (2 * groups)
    potential = weight_ref[...] * jnp.tanh(mine_ref[...] + other_ref[...])
    low = lax.broadcasted_iota(jnp.int32, (1, groups, 128), 2) < GO
    for t in range(batches):
        factor = jnp.broadcast_to(potential[t:t + 1, :], (128, points)).T
        factor = jnp.concatenate([factor] * (columns // 128), axis=1)
        weighted = (values_ref[t].astype(jnp.float32) * factor).astype(jnp.bfloat16)
        part = split_dot(left_t_ref[t], weighted)
        for q in range(groups // 2):
            cut = part[:, q * 128:(q + 1) * 128].reshape(steps, 2, groups, 128)
            first, second = cut[:, 0], cut[:, 1]
            even = jnp.where(low, first, pltpu.roll(second, GO, 2))
            odd = jnp.where(low, pltpu.roll(first, GO, 2), second)
            at = (t * groups + 2 * q) * groups
            for j in range(steps):
                both = jnp.concatenate([even[j], odd[j]], axis=0)
                top = both.astype(jnp.bfloat16)
                high[at:at + 2 * groups, j * 128:(j + 1) * 128] = top
                rest[at:at + 2 * groups, j * 128:(j + 1) * 128] = (both - top.astype(jnp.float32)).astype(jnp.bfloat16)
    step = max(1, min(pieces, 128 // held))
    for k in range(0, pieces, step):
        some = put[k * held:(k + step) * held, :]
        total = split_dot(some, high[...]) + split_dot(some, rest[...])
        for i in range(step):
            out_refs[k + i][...] = total[i * held:(i + 1) * held, :].astype(jnp.bfloat16)


def sum_kernel(*refs):
    out_ref = refs[-1]
    total = refs[0][...].astype(jnp.float32)
    for ref in refs[1:-1]:
        total = total + ref[...].astype(jnp.float32)
    out_ref[...] = total.astype(out_ref.dtype)


def finish_kernel(half_ref, mine_ref, other_ref, core_ref, out_ref):
    wide = mine_ref.shape[1]
    own = pl.multiple_of(half_ref[0] * wide, wide)
    far = pl.multiple_of((1 - half_ref[0]) * wide, wide)
    out_ref[:, pl.ds(own, wide)] = core_ref[:, pl.ds(own, wide)].astype(jnp.float32) + mine_ref[...]
    out_ref[:, pl.ds(far, wide)] = core_ref[:, pl.ds(far, wide)].astype(jnp.float32) + other_ref[...]


def call(kernel, outs, count, scratch=(), scalar=False, flops=0, moved=0, space=pltpu.VMEM):
    specs = [pl.BlockSpec(memory_space=space)] * count
    if scalar:
        specs = [pl.BlockSpec(memory_space=pltpu.SMEM)] + specs
    out_specs = jax.tree.map(lambda _: pl.BlockSpec(memory_space=pltpu.VMEM), outs)
    return pl.pallas_call(
        kernel,
        out_shape=outs,
        in_specs=specs,
        out_specs=out_specs,
        scratch_shapes=list(scratch),
        compiler_params=pltpu.CompilerParams(vmem_limit_bytes=VMEM_LIMIT),
        cost_estimate=pl.CostEstimate(flops=flops, bytes_accessed=moved, transcendentals=0),
    )


def swap(array, axis, count, step):
    return lax.ppermute(array, axis, [(i, i ^ step) for i in range(count)])


def per_device(basis_values, point_weights, slot_ids, fetch_rows, density_blocks, core_blocks):
    rows_z, rows_x = lax.axis_size("batch"), lax.axis_size("pair")
    z, x, half = lax.axis_index("batch"), lax.axis_index("pair"), lax.axis_index("orb")
    owners = rows_z * rows_x
    batches, points, columns = basis_values.shape
    groups, own_groups = slot_ids.shape[1], slot_ids.shape[2]
    held, square = density_blocks.shape
    capacity = fetch_rows.shape[3]
    wide = square // 2
    table_rows = owners * held
    entries = batches * groups * groups
    kept = columns // 2
    bf16, f32 = jnp.bfloat16, jnp.float32

    steps = list(range(rows_z // 2, rows_z)) + list(range(1, rows_z // 2))
    side = list(range(1, rows_x))

    mine = lax.dynamic_slice_in_dim(density_blocks, half * wide, wide, 1)
    pieces = {0: mine}
    for dx in side:
        pieces[dx] = swap(mine, "pair", rows_x, dx)
    for dz in steps[::-1]:
        pieces[dz * rows_x] = swap(mine, "batch", rows_z, dz)
    for dz in steps[rows_z // 2:] + steps[:rows_z // 2]:
        for dx in side:
            pieces[dz * rows_x + dx] = swap(pieces[dz * rows_x], "pair", rows_x, dx)
    order = list(pieces)

    half_at, _ = lax.optimization_barrier((half.reshape(1).astype(jnp.int32), pieces[(rows_z - 1) * rows_x]))
    left, left_t = call(
        prepare_kernel,
        (
            jax.ShapeDtypeStruct((batches, points, kept), bf16),
            jax.ShapeDtypeStruct((batches, kept, points), bf16),
        ),
        1,
        scratch=(pltpu.VMEM(basis_values.shape, bf16), pltpu.SemaphoreType.DMA((batches,))),
        scalar=True,
        space=pl.ANY,
        flops=4 * batches * points * columns * kept,
        moved=3 * batches * points * columns * 2,
    )(half_at, basis_values)

    own_rows = pl.pallas_call(
        functools.partial(index_kernel, held),
        out_shape=jax.ShapeDtypeStruct((batches, own_groups, groups), jnp.int32),
        in_specs=[pl.BlockSpec(memory_space=pltpu.VMEM)] * 2,
        out_specs=pl.BlockSpec(memory_space=pltpu.VMEM),
    )(fetch_rows.reshape(owners, capacity), slot_ids.transpose(0, 2, 1))
    other_rows = swap(own_rows, "orb", 2, 1)
    rows = jnp.concatenate(
        [jnp.where(half == 0, own_rows, other_rows), jnp.where(half == 0, other_rows, own_rows)], axis=1
    ).reshape(1, entries)
    place = (z * rows_x + x).reshape(1).astype(jnp.int32)

    partial = call(
        functools.partial(density_kernel, order),
        jax.ShapeDtypeStruct((batches, points), f32),
        owners + 3,
        scalar=True,
        scratch=(pltpu.VMEM((table_rows, wide), bf16), pltpu.VMEM((batches, kept, columns), bf16)),
        flops=2 * batches * points * columns * kept,
        moved=2 * batches * points * columns * 2,
    )(place, *[pieces[k] for k in order], rows, left, basis_values)
    partial_other = swap(partial, "orb", 2, 1)

    sums = call(
        scatter_kernel,
        [jax.ShapeDtypeStruct((held, wide), bf16)] * owners,
        6,
        scalar=True,
        scratch=(pltpu.VMEM((entries, wide), bf16), pltpu.VMEM((entries, wide), bf16)),
        flops=2 * batches * points * columns * kept,
        moved=2 * batches * points * columns * 2,
    )(place, partial, partial_other, point_weights, basis_values, left_t, rows)

    landed = []
    own = sums[:rows_x]
    for dz in steps:
        joined = sums[dz * rows_x].astype(f32)
        for dx in side:
            joined = joined + swap(sums[dz * rows_x + dx], "pair", rows_x, dx).astype(f32)
        joined = joined.astype(bf16)
        if dz == steps[0]:
            joined, *own = lax.optimization_barrier((joined, *own))
        landed.append(swap(joined, "batch", rows_z, dz))
    for dx in side:
        landed.append(swap(own[dx], "pair", rows_x, dx))
    landed.append(own[0])
    total = call(
        sum_kernel, jax.ShapeDtypeStruct((held, wide), f32), len(landed), moved=len(landed) * held * wide * 2
    )(*landed)
    total_other = swap(total, "orb", 2, 1)
    return call(
        finish_kernel, jax.ShapeDtypeStruct((held, square), f32), 3, scalar=True, moved=held * square * 12
    )(half_at, total, total_other, core_blocks)


def solution(mesh):
    placed = (
        P(("groups", "batch", "pair"), None, None),
        P(("groups", "batch", "pair"), None),
        P(("groups", "batch", "pair"), None, "orb"),
        P(("groups", "batch", "pair"), "orb", None, None),
        P(("groups", "batch", "pair"), None),
        P(("groups", "batch", "pair"), None),
    )
    return jax.shard_map(
        per_device,
        mesh=mesh,
        in_specs=placed,
        out_specs=P(("groups", "batch", "pair"), None),
        check_vma=False,
    )
```

```python
import functools

import jax
import jax.numpy as jnp
from jax import lax
from jax.experimental import pallas as pl
from jax.experimental.pallas import tpu as pltpu
from jax.sharding import PartitionSpec as P

GO = 64
VMEM_LIMIT = 50 * 1024 * 1024
NT = (((1,), (1,)), ((), ()))


def split_dot(left, right, dims=None):
    if dims is None:
        return jnp.dot(left, right, preferred_element_type=jnp.float32)
    return lax.dot_general(left, right, dims, preferred_element_type=jnp.float32)


def prepare_kernel(half_ref, values_ref, left_ref, left_t_ref):
    batches, points, columns = values_ref.shape
    groups = columns // GO
    kept = left_ref.shape[2]
    first = half_ref[0] * (kept // groups)
    at = lax.broadcasted_iota(jnp.int32, (kept, columns), 0)
    lane = lax.broadcasted_iota(jnp.int32, (kept, columns), 1)
    wanted = (at % groups) * GO + first + at // groups
    select = jnp.where(lane == wanted, 1.0, 0.0).astype(jnp.bfloat16)
    for t in range(batches):
        left_ref[t] = split_dot(values_ref[t], select, NT).astype(jnp.bfloat16)
        left_t_ref[t] = split_dot(select, values_ref[t], NT).astype(jnp.bfloat16)


def index_kernel(held, fetch_ref, slots_ref, rows_ref):
    owners, capacity = fetch_ref.shape
    slots = slots_ref[...]
    entries = slots.shape[1]
    owner = slots // capacity
    owner_hot = jnp.where(lax.broadcasted_iota(jnp.int32, (owners, entries), 0) == owner, 1.0, 0.0)
    stored = fetch_ref[...].astype(jnp.float32).T.astype(jnp.bfloat16)
    listed = split_dot(stored, owner_hot.astype(jnp.bfloat16)).astype(jnp.int32)
    at = lax.broadcasted_iota(jnp.int32, (capacity, entries), 0)
    chosen = jnp.where(at == slots - owner * capacity, listed, 0)
    rows_ref[...] = jnp.sum(chosen, axis=0, keepdims=True) + owner * held


def row_table(place_ref, own_ref, other_ref, held, owners):
    low = place_ref[1] == 0
    rows = jnp.concatenate(
        [jnp.where(low, own_ref[...], other_ref[...]), jnp.where(low, other_ref[...], own_ref[...])], axis=1
    )
    rows = lax.bitwise_xor(rows, place_ref[0] * held)
    row = lax.broadcasted_iota(jnp.int32, (owners * held, rows.shape[1]), 0)
    return jnp.where(row == rows, 1.0, 0.0)


def density_kernel(places, place_ref, *refs):
    piece_refs = refs[:len(places)]
    own_ref, other_ref, left_ref, values_ref, out_ref, table, dense = refs[len(places):]
    batches, points, columns = values_ref.shape
    groups = columns // GO
    held = piece_refs[0].shape[0]
    for ref, k in zip(piece_refs, places):
        table[k * held:(k + 1) * held, :] = ref[...]
    pick = row_table(place_ref, own_ref, other_ref, held, len(places)).T.astype(jnp.bfloat16)
    low = lax.broadcasted_iota(jnp.int32, (1, 1, 1, groups, 128), 4) < GO
    for j in range(table.shape[1] // 128):
        lanes = slice(j * 128, (j + 1) * 128)
        got = split_dot(pick, table[:, lanes])
        got = got.reshape(2, batches, groups // 4, 2, groups, 128)
        even, odd = got[:, :, :, 0], got[:, :, :, 1]
        first = jnp.where(low, even, pltpu.roll(odd, GO, 4))
        second = jnp.where(low, pltpu.roll(even, GO, 4), odd)
        for t in range(batches):
            for q in range(groups // 2):
                at = (q // (groups // 4), t, q % (groups // 4))
                both = jnp.concatenate([first[at], second[at]], axis=0)
                dense[t, j * 2 * groups:(j + 1) * 2 * groups, q * 128:(q + 1) * 128] = both.astype(jnp.bfloat16)
    for t in range(batches):
        product = split_dot(left_ref[t], dense[t]) * values_ref[t].astype(jnp.float32)
        folded = product[:, :128]
        for q in range(1, columns // 128):
            folded = folded + product[:, q * 128:(q + 1) * 128]
        out_ref[t:t + 1, :] = jnp.sum(folded.T, axis=0, keepdims=True)


def scatter_kernel(place_ref, *refs):
    mine_ref, far_ref, weight_ref, values_ref, left_t_ref, own_ref, other_ref = refs[:7]
    out_refs = refs[7:-2]
    high, rest = refs[-2:]
    pieces = len(out_refs)
    held = out_refs[0].shape[0]
    put = row_table(place_ref, own_ref, other_ref, held, pieces).astype(jnp.bfloat16)
    batches, points, columns = values_ref.shape
    groups = columns // GO
    kept = left_t_ref.shape[1]
    steps = kept // (2 * groups)
    potential = weight_ref[...] * jnp.tanh(mine_ref[...] + far_ref[...])
    low = lax.broadcasted_iota(jnp.int32, (1, groups, 128), 2) < GO
    for t in range(batches):
        factor = jnp.broadcast_to(potential[t:t + 1, :], (128, points)).T
        factor = jnp.concatenate([factor] * (columns // 128), axis=1)
        weighted = (values_ref[t].astype(jnp.float32) * factor).astype(jnp.bfloat16)
        part = split_dot(left_t_ref[t], weighted)
        for q in range(groups // 2):
            cut = part[:, q * 128:(q + 1) * 128].reshape(steps, 2, groups, 128)
            first, second = cut[:, 0], cut[:, 1]
            even = jnp.where(low, first, pltpu.roll(second, GO, 2))
            odd = jnp.where(low, pltpu.roll(first, GO, 2), second)
            side, pair = q // (groups // 4), q % (groups // 4)
            at = ((side * batches + t) * (groups // 2) + 2 * pair) * groups
            for j in range(steps):
                both = jnp.concatenate([even[j], odd[j]], axis=0)
                top = both.astype(jnp.bfloat16)
                high[at:at + 2 * groups, j * 128:(j + 1) * 128] = top
                rest[at:at + 2 * groups, j * 128:(j + 1) * 128] = (both - top.astype(jnp.float32)).astype(jnp.bfloat16)
    step = max(1, min(pieces, 128 // held))
    for k in range(0, pieces, step):
        some = put[k * held:(k + step) * held, :]
        total = split_dot(some, high[...]) + split_dot(some, rest[...])
        for i in range(step):
            out_refs[k + i][...] = total[i * held:(i + 1) * held, :].astype(jnp.bfloat16)


def sum_kernel(*refs):
    out_ref = refs[-1]
    total = refs[0][...].astype(jnp.float32)
    for ref in refs[1:-1]:
        total = total + ref[...].astype(jnp.float32)
    out_ref[...] = total.astype(out_ref.dtype)


def finish_kernel(half_ref, mine_ref, other_ref, core_ref, out_ref):
    wide = mine_ref.shape[1]
    own = pl.multiple_of(half_ref[0] * wide, wide)
    far = pl.multiple_of((1 - half_ref[0]) * wide, wide)
    out_ref[:, pl.ds(own, wide)] = core_ref[:, pl.ds(own, wide)].astype(jnp.float32) + mine_ref[...]
    out_ref[:, pl.ds(far, wide)] = core_ref[:, pl.ds(far, wide)].astype(jnp.float32) + other_ref[...]


def call(kernel, outs, count, scratch=(), scalar=False, flops=0, moved=0):
    specs = [pl.BlockSpec(memory_space=pltpu.VMEM)] * count
    if scalar:
        specs = [pl.BlockSpec(memory_space=pltpu.SMEM)] + specs
    out_specs = jax.tree.map(lambda _: pl.BlockSpec(memory_space=pltpu.VMEM), outs)
    return pl.pallas_call(
        kernel,
        out_shape=outs,
        in_specs=specs,
        out_specs=out_specs,
        scratch_shapes=list(scratch),
        compiler_params=pltpu.CompilerParams(vmem_limit_bytes=VMEM_LIMIT),
        cost_estimate=pl.CostEstimate(flops=flops, bytes_accessed=moved, transcendentals=0),
    )


def swap(array, axis, count, step):
    return lax.ppermute(array, axis, [(i, i ^ step) for i in range(count)])


def per_device(basis_values, point_weights, slot_ids, fetch_rows, density_blocks, core_blocks):
    rows_z, rows_x = lax.axis_size("batch"), lax.axis_size("pair")
    z, x, half = lax.axis_index("batch"), lax.axis_index("pair"), lax.axis_index("orb")
    owners = rows_z * rows_x
    batches, points, columns = basis_values.shape
    groups, own_groups = slot_ids.shape[1], slot_ids.shape[2]
    held, square = density_blocks.shape
    capacity = fetch_rows.shape[3]
    wide = square // 2
    table_rows = owners * held
    entries = batches * groups * groups
    kept = columns // 2
    bf16, f32 = jnp.bfloat16, jnp.float32

    steps = list(range(rows_z // 2, rows_z)) + list(range(1, rows_z // 2))
    side = list(range(1, rows_x))

    mine = lax.dynamic_slice_in_dim(density_blocks, half * wide, wide, 1)
    pieces = {0: mine}
    for dx in side:
        pieces[dx] = swap(mine, "pair", rows_x, dx)
    for dz in steps[::-1]:
        pieces[dz * rows_x] = swap(mine, "batch", rows_z, dz)
    for dz in steps[rows_z // 2:] + steps[:rows_z // 2]:
        for dx in side:
            pieces[dz * rows_x + dx] = swap(pieces[dz * rows_x], "pair", rows_x, dx)
    order = list(pieces)

    half_at, _ = lax.optimization_barrier((half.reshape(1).astype(jnp.int32), pieces[(rows_z - 1) * rows_x]))
    left, left_t = call(
        prepare_kernel,
        (
            jax.ShapeDtypeStruct((batches, points, kept), bf16),
            jax.ShapeDtypeStruct((batches, kept, points), bf16),
        ),
        1,
        scalar=True,
        flops=4 * batches * points * columns * kept,
        moved=3 * batches * points * columns * 2,
    )(half_at, basis_values)

    own_rows = call(
        functools.partial(index_kernel, held),
        jax.ShapeDtypeStruct((1, batches * own_groups * groups), jnp.int32),
        2,
    )(fetch_rows.reshape(owners, capacity), slot_ids.transpose(0, 2, 1).reshape(1, -1))
    other_rows = swap(own_rows, "orb", 2, 1)
    place = jnp.stack([z * rows_x + x, half]).astype(jnp.int32)

    partial = call(
        functools.partial(density_kernel, order),
        jax.ShapeDtypeStruct((batches, points), f32),
        owners + 4,
        scalar=True,
        scratch=(pltpu.VMEM((table_rows, wide), bf16), pltpu.VMEM((batches, kept, columns), bf16)),
        flops=2 * batches * points * columns * kept,
        moved=2 * batches * points * columns * 2,
    )(place, *[pieces[k] for k in order], own_rows, other_rows, left, basis_values)
    partial_other = swap(partial, "orb", 2, 1)

    sums = call(
        scatter_kernel,
        [jax.ShapeDtypeStruct((held, wide), bf16)] * owners,
        7,
        scalar=True,
        scratch=(pltpu.VMEM((entries, wide), bf16), pltpu.VMEM((entries, wide), bf16)),
        flops=2 * batches * points * columns * kept,
        moved=2 * batches * points * columns * 2,
    )(place, partial, partial_other, point_weights, basis_values, left_t, own_rows, other_rows)

    landed = []
    own = sums[:rows_x]
    for dz in steps:
        joined = sums[dz * rows_x].astype(f32)
        for dx in side:
            joined = joined + swap(sums[dz * rows_x + dx], "pair", rows_x, dx).astype(f32)
        joined = joined.astype(bf16)
        if dz == steps[:2][-1]:
            joined, *own = lax.optimization_barrier((joined, *own))
        landed.append(swap(joined, "batch", rows_z, dz))
    for dx in side:
        landed.append(swap(own[dx], "pair", rows_x, dx))
    landed.append(own[0])
    total = call(
        sum_kernel, jax.ShapeDtypeStruct((held, wide), f32), len(landed), moved=len(landed) * held * wide * 2
    )(*landed)
    total_other = swap(total, "orb", 2, 1)
    return call(
        finish_kernel, jax.ShapeDtypeStruct((held, square), f32), 3, scalar=True, moved=held * square * 12
    )(half_at, total, total_other, core_blocks)


def solution(mesh):
    placed = (
        P(("groups", "batch", "pair"), None, None),
        P(("groups", "batch", "pair"), None),
        P(("groups", "batch", "pair"), None, "orb"),
        P(("groups", "batch", "pair"), "orb", None, None),
        P(("groups", "batch", "pair"), None),
        P(("groups", "batch", "pair"), None),
    )
    return jax.shard_map(
        per_device,
        mesh=mesh,
        in_specs=placed,
        out_specs=P(("groups", "batch", "pair"), None),
        check_vma=False,
    )
```

```python
import functools

import jax
import jax.numpy as jnp
from jax import lax
from jax.experimental import pallas as pl
from jax.experimental.pallas import tpu as pltpu
from jax.sharding import PartitionSpec as P

GO = 64
VMEM_LIMIT = 50 * 1024 * 1024
NT = (((1,), (1,)), ((), ()))


def split_dot(left, right, dims=None):
    if dims is None:
        return jnp.dot(left, right, preferred_element_type=jnp.float32)
    return lax.dot_general(left, right, dims, preferred_element_type=jnp.float32)


def prepare_kernel(half_ref, values_ref, left_ref, left_t_ref):
    batches, points, columns = values_ref.shape
    groups = columns // GO
    kept = left_ref.shape[2]
    first = half_ref[0] * (kept // groups)
    at = lax.broadcasted_iota(jnp.int32, (kept, columns), 0)
    lane = lax.broadcasted_iota(jnp.int32, (kept, columns), 1)
    wanted = (at % groups) * GO + first + at // groups
    select = jnp.where(lane == wanted, 1.0, 0.0).astype(jnp.bfloat16)
    for t in range(batches):
        left_ref[t] = split_dot(values_ref[t], select, NT).astype(jnp.bfloat16)
        left_t_ref[t] = split_dot(select, values_ref[t], NT).astype(jnp.bfloat16)


def index_kernel(held, fetch_ref, slots_ref, rows_ref):
    owners, capacity = fetch_ref.shape
    slots = slots_ref[...]
    entries = slots.shape[1]
    owner = slots // capacity
    owner_hot = jnp.where(lax.broadcasted_iota(jnp.int32, (owners, entries), 0) == owner, 1.0, 0.0)
    stored = fetch_ref[...].astype(jnp.float32).T.astype(jnp.bfloat16)
    listed = split_dot(stored, owner_hot.astype(jnp.bfloat16)).astype(jnp.int32)
    at = lax.broadcasted_iota(jnp.int32, (capacity, entries), 0)
    chosen = jnp.where(at == slots - owner * capacity, listed, 0)
    rows_ref[...] = jnp.sum(chosen, axis=0, keepdims=True) + owner * held


def row_table(place_ref, half_ref, own_ref, other_ref, held, owners):
    low = half_ref[0] == 0
    rows = jnp.concatenate(
        [jnp.where(low, own_ref[...], other_ref[...]), jnp.where(low, other_ref[...], own_ref[...])], axis=1
    )
    rows = lax.bitwise_xor(rows, place_ref[0] * held)
    row = lax.broadcasted_iota(jnp.int32, (owners * held, rows.shape[1]), 0)
    return jnp.where(row == rows, 1.0, 0.0)


def density_kernel(places, place_ref, half_ref, *refs):
    piece_refs = refs[:len(places)]
    own_ref, other_ref, left_ref, values_ref, out_ref, table, dense = refs[len(places):]
    batches, points, columns = values_ref.shape
    groups = columns // GO
    held = piece_refs[0].shape[0]
    for ref, k in zip(piece_refs, places):
        table[k * held:(k + 1) * held, :] = ref[...]
    pick = row_table(place_ref, half_ref, own_ref, other_ref, held, len(places)).T.astype(jnp.bfloat16)
    low = lax.broadcasted_iota(jnp.int32, (1, 1, 1, groups, 128), 4) < GO
    for j in range(table.shape[1] // 128):
        lanes = slice(j * 128, (j + 1) * 128)
        got = split_dot(pick, table[:, lanes])
        got = got.reshape(2, batches, groups // 4, 2, groups, 128)
        even, odd = got[:, :, :, 0], got[:, :, :, 1]
        first = jnp.where(low, even, pltpu.roll(odd, GO, 4))
        second = jnp.where(low, pltpu.roll(even, GO, 4), odd)
        for t in range(batches):
            for q in range(groups // 2):
                at = (q // (groups // 4), t, q % (groups // 4))
                both = jnp.concatenate([first[at], second[at]], axis=0)
                dense[t, j * 2 * groups:(j + 1) * 2 * groups, q * 128:(q + 1) * 128] = both.astype(jnp.bfloat16)
    for t in range(batches):
        product = split_dot(left_ref[t], dense[t]) * values_ref[t].astype(jnp.float32)
        folded = product[:, :128]
        for q in range(1, columns // 128):
            folded = folded + product[:, q * 128:(q + 1) * 128]
        out_ref[t:t + 1, :] = jnp.sum(folded.T, axis=0, keepdims=True)


def scatter_kernel(place_ref, half_ref, *refs):
    mine_ref, far_ref, weight_ref, values_ref, left_t_ref, own_ref, other_ref = refs[:7]
    out_refs = refs[7:-2]
    high, rest = refs[-2:]
    pieces = len(out_refs)
    held = out_refs[0].shape[0]
    put = row_table(place_ref, half_ref, own_ref, other_ref, held, pieces).astype(jnp.bfloat16)
    batches, points, columns = values_ref.shape
    groups = columns // GO
    kept = left_t_ref.shape[1]
    steps = kept // (2 * groups)
    potential = weight_ref[...] * jnp.tanh(mine_ref[...] + far_ref[...])
    low = lax.broadcasted_iota(jnp.int32, (1, groups, 128), 2) < GO
    for t in range(batches):
        factor = jnp.broadcast_to(potential[t:t + 1, :], (128, points)).T
        factor = jnp.concatenate([factor] * (columns // 128), axis=1)
        weighted = (values_ref[t].astype(jnp.float32) * factor).astype(jnp.bfloat16)
        part = split_dot(left_t_ref[t], weighted)
        for q in range(groups // 2):
            cut = part[:, q * 128:(q + 1) * 128].reshape(steps, 2, groups, 128)
            first, second = cut[:, 0], cut[:, 1]
            even = jnp.where(low, first, pltpu.roll(second, GO, 2))
            odd = jnp.where(low, pltpu.roll(first, GO, 2), second)
            side, pair = q // (groups // 4), q % (groups // 4)
            at = ((side * batches + t) * (groups // 2) + 2 * pair) * groups
            for j in range(steps):
                both = jnp.concatenate([even[j], odd[j]], axis=0)
                top = both.astype(jnp.bfloat16)
                high[at:at + 2 * groups, j * 128:(j + 1) * 128] = top
                rest[at:at + 2 * groups, j * 128:(j + 1) * 128] = (both - top.astype(jnp.float32)).astype(jnp.bfloat16)
    step = max(1, min(pieces, 128 // held))
    for k in range(0, pieces, step):
        some = put[k * held:(k + step) * held, :]
        total = split_dot(some, high[...]) + split_dot(some, rest[...])
        for i in range(step):
            out_refs[k + i][...] = total[i * held:(i + 1) * held, :].astype(jnp.bfloat16)


def finish_kernel(half_ref, mine_ref, other_ref, core_ref, out_ref):
    wide = mine_ref.shape[1]
    own = pl.multiple_of(half_ref[0] * wide, wide)
    far = pl.multiple_of((1 - half_ref[0]) * wide, wide)
    out_ref[:, pl.ds(own, wide)] = core_ref[:, pl.ds(own, wide)].astype(jnp.float32) + mine_ref[...]
    out_ref[:, pl.ds(far, wide)] = core_ref[:, pl.ds(far, wide)].astype(jnp.float32) + other_ref[...]


def call(kernel, outs, count, scratch=(), scalars=0, flops=0, moved=0):
    specs = [pl.BlockSpec(memory_space=pltpu.VMEM)] * count
    specs = [pl.BlockSpec(memory_space=pltpu.SMEM)] * scalars + specs
    out_specs = jax.tree.map(lambda _: pl.BlockSpec(memory_space=pltpu.VMEM), outs)
    return pl.pallas_call(
        kernel,
        out_shape=outs,
        in_specs=specs,
        out_specs=out_specs,
        scratch_shapes=list(scratch),
        compiler_params=pltpu.CompilerParams(vmem_limit_bytes=VMEM_LIMIT),
        cost_estimate=pl.CostEstimate(flops=flops, bytes_accessed=moved, transcendentals=0),
    )


def swap(array, axis, count, step):
    return lax.ppermute(array, axis, [(i, i ^ step) for i in range(count)])


def add_all(terms):
    total = terms[0]
    for term in terms[1:]:
        total = total + term
    return total


def per_device(basis_values, point_weights, slot_ids, fetch_rows, density_blocks, core_blocks):
    rows_z, rows_x = lax.axis_size("batch"), lax.axis_size("pair")
    z, x, half = lax.axis_index("batch"), lax.axis_index("pair"), lax.axis_index("orb")
    owners = rows_z * rows_x
    batches, points, columns = basis_values.shape
    groups, own_groups = slot_ids.shape[1], slot_ids.shape[2]
    held, square = density_blocks.shape
    capacity = fetch_rows.shape[3]
    wide = square // 2
    table_rows = owners * held
    entries = batches * groups * groups
    kept = columns // 2
    bf16, f32 = jnp.bfloat16, jnp.float32

    own_rows = call(
        functools.partial(index_kernel, held),
        jax.ShapeDtypeStruct((1, batches * own_groups * groups), jnp.int32),
        2,
    )(fetch_rows.reshape(owners, capacity), slot_ids.transpose(0, 2, 1).reshape(1, -1))
    other_rows = swap(own_rows, "orb", 2, 1)

    bits = [1 << i for i in reversed(range(rows_z.bit_length() - 1))]
    side = list(range(1, rows_x))

    mine = lax.dynamic_slice_in_dim(density_blocks, half * wide, wide, 1)
    pieces = {0: mine}
    have = [0]
    for bit in bits:
        for dz in have:
            pieces[(dz | bit) * rows_x] = swap(pieces[dz * rows_x], "batch", rows_z, bit)
        if bit == bits[0]:
            for dx in side:
                pieces[dx] = swap(mine, "pair", rows_x, dx)
            ready = side + [bit * rows_x]
            ordered = lax.optimization_barrier([pieces[k] for k in ready])
            pieces.update(zip(ready, ordered))
        have = have + [dz | bit for dz in have]
    first = bits[0] * rows_x
    pieces[first], other_rows = lax.optimization_barrier((pieces[first], other_rows))
    for dz in have[1:]:
        for dx in side:
            pieces[dz * rows_x + dx] = swap(pieces[dz * rows_x], "pair", rows_x, dx)
    order = list(pieces)

    half_at, _ = lax.optimization_barrier((half.reshape(1).astype(jnp.int32), pieces[(rows_z - 1) * rows_x]))
    left, left_t = call(
        prepare_kernel,
        (
            jax.ShapeDtypeStruct((batches, points, kept), bf16),
            jax.ShapeDtypeStruct((batches, kept, points), bf16),
        ),
        1,
        scalars=1,
        flops=4 * batches * points * columns * kept,
        moved=3 * batches * points * columns * 2,
    )(half_at, basis_values)

    place = (z * rows_x + x).reshape(1).astype(jnp.int32)
    side_at = half.reshape(1).astype(jnp.int32)

    partial = call(
        functools.partial(density_kernel, order),
        jax.ShapeDtypeStruct((batches, points), f32),
        owners + 4,
        scalars=2,
        scratch=(pltpu.VMEM((table_rows, wide), bf16), pltpu.VMEM((batches, kept, columns), bf16)),
        flops=2 * batches * points * columns * kept,
        moved=2 * batches * points * columns * 2,
    )(place, side_at, *[pieces[k] for k in order], own_rows, other_rows, left, basis_values)
    partial_other = swap(partial, "orb", 2, 1)

    sums = call(
        scatter_kernel,
        [jax.ShapeDtypeStruct((held, wide), bf16)] * owners,
        7,
        scalars=2,
        scratch=(pltpu.VMEM((entries, wide), bf16), pltpu.VMEM((entries, wide), bf16)),
        flops=2 * batches * points * columns * kept,
        moved=2 * batches * points * columns * 2,
    )(place, side_at, partial, partial_other, point_weights, basis_values, left_t, own_rows, other_rows)

    sums = list(sums)
    joined = {}
    for dz in reversed(have):
        terms = [sums[dz * rows_x]] + [swap(sums[dz * rows_x + dx], "pair", rows_x, dx) for dx in side]
        if dz == rows_z - 1:
            terms[-1], *sums[1:rows_x] = lax.optimization_barrier((terms[-1], *sums[1:rows_x]))
        joined[dz] = [term.astype(f32) for term in terms]
    for bit in reversed(bits):
        for dz in range(rows_z - bit, 0, -2 * bit):
            sent = add_all(joined.pop(dz)).astype(bf16)
            came = swap(sent, "batch", rows_z, bit)
            joined[dz ^ bit].append(came.astype(f32))
    landed = joined[0]
    total = add_all(landed)
    total_other = swap(total, "orb", 2, 1)
    return call(
        finish_kernel, jax.ShapeDtypeStruct((held, square), f32), 3, scalars=1, moved=held * square * 12
    )(half_at, total, total_other, core_blocks)


def solution(mesh):
    placed = (
        P(("groups", "batch", "pair"), None, None),
        P(("groups", "batch", "pair"), None),
        P(("groups", "batch", "pair"), None, "orb"),
        P(("groups", "batch", "pair"), "orb", None, None),
        P(("groups", "batch", "pair"), None),
        P(("groups", "batch", "pair"), None),
    )
    return jax.shard_map(
        per_device,
        mesh=mesh,
        in_specs=placed,
        out_specs=P(("groups", "batch", "pair"), None),
        check_vma=False,
    )
```

```python
import functools

import jax
import jax.numpy as jnp
from jax import lax
from jax.experimental import pallas as pl
from jax.experimental.pallas import tpu as pltpu
from jax.sharding import PartitionSpec as P

GO = 64
VMEM_LIMIT = 50 * 1024 * 1024
NT = (((1,), (1,)), ((), ()))


def split_dot(left, right, dims=None):
    if dims is None:
        return jnp.dot(left, right, preferred_element_type=jnp.float32)
    return lax.dot_general(left, right, dims, preferred_element_type=jnp.float32)


def prepare_kernel(half_ref, values_ref, left_ref, left_t_ref):
    batches, points, columns = values_ref.shape
    groups = columns // GO
    kept = left_ref.shape[2]
    first = half_ref[0] * (kept // groups)
    at = lax.broadcasted_iota(jnp.int32, (kept, columns), 0)
    lane = lax.broadcasted_iota(jnp.int32, (kept, columns), 1)
    wanted = (at % groups) * GO + first + at // groups
    select = jnp.where(lane == wanted, 1.0, 0.0).astype(jnp.bfloat16)
    for t in range(batches):
        left_ref[t] = split_dot(values_ref[t], select, NT).astype(jnp.bfloat16)
        left_t_ref[t] = split_dot(select, values_ref[t], NT).astype(jnp.bfloat16)


def index_kernel(held, fetch_ref, slots_ref, rows_ref):
    owners, capacity = fetch_ref.shape
    slots = slots_ref[...]
    entries = slots.shape[1]
    owner = slots // capacity
    owner_hot = jnp.where(lax.broadcasted_iota(jnp.int32, (owners, entries), 0) == owner, 1.0, 0.0)
    stored = fetch_ref[...].astype(jnp.float32).T.astype(jnp.bfloat16)
    listed = split_dot(stored, owner_hot.astype(jnp.bfloat16)).astype(jnp.int32)
    at = lax.broadcasted_iota(jnp.int32, (capacity, entries), 0)
    chosen = jnp.where(at == slots - owner * capacity, listed, 0)
    rows_ref[...] = jnp.sum(chosen, axis=0, keepdims=True) + owner * held


def row_table(place_ref, core_ref, own_ref, other_ref, held, owners):
    low = core_ref[0] == 0
    rows = jnp.concatenate(
        [jnp.where(low, own_ref[...], other_ref[...]), jnp.where(low, other_ref[...], own_ref[...])], axis=1
    )
    rows = lax.bitwise_xor(rows, place_ref[0] * held)
    row = lax.broadcasted_iota(jnp.int32, (owners * held, rows.shape[1]), 0)
    return jnp.where(row == rows, 1.0, 0.0)


def density_kernel(places, place_ref, core_ref, *refs):
    piece_refs = refs[:len(places)]
    own_ref, other_ref, left_ref, values_ref, out_ref, table, dense = refs[len(places):]
    batches, points, columns = values_ref.shape
    groups = columns // GO
    held = piece_refs[0].shape[0]
    for ref, k in zip(piece_refs, places):
        table[k * held:(k + 1) * held, :] = ref[...]
    pick = row_table(place_ref, core_ref, own_ref, other_ref, held, len(places)).T.astype(jnp.bfloat16)
    low = lax.broadcasted_iota(jnp.int32, (1, 1, 1, groups, 128), 4) < GO
    for j in range(table.shape[1] // 128):
        lanes = slice(j * 128, (j + 1) * 128)
        got = split_dot(pick, table[:, lanes])
        got = got.reshape(2, batches, groups // 4, 2, groups, 128)
        even, odd = got[:, :, :, 0], got[:, :, :, 1]
        first = jnp.where(low, even, pltpu.roll(odd, GO, 4))
        second = jnp.where(low, pltpu.roll(even, GO, 4), odd)
        for t in range(batches):
            for q in range(groups // 2):
                at = (q // (groups // 4), t, q % (groups // 4))
                both = jnp.concatenate([first[at], second[at]], axis=0)
                dense[t, j * 2 * groups:(j + 1) * 2 * groups, q * 128:(q + 1) * 128] = both.astype(jnp.bfloat16)
    for t in range(batches):
        product = split_dot(left_ref[t], dense[t]) * values_ref[t].astype(jnp.float32)
        folded = product[:, :128]
        for q in range(1, columns // 128):
            folded = folded + product[:, q * 128:(q + 1) * 128]
        out_ref[t:t + 1, :] = jnp.sum(folded.T, axis=0, keepdims=True)


def scatter_kernel(place_ref, core_ref, *refs):
    mine_ref, far_ref, weight_ref, values_ref, left_t_ref, own_ref, other_ref = refs[:7]
    out_refs = refs[7:-2]
    high, rest = refs[-2:]
    pieces = len(out_refs)
    held = out_refs[0].shape[0]
    put = row_table(place_ref, core_ref, own_ref, other_ref, held, pieces).astype(jnp.bfloat16)
    batches, points, columns = values_ref.shape
    groups = columns // GO
    kept = left_t_ref.shape[1]
    steps = kept // (2 * groups)
    potential = weight_ref[...] * jnp.tanh(mine_ref[...] + far_ref[...])
    low = lax.broadcasted_iota(jnp.int32, (1, groups, 128), 2) < GO
    for t in range(batches):
        factor = jnp.broadcast_to(potential[t:t + 1, :], (128, points)).T
        factor = jnp.concatenate([factor] * (columns // 128), axis=1)
        weighted = (values_ref[t].astype(jnp.float32) * factor).astype(jnp.bfloat16)
        part = split_dot(left_t_ref[t], weighted)
        for q in range(groups // 2):
            cut = part[:, q * 128:(q + 1) * 128].reshape(steps, 2, groups, 128)
            first, second = cut[:, 0], cut[:, 1]
            even = jnp.where(low, first, pltpu.roll(second, GO, 2))
            odd = jnp.where(low, pltpu.roll(first, GO, 2), second)
            side, pair = q // (groups // 4), q % (groups // 4)
            at = ((side * batches + t) * (groups // 2) + 2 * pair) * groups
            for j in range(steps):
                both = jnp.concatenate([even[j], odd[j]], axis=0)
                top = both.astype(jnp.bfloat16)
                high[at:at + 2 * groups, j * 128:(j + 1) * 128] = top
                rest[at:at + 2 * groups, j * 128:(j + 1) * 128] = (both - top.astype(jnp.float32)).astype(jnp.bfloat16)
    step = max(1, min(pieces, 128 // held))
    for k in range(0, pieces, step):
        some = put[k * held:(k + step) * held, :]
        total = split_dot(some, high[...]) + split_dot(some, rest[...])
        for i in range(step):
            out_refs[k + i][...] = total[i * held:(i + 1) * held, :].astype(jnp.bfloat16)


def finish_kernel(half_ref, mine_ref, other_ref, core_ref, out_ref):
    wide = mine_ref.shape[1]
    own = pl.multiple_of(half_ref[0] * wide, wide)
    far = pl.multiple_of((1 - half_ref[0]) * wide, wide)
    out_ref[:, pl.ds(own, wide)] = core_ref[:, pl.ds(own, wide)].astype(jnp.float32) + mine_ref[...]
    out_ref[:, pl.ds(far, wide)] = core_ref[:, pl.ds(far, wide)].astype(jnp.float32) + other_ref[...]


def call(kernel, outs, count, scratch=(), scalars=0, flops=0, moved=0):
    specs = [pl.BlockSpec(memory_space=pltpu.VMEM)] * count
    specs = [pl.BlockSpec(memory_space=pltpu.SMEM)] * scalars + specs
    out_specs = jax.tree.map(lambda _: pl.BlockSpec(memory_space=pltpu.VMEM), outs)
    return pl.pallas_call(
        kernel,
        out_shape=outs,
        in_specs=specs,
        out_specs=out_specs,
        scratch_shapes=list(scratch),
        compiler_params=pltpu.CompilerParams(vmem_limit_bytes=VMEM_LIMIT),
        cost_estimate=pl.CostEstimate(flops=flops, bytes_accessed=moved, transcendentals=0),
    )


def odd_bits(number, count):
    parity = number & 1
    for shift in range(1, (count - 1).bit_length()):
        parity = parity ^ ((number >> shift) & 1)
    return parity


def swap(array, sizes, dz, dx):
    rows_z, rows_x = sizes
    turn = odd_bits(dz, rows_z) ^ odd_bits(dx, rows_x)
    step = (dz * rows_x + dx) * 2 + turn
    return lax.ppermute(array, ("batch", "pair", "orb"), [(i, i ^ step) for i in range(rows_z * rows_x * 2)])


def swap_cores(array):
    return lax.ppermute(array, "orb", [(0, 1), (1, 0)])


def add_all(terms):
    total = terms[0]
    for term in terms[1:]:
        total = total + term
    return total


def per_device(basis_values, point_weights, slot_ids, fetch_rows, density_blocks, core_blocks):
    rows_z, rows_x = lax.axis_size("batch"), lax.axis_size("pair")
    z, x, core = lax.axis_index("batch"), lax.axis_index("pair"), lax.axis_index("orb")
    sizes = (rows_z, rows_x)
    half = core ^ odd_bits(z, rows_z) ^ odd_bits(x, rows_x)
    owners = rows_z * rows_x
    batches, points, columns = basis_values.shape
    groups, own_groups = slot_ids.shape[1], slot_ids.shape[2]
    held, square = density_blocks.shape
    capacity = fetch_rows.shape[3]
    wide = square // 2
    table_rows = owners * held
    entries = batches * groups * groups
    kept = columns // 2
    bf16, f32 = jnp.bfloat16, jnp.float32

    own_rows = call(
        functools.partial(index_kernel, held),
        jax.ShapeDtypeStruct((1, batches * own_groups * groups), jnp.int32),
        2,
    )(fetch_rows.reshape(owners, capacity), slot_ids.transpose(0, 2, 1).reshape(1, -1))
    other_rows = swap_cores(own_rows)

    steps = list(range(rows_z // 2, rows_z)) + list(range(1, rows_z // 2))
    side = list(range(1, rows_x))

    mine = lax.dynamic_slice_in_dim(density_blocks, half * wide, wide, 1)
    pieces = {0: mine}
    for dx in side:
        pieces[dx] = swap(mine, sizes, 0, dx)
    for dz in steps[::-1]:
        pieces[dz * rows_x] = swap(mine, sizes, dz, 0)
    first, last = steps[0] * rows_x, (rows_z - 1) * rows_x
    pieces[first], own_rows = lax.optimization_barrier((pieces[first], own_rows))
    pieces[last], other_rows = lax.optimization_barrier((pieces[last], other_rows))
    for dz in steps[rows_z // 2:] + steps[:rows_z // 2]:
        for dx in side:
            pieces[dz * rows_x + dx] = swap(pieces[dz * rows_x], sizes, 0, dx)
    order = list(pieces)

    half_at, _ = lax.optimization_barrier((half.reshape(1).astype(jnp.int32), pieces[last]))
    left, left_t = call(
        prepare_kernel,
        (
            jax.ShapeDtypeStruct((batches, points, kept), bf16),
            jax.ShapeDtypeStruct((batches, kept, points), bf16),
        ),
        1,
        scalars=1,
        flops=4 * batches * points * columns * kept,
        moved=3 * batches * points * columns * 2,
    )(half_at, basis_values)

    place = (z * rows_x + x).reshape(1).astype(jnp.int32)
    core_at = core.reshape(1).astype(jnp.int32)

    partial = call(
        functools.partial(density_kernel, order),
        jax.ShapeDtypeStruct((batches, points), f32),
        owners + 4,
        scalars=2,
        scratch=(pltpu.VMEM((table_rows, wide), bf16), pltpu.VMEM((batches, kept, columns), bf16)),
        flops=2 * batches * points * columns * kept,
        moved=2 * batches * points * columns * 2,
    )(place, core_at, *[pieces[k] for k in order], own_rows, other_rows, left, basis_values)
    partial_other = swap_cores(partial)

    sums = call(
        scatter_kernel,
        [jax.ShapeDtypeStruct((held, wide), bf16)] * owners,
        7,
        scalars=2,
        scratch=(pltpu.VMEM((entries, wide), bf16), pltpu.VMEM((entries, wide), bf16)),
        flops=2 * batches * points * columns * kept,
        moved=2 * batches * points * columns * 2,
    )(place, core_at, partial, partial_other, point_weights, basis_values, left_t, own_rows, other_rows)

    landed = []
    own = sums[:rows_x]
    for dz in steps:
        joined = sums[dz * rows_x].astype(f32)
        for dx in side:
            joined = joined + swap(sums[dz * rows_x + dx], sizes, 0, dx).astype(f32)
        joined = joined.astype(bf16)
        if dz == steps[0]:
            joined, *own = lax.optimization_barrier((joined, *own))
        landed.append(swap(joined, sizes, dz, 0))
    for dx in side:
        landed.append(swap(own[dx], sizes, 0, dx))
    landed.append(own[0])
    total = add_all([term.astype(f32) for term in landed])
    total_other = swap_cores(total)
    return call(
        finish_kernel, jax.ShapeDtypeStruct((held, square), f32), 3, scalars=1, moved=held * square * 12
    )(half_at, total, total_other, core_blocks)


def solution(mesh):
    placed = (
        P(("groups", "batch", "pair"), None, None),
        P(("groups", "batch", "pair"), None),
        P(("groups", "batch", "pair"), None, "orb"),
        P(("groups", "batch", "pair"), "orb", None, None),
        P(("groups", "batch", "pair"), None),
        P(("groups", "batch", "pair"), None),
    )
    return jax.shard_map(
        per_device,
        mesh=mesh,
        in_specs=placed,
        out_specs=P(("groups", "batch", "pair"), None),
        check_vma=False,
    )
```

```python
import functools

import jax
import jax.numpy as jnp
from jax import lax
from jax.experimental import pallas as pl
from jax.experimental.pallas import tpu as pltpu
from jax.sharding import PartitionSpec as P

GO = 64
VMEM_LIMIT = 50 * 1024 * 1024
NT = (((1,), (1,)), ((), ()))


def split_dot(left, right, dims=None):
    if dims is None:
        return jnp.dot(left, right, preferred_element_type=jnp.float32)
    return lax.dot_general(left, right, dims, preferred_element_type=jnp.float32)


def prepare_kernel(half_ref, values_ref, left_ref, left_t_ref):
    batches, points, columns = values_ref.shape
    groups = columns // GO
    kept = left_ref.shape[2]
    first = half_ref[0] * (kept // groups)
    at = lax.broadcasted_iota(jnp.int32, (kept, columns), 0)
    lane = lax.broadcasted_iota(jnp.int32, (kept, columns), 1)
    wanted = (at % groups) * GO + first + at // groups
    select = jnp.where(lane == wanted, 1.0, 0.0).astype(jnp.bfloat16)
    for t in range(batches):
        left_ref[t] = split_dot(values_ref[t], select, NT).astype(jnp.bfloat16)
        left_t_ref[t] = split_dot(select, values_ref[t], NT).astype(jnp.bfloat16)


def index_kernel(held, fetch_ref, slots_ref, rows_ref):
    owners, capacity = fetch_ref.shape
    slots = slots_ref[...]
    entries = slots.shape[1]
    owner = slots // capacity
    owner_hot = jnp.where(lax.broadcasted_iota(jnp.int32, (owners, entries), 0) == owner, 1.0, 0.0)
    stored = fetch_ref[...].astype(jnp.float32).T.astype(jnp.bfloat16)
    listed = split_dot(stored, owner_hot.astype(jnp.bfloat16)).astype(jnp.int32)
    at = lax.broadcasted_iota(jnp.int32, (capacity, entries), 0)
    chosen = jnp.where(at == slots - owner * capacity, listed, 0)
    rows_ref[...] = jnp.sum(chosen, axis=0, keepdims=True) + owner * held


def row_table(core_ref, own_ref, other_ref, table_rows):
    low = core_ref[0] == 0
    rows = jnp.concatenate(
        [jnp.where(low, own_ref[...], other_ref[...]), jnp.where(low, other_ref[...], own_ref[...])], axis=1
    )
    row = lax.broadcasted_iota(jnp.int32, (table_rows, rows.shape[1]), 0)
    return jnp.where(row == rows, 1.0, 0.0)


def density_kernel(core_ref, table, own_ref, other_ref, left_ref, values_ref, out_ref, dense):
    batches, points, columns = values_ref.shape
    groups = columns // GO
    pick = row_table(core_ref, own_ref, other_ref, table.shape[0]).T.astype(jnp.bfloat16)
    low = lax.broadcasted_iota(jnp.int32, (1, 1, 1, groups, 128), 4) < GO
    for j in range(table.shape[1] // 128):
        lanes = slice(j * 128, (j + 1) * 128)
        got = split_dot(pick, table[:, lanes])
        got = got.reshape(2, batches, groups // 4, 2, groups, 128)
        even, odd = got[:, :, :, 0], got[:, :, :, 1]
        first = jnp.where(low, even, pltpu.roll(odd, GO, 4))
        second = jnp.where(low, pltpu.roll(even, GO, 4), odd)
        for t in range(batches):
            for q in range(groups // 2):
                at = (q // (groups // 4), t, q % (groups // 4))
                both = jnp.concatenate([first[at], second[at]], axis=0)
                dense[t, j * 2 * groups:(j + 1) * 2 * groups, q * 128:(q + 1) * 128] = both.astype(jnp.bfloat16)
    for t in range(batches):
        product = split_dot(left_ref[t], dense[t]) * values_ref[t].astype(jnp.float32)
        folded = product[:, :128]
        for q in range(1, columns // 128):
            folded = folded + product[:, q * 128:(q + 1) * 128]
        out_ref[t:t + 1, :] = jnp.sum(folded.T, axis=0, keepdims=True)


def scatter_kernel(
    core_ref, mine_ref, far_ref, weight_ref, values_ref, left_t_ref, own_ref, other_ref, out_ref, high, rest
):
    put = row_table(core_ref, own_ref, other_ref, out_ref.shape[0]).astype(jnp.bfloat16)
    batches, points, columns = values_ref.shape
    groups = columns // GO
    kept = left_t_ref.shape[1]
    steps = kept // (2 * groups)
    potential = weight_ref[...] * jnp.tanh(mine_ref[...] + far_ref[...])
    low = lax.broadcasted_iota(jnp.int32, (1, groups, 128), 2) < GO
    for t in range(batches):
        factor = jnp.broadcast_to(potential[t:t + 1, :], (128, points)).T
        factor = jnp.concatenate([factor] * (columns // 128), axis=1)
        weighted = (values_ref[t].astype(jnp.float32) * factor).astype(jnp.bfloat16)
        part = split_dot(left_t_ref[t], weighted)
        for q in range(groups // 2):
            cut = part[:, q * 128:(q + 1) * 128].reshape(steps, 2, groups, 128)
            first, second = cut[:, 0], cut[:, 1]
            even = jnp.where(low, first, pltpu.roll(second, GO, 2))
            odd = jnp.where(low, pltpu.roll(first, GO, 2), second)
            side, pair = q // (groups // 4), q % (groups // 4)
            at = ((side * batches + t) * (groups // 2) + 2 * pair) * groups
            for j in range(steps):
                both = jnp.concatenate([even[j], odd[j]], axis=0)
                top = both.astype(jnp.bfloat16)
                high[at:at + 2 * groups, j * 128:(j + 1) * 128] = top
                rest[at:at + 2 * groups, j * 128:(j + 1) * 128] = (both - top.astype(jnp.float32)).astype(jnp.bfloat16)
    step = min(out_ref.shape[0], 128)
    for at in range(0, out_ref.shape[0], step):
        some = put[at:at + step, :]
        total = split_dot(some, high[...]) + split_dot(some, rest[...])
        out_ref[at:at + step, :] = total.astype(jnp.bfloat16)


def finish_kernel(half_ref, mine_ref, other_ref, core_ref, out_ref):
    wide = mine_ref.shape[1]
    own = pl.multiple_of(half_ref[0] * wide, wide)
    far = pl.multiple_of((1 - half_ref[0]) * wide, wide)
    out_ref[:, pl.ds(own, wide)] = core_ref[:, pl.ds(own, wide)].astype(jnp.float32) + mine_ref[...]
    out_ref[:, pl.ds(far, wide)] = core_ref[:, pl.ds(far, wide)].astype(jnp.float32) + other_ref[...]


def call(kernel, outs, count, scratch=(), scalars=0, flops=0, moved=0):
    specs = [pl.BlockSpec(memory_space=pltpu.VMEM)] * count
    specs = [pl.BlockSpec(memory_space=pltpu.SMEM)] * scalars + specs
    out_specs = jax.tree.map(lambda _: pl.BlockSpec(memory_space=pltpu.VMEM), outs)
    return pl.pallas_call(
        kernel,
        out_shape=outs,
        in_specs=specs,
        out_specs=out_specs,
        scratch_shapes=list(scratch),
        compiler_params=pltpu.CompilerParams(vmem_limit_bytes=VMEM_LIMIT),
        cost_estimate=pl.CostEstimate(flops=flops, bytes_accessed=moved, transcendentals=0),
    )


def swap_cores(array):
    return lax.ppermute(array, "orb", [(0, 1), (1, 0)])


def per_device(basis_values, point_weights, slot_ids, fetch_rows, density_blocks, core_blocks):
    grid = ("batch", "pair")
    owners = lax.axis_size(grid)
    half = lax.axis_index("orb")
    batches, points, columns = basis_values.shape
    groups, own_groups = slot_ids.shape[1], slot_ids.shape[2]
    held, square = density_blocks.shape
    capacity = fetch_rows.shape[3]
    wide = square // 2
    table_rows = owners * held
    entries = batches * groups * groups
    kept = columns // 2
    bf16, f32 = jnp.bfloat16, jnp.float32

    own_rows = call(
        functools.partial(index_kernel, held),
        jax.ShapeDtypeStruct((1, batches * own_groups * groups), jnp.int32),
        2,
    )(fetch_rows.reshape(owners, capacity), slot_ids.transpose(0, 2, 1).reshape(1, -1))
    other_rows = swap_cores(own_rows)

    half_at = half.reshape(1).astype(jnp.int32)
    mine = lax.dynamic_slice_in_dim(density_blocks, half * wide, wide, 1)
    table = lax.all_to_all(jnp.tile(mine, (owners, 1)), grid, split_axis=0, concat_axis=0, tiled=True)

    left, left_t = call(
        prepare_kernel,
        (
            jax.ShapeDtypeStruct((batches, points, kept), bf16),
            jax.ShapeDtypeStruct((batches, kept, points), bf16),
        ),
        1,
        scalars=1,
        flops=4 * batches * points * columns * kept,
        moved=3 * batches * points * columns * 2,
    )(half_at, basis_values)

    partial = call(
        density_kernel,
        jax.ShapeDtypeStruct((batches, points), f32),
        5,
        scalars=1,
        scratch=(pltpu.VMEM((batches, kept, columns), bf16),),
        flops=2 * batches * points * columns * kept,
        moved=2 * batches * points * columns * 2,
    )(half_at, table, own_rows, other_rows, left, basis_values)
    partial_other = swap_cores(partial)

    sums = call(
        scatter_kernel,
        jax.ShapeDtypeStruct((table_rows, wide), bf16),
        7,
        scalars=1,
        scratch=(pltpu.VMEM((entries, wide), bf16), pltpu.VMEM((entries, wide), bf16)),
        flops=2 * batches * points * columns * kept,
        moved=2 * batches * points * columns * 2,
    )(half_at, partial, partial_other, point_weights, basis_values, left_t, own_rows, other_rows)
    landed = lax.all_to_all(sums, grid, split_axis=0, concat_axis=0, tiled=True)
    total = jnp.sum(landed.reshape(owners, held, wide).astype(f32), axis=0)
    total_other = swap_cores(total)
    return call(
        finish_kernel, jax.ShapeDtypeStruct((held, square), f32), 3, scalars=1, moved=held * square * 12
    )(half_at, total, total_other, core_blocks)


def solution(mesh):
    placed = (
        P(("groups", "batch", "pair"), None, None),
        P(("groups", "batch", "pair"), None),
        P(("groups", "batch", "pair"), None, "orb"),
        P(("groups", "batch", "pair"), "orb", None, None),
        P(("groups", "batch", "pair"), None),
        P(("groups", "batch", "pair"), None),
    )
    return jax.shard_map(
        per_device,
        mesh=mesh,
        in_specs=placed,
        out_specs=P(("groups", "batch", "pair"), None),
        check_vma=False,
    )
```

```python
import functools

import jax
import jax.numpy as jnp
from jax import lax
from jax.experimental import pallas as pl
from jax.experimental.pallas import tpu as pltpu
from jax.sharding import PartitionSpec as P

GO = 64
VMEM_LIMIT = 50 * 1024 * 1024
NT = (((1,), (1,)), ((), ()))


def split_dot(left, right, dims=None):
    if dims is None:
        return jnp.dot(left, right, preferred_element_type=jnp.float32)
    return lax.dot_general(left, right, dims, preferred_element_type=jnp.float32)


def prepare_kernel(half_ref, values_ref, left_ref, left_t_ref):
    batches, points, columns = values_ref.shape
    groups = columns // GO
    kept = left_ref.shape[2]
    first = half_ref[0] * (kept // groups)
    at = lax.broadcasted_iota(jnp.int32, (kept, columns), 0)
    lane = lax.broadcasted_iota(jnp.int32, (kept, columns), 1)
    wanted = (at % groups) * GO + first + at // groups
    select = jnp.where(lane == wanted, 1.0, 0.0).astype(jnp.bfloat16)
    for t in range(batches):
        left_ref[t] = split_dot(values_ref[t], select, NT).astype(jnp.bfloat16)
        left_t_ref[t] = split_dot(select, values_ref[t], NT).astype(jnp.bfloat16)


def index_kernel(held, fetch_ref, slots_ref, rows_ref):
    owners, capacity = fetch_ref.shape
    slots = slots_ref[...]
    entries = slots.shape[1]
    owner = slots // capacity
    owner_hot = jnp.where(lax.broadcasted_iota(jnp.int32, (owners, entries), 0) == owner, 1.0, 0.0)
    stored = fetch_ref[...].astype(jnp.float32).T.astype(jnp.bfloat16)
    listed = split_dot(stored, owner_hot.astype(jnp.bfloat16)).astype(jnp.int32)
    at = lax.broadcasted_iota(jnp.int32, (capacity, entries), 0)
    chosen = jnp.where(at == slots - owner * capacity, listed, 0)
    rows_ref[...] = jnp.sum(chosen, axis=0, keepdims=True) + owner * held


def row_table(stages, place_ref, core_ref, own_ref, other_ref, held):
    first_core = core_ref[0] == 0
    rows = jnp.concatenate(
        [
            jnp.where(first_core, own_ref[...], other_ref[...]),
            jnp.where(first_core, other_ref[...], own_ref[...]),
        ],
        axis=1,
    )
    owner = lax.bitwise_xor(rows // held, place_ref[0])
    at = rows % held
    for i, steps in enumerate(stages):
        here = [(owner // step) % 2 for step in steps]
        at = at + jnp.where(first_core, here[0], here[1]) * (held << i)
    row = lax.broadcasted_iota(jnp.int32, (held << len(stages), rows.shape[1]), 0)
    return jnp.where(row == at, 1.0, 0.0)


def density_kernel(stages, place_ref, core_ref, *refs):
    piece_refs = refs[:-7]
    own_ref, other_ref, left_ref, values_ref, out_ref, table, dense = refs[-7:]
    batches, points, columns = values_ref.shape
    groups = columns // GO
    held = table.shape[0] >> len(stages)
    at = 0
    for ref in piece_refs:
        table[at:at + ref.shape[0], :] = ref[...]
        at += ref.shape[0]
    pick = row_table(stages, place_ref, core_ref, own_ref, other_ref, held).T.astype(jnp.bfloat16)
    low = lax.broadcasted_iota(jnp.int32, (1, 1, 1, groups, 128), 4) < GO
    for j in range(table.shape[1] // 128):
        lanes = slice(j * 128, (j + 1) * 128)
        got = split_dot(pick, table[:, lanes])
        got = got.reshape(2, batches, groups // 4, 2, groups, 128)
        even, odd = got[:, :, :, 0], got[:, :, :, 1]
        first = jnp.where(low, even, pltpu.roll(odd, GO, 4))
        second = jnp.where(low, pltpu.roll(even, GO, 4), odd)
        for t in range(batches):
            for q in range(groups // 2):
                at = (q // (groups // 4), t, q % (groups // 4))
                both = jnp.concatenate([first[at], second[at]], axis=0)
                dense[t, j * 2 * groups:(j + 1) * 2 * groups, q * 128:(q + 1) * 128] = both.astype(jnp.bfloat16)
    for t in range(batches):
        product = split_dot(left_ref[t], dense[t]) * values_ref[t].astype(jnp.float32)
        folded = product[:, :128]
        for q in range(1, columns // 128):
            folded = folded + product[:, q * 128:(q + 1) * 128]
        out_ref[t:t + 1, :] = jnp.sum(folded.T, axis=0, keepdims=True)


def scatter_kernel(stages, place_ref, core_ref, *refs):
    mine_ref, far_ref, weight_ref, values_ref, left_t_ref, own_ref, other_ref = refs[:7]
    out_refs = refs[7:-2]
    high, rest = refs[-2:]
    part_rows = out_refs[0].shape[0]
    held = len(out_refs) * part_rows >> len(stages)
    put = row_table(stages, place_ref, core_ref, own_ref, other_ref, held).astype(jnp.bfloat16)
    batches, points, columns = values_ref.shape
    groups = columns // GO
    kept = left_t_ref.shape[1]
    steps = kept // (2 * groups)
    potential = weight_ref[...] * jnp.tanh(mine_ref[...] + far_ref[...])
    low = lax.broadcasted_iota(jnp.int32, (1, groups, 128), 2) < GO
    for t in range(batches):
        factor = jnp.broadcast_to(potential[t:t + 1, :], (128, points)).T
        factor = jnp.concatenate([factor] * (columns // 128), axis=1)
        weighted = (values_ref[t].astype(jnp.float32) * factor).astype(jnp.bfloat16)
        part = split_dot(left_t_ref[t], weighted)
        for q in range(groups // 2):
            cut = part[:, q * 128:(q + 1) * 128].reshape(steps, 2, groups, 128)
            first, second = cut[:, 0], cut[:, 1]
            even = jnp.where(low, first, pltpu.roll(second, GO, 2))
            odd = jnp.where(low, pltpu.roll(first, GO, 2), second)
            side, pair = q // (groups // 4), q % (groups // 4)
            at = ((side * batches + t) * (groups // 2) + 2 * pair) * groups
            for j in range(steps):
                both = jnp.concatenate([even[j], odd[j]], axis=0)
                top = both.astype(jnp.bfloat16)
                high[at:at + 2 * groups, j * 128:(j + 1) * 128] = top
                rest[at:at + 2 * groups, j * 128:(j + 1) * 128] = (both - top.astype(jnp.float32)).astype(jnp.bfloat16)
    step = min(put.shape[0], 128)
    for at in range(0, put.shape[0], step):
        some = put[at:at + step, :]
        total = (split_dot(some, high[...]) + split_dot(some, rest[...])).astype(jnp.bfloat16)
        size = min(step, part_rows)
        for i in range(0, step, size):
            part, begin = divmod(at + i, part_rows)
            out_refs[part][begin:begin + size, :] = total[i:i + size, :]


def finish_kernel(half_ref, mine_ref, other_ref, core_ref, out_ref):
    wide = mine_ref.shape[1]
    own = pl.multiple_of(half_ref[0] * wide, wide)
    far = pl.multiple_of((1 - half_ref[0]) * wide, wide)
    out_ref[:, pl.ds(own, wide)] = core_ref[:, pl.ds(own, wide)].astype(jnp.float32) + mine_ref[...]
    out_ref[:, pl.ds(far, wide)] = core_ref[:, pl.ds(far, wide)].astype(jnp.float32) + other_ref[...]


def call(kernel, outs, count, scratch=(), scalars=0, flops=0, moved=0):
    specs = [pl.BlockSpec(memory_space=pltpu.VMEM)] * count
    specs = [pl.BlockSpec(memory_space=pltpu.SMEM)] * scalars + specs
    out_specs = jax.tree.map(lambda _: pl.BlockSpec(memory_space=pltpu.VMEM), outs)
    return pl.pallas_call(
        kernel,
        out_shape=outs,
        in_specs=specs,
        out_specs=out_specs,
        scratch_shapes=list(scratch),
        compiler_params=pltpu.CompilerParams(vmem_limit_bytes=VMEM_LIMIT),
        cost_estimate=pl.CostEstimate(flops=flops, bytes_accessed=moved, transcendentals=0),
    )


def swap(array, owners, steps):
    pairs = [(i * 2 + core, (i ^ steps[core]) * 2 + core) for i in range(owners) for core in range(2)]
    return lax.ppermute(array, ("batch", "pair", "orb"), pairs)


def swap_cores(array):
    return lax.ppermute(array, "orb", [(0, 1), (1, 0)])


def per_device(basis_values, point_weights, slot_ids, fetch_rows, density_blocks, core_blocks):
    rows_z, rows_x = lax.axis_size("batch"), lax.axis_size("pair")
    z, x, core = lax.axis_index("batch"), lax.axis_index("pair"), lax.axis_index("orb")
    owners = rows_z * rows_x
    batches, points, columns = basis_values.shape
    groups, own_groups = slot_ids.shape[1], slot_ids.shape[2]
    held, square = density_blocks.shape
    capacity = fetch_rows.shape[3]
    wide = square // 2
    table_rows = owners * held
    entries = batches * groups * groups
    kept = columns // 2
    bf16, f32 = jnp.bfloat16, jnp.float32

    own_rows = call(
        functools.partial(index_kernel, held),
        jax.ShapeDtypeStruct((1, batches * own_groups * groups), jnp.int32),
        2,
    )(fetch_rows.reshape(owners, capacity), slot_ids.transpose(0, 2, 1).reshape(1, -1))
    other_rows = swap_cores(own_rows)

    along_z = [rows_x << i for i in reversed(range(rows_z.bit_length() - 1))]
    along_x = [1 << i for i in reversed(range(rows_x.bit_length() - 1))]
    stages = list(zip(along_z + along_x, along_z[:-1] + along_x + along_z[-1:]))

    mine = lax.dynamic_slice_in_dim(density_blocks, core * wide, wide, 1)
    pieces = [mine, swap(mine, owners, stages[0])]
    early = swap(mine, owners, stages[-1])
    early, pieces[-1], own_rows = lax.optimization_barrier((early, pieces[-1], own_rows))
    for steps in stages[1:-1]:
        pieces.append(swap(jnp.concatenate(pieces, axis=0), owners, steps))
    middle = pieces[1:-1]
    middle = middle[0] if len(middle) == 1 else jnp.concatenate(middle, axis=0)
    middle = swap(middle, owners, stages[-1])
    pieces[-1], middle, other_rows = lax.optimization_barrier((pieces[-1], middle, other_rows))
    pieces = pieces + [early, middle, swap(pieces[-1], owners, stages[-1])]

    core_at = core.reshape(1).astype(jnp.int32)
    half_at, _ = lax.optimization_barrier((core_at, pieces[-4]))
    left, left_t = call(
        prepare_kernel,
        (
            jax.ShapeDtypeStruct((batches, points, kept), bf16),
            jax.ShapeDtypeStruct((batches, kept, points), bf16),
        ),
        1,
        scalars=1,
        flops=4 * batches * points * columns * kept,
        moved=3 * batches * points * columns * 2,
    )(half_at, basis_values)

    place = (z * rows_x + x).reshape(1).astype(jnp.int32)
    partial = call(
        functools.partial(density_kernel, stages),
        jax.ShapeDtypeStruct((batches, points), f32),
        len(pieces) + 4,
        scalars=2,
        scratch=(pltpu.VMEM((table_rows, wide), bf16), pltpu.VMEM((batches, kept, columns), bf16)),
        flops=2 * batches * points * columns * kept,
        moved=2 * batches * points * columns * 2,
    )(place, core_at, *pieces, own_rows, other_rows, left, basis_values)
    partial_other = swap_cores(partial)

    quarter = jax.ShapeDtypeStruct((table_rows // 4, wide), bf16)
    none, upper, last, both = call(
        functools.partial(scatter_kernel, stages),
        [quarter] * 4,
        7,
        scalars=2,
        scratch=(pltpu.VMEM((entries, wide), bf16), pltpu.VMEM((entries, wide), bf16)),
        flops=2 * batches * points * columns * kept,
        moved=2 * batches * points * columns * 2,
    )(place, core_at, partial, partial_other, point_weights, basis_values, left_t, own_rows, other_rows)

    upper = upper.astype(f32) + swap(both, owners, stages[-1]).astype(f32)
    total = none.astype(f32) + swap(last, owners, stages[-1]).astype(f32)
    total = total + swap(upper.astype(bf16), owners, stages[-2]).astype(f32)
    for steps in reversed(stages[:-2]):
        rows = total.shape[0] // 2
        total = total[:rows] + swap(total[rows:].astype(bf16), owners, steps).astype(f32)
    total_other = swap_cores(total)
    return call(
        finish_kernel, jax.ShapeDtypeStruct((held, square), f32), 3, scalars=1, moved=held * square * 12
    )(core_at, total, total_other, core_blocks)


def solution(mesh):
    placed = (
        P(("groups", "batch", "pair"), None, None),
        P(("groups", "batch", "pair"), None),
        P(("groups", "batch", "pair"), None, "orb"),
        P(("groups", "batch", "pair"), "orb", None, None),
        P(("groups", "batch", "pair"), None),
        P(("groups", "batch", "pair"), None),
    )
    return jax.shard_map(
        per_device,
        mesh=mesh,
        in_specs=placed,
        out_specs=P(("groups", "batch", "pair"), None),
        check_vma=False,
    )
```

```python
import functools

import jax
import jax.numpy as jnp
from jax import lax
from jax.experimental import pallas as pl
from jax.experimental.pallas import tpu as pltpu
from jax.sharding import PartitionSpec as P

GO = 64
VMEM_LIMIT = 50 * 1024 * 1024
NT = (((1,), (1,)), ((), ()))


def split_dot(left, right, dims=None):
    if dims is None:
        return jnp.dot(left, right, preferred_element_type=jnp.float32)
    return lax.dot_general(left, right, dims, preferred_element_type=jnp.float32)


def prepare_kernel(half_ref, values_ref, left_ref, left_t_ref):
    batches, points, columns = values_ref.shape
    groups = columns // GO
    kept = left_ref.shape[2]
    first = half_ref[0] * (kept // groups)
    at = lax.broadcasted_iota(jnp.int32, (kept, columns), 0)
    lane = lax.broadcasted_iota(jnp.int32, (kept, columns), 1)
    wanted = (at % groups) * GO + first + at // groups
    select = jnp.where(lane == wanted, 1.0, 0.0).astype(jnp.bfloat16)
    for t in range(batches):
        left_ref[t] = split_dot(values_ref[t], select, NT).astype(jnp.bfloat16)
        left_t_ref[t] = split_dot(select, values_ref[t], NT).astype(jnp.bfloat16)


def index_kernel(held, fetch_ref, slots_ref, rows_ref):
    owners, capacity = fetch_ref.shape
    slots = slots_ref[...]
    entries = slots.shape[1]
    owner = slots // capacity
    owner_hot = jnp.where(lax.broadcasted_iota(jnp.int32, (owners, entries), 0) == owner, 1.0, 0.0)
    stored = fetch_ref[...].astype(jnp.float32).T.astype(jnp.bfloat16)
    listed = split_dot(stored, owner_hot.astype(jnp.bfloat16)).astype(jnp.int32)
    at = lax.broadcasted_iota(jnp.int32, (capacity, entries), 0)
    chosen = jnp.where(at == slots - owner * capacity, listed, 0)
    rows_ref[...] = jnp.sum(chosen, axis=0, keepdims=True) + owner * held


def row_table(place_ref, core_ref, own_ref, other_ref, held, owners):
    low = core_ref[0] == 0
    rows = jnp.concatenate(
        [jnp.where(low, own_ref[...], other_ref[...]), jnp.where(low, other_ref[...], own_ref[...])], axis=1
    )
    rows = lax.bitwise_xor(rows, place_ref[0] * held)
    row = lax.broadcasted_iota(jnp.int32, (owners * held, rows.shape[1]), 0)
    return jnp.where(row == rows, 1.0, 0.0)


def density_kernel(places, place_ref, core_ref, *refs):
    piece_refs = refs[:len(places)]
    own_ref, other_ref, left_ref, values_ref, out_ref, table, dense = refs[len(places):]
    batches, points, columns = values_ref.shape
    groups = columns // GO
    held = piece_refs[0].shape[0]
    for ref, k in zip(piece_refs, places):
        table[k * held:(k + 1) * held, :] = ref[...]
    pick = row_table(place_ref, core_ref, own_ref, other_ref, held, len(places)).T.astype(jnp.bfloat16)
    low = lax.broadcasted_iota(jnp.int32, (1, 1, 1, groups, 128), 4) < GO
    for j in range(table.shape[1] // 128):
        lanes = slice(j * 128, (j + 1) * 128)
        got = split_dot(pick, table[:, lanes])
        got = got.reshape(2, batches, groups // 4, 2, groups, 128)
        even, odd = got[:, :, :, 0], got[:, :, :, 1]
        first = jnp.where(low, even, pltpu.roll(odd, GO, 4))
        second = jnp.where(low, pltpu.roll(even, GO, 4), odd)
        for t in range(batches):
            for q in range(groups // 2):
                at = (q // (groups // 4), t, q % (groups // 4))
                both = jnp.concatenate([first[at], second[at]], axis=0)
                dense[t, j * 2 * groups:(j + 1) * 2 * groups, q * 128:(q + 1) * 128] = both.astype(jnp.bfloat16)
    for t in range(batches):
        product = split_dot(left_ref[t], dense[t]) * values_ref[t].astype(jnp.float32)
        folded = product[:, :128]
        for q in range(1, columns // 128):
            folded = folded + product[:, q * 128:(q + 1) * 128]
        out_ref[t:t + 1, :] = jnp.sum(folded.T, axis=0, keepdims=True)


def scatter_kernel(place_ref, core_ref, *refs):
    mine_ref, far_ref, weight_ref, values_ref, left_t_ref, own_ref, other_ref = refs[:7]
    out_refs = refs[7:-2]
    high, rest = refs[-2:]
    pieces = len(out_refs)
    held = out_refs[0].shape[0]
    put = row_table(place_ref, core_ref, own_ref, other_ref, held, pieces).astype(jnp.bfloat16)
    batches, points, columns = values_ref.shape
    groups = columns // GO
    kept = left_t_ref.shape[1]
    steps = kept // (2 * groups)
    potential = weight_ref[...] * jnp.tanh(mine_ref[...] + far_ref[...])
    low = lax.broadcasted_iota(jnp.int32, (1, groups, 128), 2) < GO
    for t in range(batches):
        factor = jnp.broadcast_to(potential[t:t + 1, :], (128, points)).T
        factor = jnp.concatenate([factor] * (columns // 128), axis=1)
        weighted = (values_ref[t].astype(jnp.float32) * factor).astype(jnp.bfloat16)
        part = split_dot(left_t_ref[t], weighted)
        for q in range(groups // 2):
            cut = part[:, q * 128:(q + 1) * 128].reshape(steps, 2, groups, 128)
            first, second = cut[:, 0], cut[:, 1]
            even = jnp.where(low, first, pltpu.roll(second, GO, 2))
            odd = jnp.where(low, pltpu.roll(first, GO, 2), second)
            side, pair = q // (groups // 4), q % (groups // 4)
            at = ((side * batches + t) * (groups // 2) + 2 * pair) * groups
            for j in range(steps):
                both = jnp.concatenate([even[j], odd[j]], axis=0)
                top = both.astype(jnp.bfloat16)
                high[at:at + 2 * groups, j * 128:(j + 1) * 128] = top
                rest[at:at + 2 * groups, j * 128:(j + 1) * 128] = (both - top.astype(jnp.float32)).astype(jnp.bfloat16)
    step = max(1, min(pieces, 128 // held))
    for k in range(0, pieces, step):
        some = put[k * held:(k + step) * held, :]
        total = split_dot(some, high[...]) + split_dot(some, rest[...])
        for i in range(step):
            out_refs[k + i][...] = total[i * held:(i + 1) * held, :].astype(jnp.bfloat16)


def finish_kernel(half_ref, mine_ref, other_ref, core_ref, out_ref):
    wide = mine_ref.shape[1]
    own = pl.multiple_of(half_ref[0] * wide, wide)
    far = pl.multiple_of((1 - half_ref[0]) * wide, wide)
    out_ref[:, pl.ds(own, wide)] = core_ref[:, pl.ds(own, wide)].astype(jnp.float32) + mine_ref[...]
    out_ref[:, pl.ds(far, wide)] = core_ref[:, pl.ds(far, wide)].astype(jnp.float32) + other_ref[...]


def call(kernel, outs, count, scratch=(), scalars=0, flops=0, moved=0):
    specs = [pl.BlockSpec(memory_space=pltpu.VMEM)] * count
    specs = [pl.BlockSpec(memory_space=pltpu.SMEM)] * scalars + specs
    out_specs = jax.tree.map(lambda _: pl.BlockSpec(memory_space=pltpu.VMEM), outs)
    return pl.pallas_call(
        kernel,
        out_shape=outs,
        in_specs=specs,
        out_specs=out_specs,
        scratch_shapes=list(scratch),
        compiler_params=pltpu.CompilerParams(vmem_limit_bytes=VMEM_LIMIT),
        cost_estimate=pl.CostEstimate(flops=flops, bytes_accessed=moved, transcendentals=0),
    )


def swap(array, axis, count, step):
    return lax.ppermute(array, axis, [(i, i ^ step) for i in range(count)])


def per_device(basis_values, point_weights, slot_ids, fetch_rows, density_blocks, core_blocks):
    rows_z, rows_x = lax.axis_size("batch"), lax.axis_size("pair")
    z, x, half = lax.axis_index("batch"), lax.axis_index("pair"), lax.axis_index("orb")
    owners = rows_z * rows_x
    batches, points, columns = basis_values.shape
    groups, own_groups = slot_ids.shape[1], slot_ids.shape[2]
    held, square = density_blocks.shape
    capacity = fetch_rows.shape[3]
    wide = square // 2
    table_rows = owners * held
    entries = batches * groups * groups
    kept = columns // 2
    bf16, f32 = jnp.bfloat16, jnp.float32

    own_rows = call(
        functools.partial(index_kernel, held),
        jax.ShapeDtypeStruct((1, batches * own_groups * groups), jnp.int32),
        2,
    )(fetch_rows.reshape(owners, capacity), slot_ids.transpose(0, 2, 1).reshape(1, -1))
    other_rows = swap(own_rows, "orb", 2, 1)

    steps = list(range(rows_z // 2, rows_z)) + list(range(1, rows_z // 2))
    side = list(range(1, rows_x))

    mine = lax.dynamic_slice_in_dim(density_blocks, half * wide, wide, 1)
    pieces = {0: mine}
    for dx in side:
        pieces[dx] = swap(mine, "pair", rows_x, dx)
    for dz in steps[::-1]:
        pieces[dz * rows_x] = swap(mine, "batch", rows_z, dz)
    first, last = steps[0] * rows_x, steps[-1] * rows_x
    pieces[first], own_rows = lax.optimization_barrier((pieces[first], own_rows))
    pieces[last], other_rows = lax.optimization_barrier((pieces[last], other_rows))
    for dz in steps[rows_z // 2:] + steps[:rows_z // 2]:
        for dx in side:
            pieces[dz * rows_x + dx] = swap(pieces[dz * rows_x], "pair", rows_x, dx)
    order = list(pieces)

    half_at, _ = lax.optimization_barrier((half.reshape(1).astype(jnp.int32), pieces[(rows_z - 1) * rows_x]))
    left, left_t = call(
        prepare_kernel,
        (
            jax.ShapeDtypeStruct((batches, points, kept), bf16),
            jax.ShapeDtypeStruct((batches, kept, points), bf16),
        ),
        1,
        scalars=1,
        flops=4 * batches * points * columns * kept,
        moved=3 * batches * points * columns * 2,
    )(half_at, basis_values)

    place = (z * rows_x + x).reshape(1).astype(jnp.int32)
    core_at = half.reshape(1).astype(jnp.int32)

    partial = call(
        functools.partial(density_kernel, order),
        jax.ShapeDtypeStruct((batches, points), f32),
        owners + 4,
        scalars=2,
        scratch=(pltpu.VMEM((table_rows, wide), bf16), pltpu.VMEM((batches, kept, columns), bf16)),
        flops=2 * batches * points * columns * kept,
        moved=2 * batches * points * columns * 2,
    )(place, core_at, *[pieces[k] for k in order], own_rows, other_rows, left, basis_values)
    partial_other = swap(partial, "orb", 2, 1)

    sums = call(
        scatter_kernel,
        [jax.ShapeDtypeStruct((held, wide), bf16)] * owners,
        7,
        scalars=2,
        scratch=(pltpu.VMEM((entries, wide), bf16), pltpu.VMEM((entries, wide), bf16)),
        flops=2 * batches * points * columns * kept,
        moved=2 * batches * points * columns * 2,
    )(place, core_at, partial, partial_other, point_weights, basis_values, left_t, own_rows, other_rows)

    landed = []
    own = sums[:rows_x]
    for dz in steps:
        joined = sums[dz * rows_x].astype(f32)
        for dx in side:
            joined = joined + swap(sums[dz * rows_x + dx], "pair", rows_x, dx).astype(f32)
        joined = joined.astype(bf16)
        if dz == steps[0]:
            joined, *own = lax.optimization_barrier((joined, *own))
        landed.append(swap(joined, "batch", rows_z, dz))
    for dx in side:
        landed.append(swap(own[dx], "pair", rows_x, dx))
    landed.append(own[0])
    total = landed[0].astype(f32)
    for term in landed[1:]:
        total = total + term.astype(f32)
    total_other = swap(total, "orb", 2, 1)
    return call(
        finish_kernel, jax.ShapeDtypeStruct((held, square), f32), 3, scalars=1, moved=held * square * 12
    )(half_at, total, total_other, core_blocks)


def solution(mesh):
    placed = (
        P(("groups", "batch", "pair"), None, None),
        P(("groups", "batch", "pair"), None),
        P(("groups", "batch", "pair"), None, "orb"),
        P(("groups", "batch", "pair"), "orb", None, None),
        P(("groups", "batch", "pair"), None),
        P(("groups", "batch", "pair"), None),
    )
    return jax.shard_map(
        per_device,
        mesh=mesh,
        in_specs=placed,
        out_specs=P(("groups", "batch", "pair"), None),
        check_vma=False,
    )
```

```python
import functools

import jax
import jax.numpy as jnp
from jax import lax
from jax.experimental import pallas as pl
from jax.experimental.pallas import tpu as pltpu
from jax.sharding import PartitionSpec as P

GO = 64
VMEM_LIMIT = 50 * 1024 * 1024
NT = (((1,), (1,)), ((), ()))


def split_dot(left, right, dims=None):
    if dims is None:
        return jnp.dot(left, right, preferred_element_type=jnp.float32)
    return lax.dot_general(left, right, dims, preferred_element_type=jnp.float32)


def prepare_kernel(half_ref, values_ref, left_ref, left_t_ref):
    batches, points, columns = values_ref.shape
    groups = columns // GO
    kept = left_ref.shape[2]
    first = half_ref[0] * (kept // groups)
    at = lax.broadcasted_iota(jnp.int32, (kept, columns), 0)
    lane = lax.broadcasted_iota(jnp.int32, (kept, columns), 1)
    wanted = (at % groups) * GO + first + at // groups
    select = jnp.where(lane == wanted, 1.0, 0.0).astype(jnp.bfloat16)
    for t in range(batches):
        left_ref[t] = split_dot(values_ref[t], select, NT).astype(jnp.bfloat16)
        left_t_ref[t] = split_dot(select, values_ref[t], NT).astype(jnp.bfloat16)


def index_kernel(held, fetch_ref, slots_ref, rows_ref):
    owners, capacity = fetch_ref.shape
    slots = slots_ref[...]
    entries = slots.shape[1]
    owner = slots // capacity
    owner_hot = jnp.where(lax.broadcasted_iota(jnp.int32, (owners, entries), 0) == owner, 1.0, 0.0)
    stored = fetch_ref[...].astype(jnp.float32).T.astype(jnp.bfloat16)
    listed = split_dot(stored, owner_hot.astype(jnp.bfloat16)).astype(jnp.int32)
    at = lax.broadcasted_iota(jnp.int32, (capacity, entries), 0)
    chosen = jnp.where(at == slots - owner * capacity, listed, 0)
    rows_ref[...] = jnp.sum(chosen, axis=0, keepdims=True) + owner * held


def row_table(place_ref, core_ref, own_ref, other_ref, held, owners):
    low = core_ref[0] == 0
    rows = jnp.concatenate(
        [jnp.where(low, own_ref[...], other_ref[...]), jnp.where(low, other_ref[...], own_ref[...])], axis=1
    )
    rows = lax.bitwise_xor(rows, place_ref[0] * held)
    row = lax.broadcasted_iota(jnp.int32, (owners * held, rows.shape[1]), 0)
    return jnp.where(row == rows, 1.0, 0.0)


def density_kernel(places, place_ref, core_ref, *refs):
    piece_refs = refs[:len(places)]
    own_ref, other_ref, left_ref, values_ref, out_ref, table, dense = refs[len(places):]
    batches, points, columns = values_ref.shape
    groups = columns // GO
    owners = sum(len(blocks) for blocks in places)
    held = table.shape[0] // owners
    for ref, blocks in zip(piece_refs, places):
        table[blocks[0] * held:(blocks[-1] + 1) * held, :] = ref[...]
    pick = row_table(place_ref, core_ref, own_ref, other_ref, held, owners).T.astype(jnp.bfloat16)
    low = lax.broadcasted_iota(jnp.int32, (1, 1, 1, groups, 128), 4) < GO
    for j in range(table.shape[1] // 128):
        lanes = slice(j * 128, (j + 1) * 128)
        got = split_dot(pick, table[:, lanes])
        got = got.reshape(2, batches, groups // 4, 2, groups, 128)
        even, odd = got[:, :, :, 0], got[:, :, :, 1]
        first = jnp.where(low, even, pltpu.roll(odd, GO, 4))
        second = jnp.where(low, pltpu.roll(even, GO, 4), odd)
        for t in range(batches):
            for q in range(groups // 2):
                at = (q // (groups // 4), t, q % (groups // 4))
                both = jnp.concatenate([first[at], second[at]], axis=0)
                dense[t, j * 2 * groups:(j + 1) * 2 * groups, q * 128:(q + 1) * 128] = both.astype(jnp.bfloat16)
    for t in range(batches):
        product = split_dot(left_ref[t], dense[t]) * values_ref[t].astype(jnp.float32)
        folded = product[:, :128]
        for q in range(1, columns // 128):
            folded = folded + product[:, q * 128:(q + 1) * 128]
        out_ref[t:t + 1, :] = jnp.sum(folded.T, axis=0, keepdims=True)


def scatter_kernel(places, place_ref, core_ref, *refs):
    mine_ref, far_ref, weight_ref, values_ref, left_t_ref, own_ref, other_ref = refs[:7]
    out_refs = refs[7:-2]
    high, rest = refs[-2:]
    target = {k: (ref, i) for ref, blocks in zip(out_refs, places) for i, k in enumerate(blocks)}
    pieces = len(target)
    held = out_refs[0].shape[0] // len(places[0])
    put = row_table(place_ref, core_ref, own_ref, other_ref, held, pieces).astype(jnp.bfloat16)
    batches, points, columns = values_ref.shape
    groups = columns // GO
    kept = left_t_ref.shape[1]
    steps = kept // (2 * groups)
    potential = weight_ref[...] * jnp.tanh(mine_ref[...] + far_ref[...])
    low = lax.broadcasted_iota(jnp.int32, (1, groups, 128), 2) < GO
    for t in range(batches):
        factor = jnp.broadcast_to(potential[t:t + 1, :], (128, points)).T
        factor = jnp.concatenate([factor] * (columns // 128), axis=1)
        weighted = (values_ref[t].astype(jnp.float32) * factor).astype(jnp.bfloat16)
        part = split_dot(left_t_ref[t], weighted)
        for q in range(groups // 2):
            cut = part[:, q * 128:(q + 1) * 128].reshape(steps, 2, groups, 128)
            first, second = cut[:, 0], cut[:, 1]
            even = jnp.where(low, first, pltpu.roll(second, GO, 2))
            odd = jnp.where(low, pltpu.roll(first, GO, 2), second)
            side, pair = q // (groups // 4), q % (groups // 4)
            at = ((side * batches + t) * (groups // 2) + 2 * pair) * groups
            for j in range(steps):
                both = jnp.concatenate([even[j], odd[j]], axis=0)
                top = both.astype(jnp.bfloat16)
                high[at:at + 2 * groups, j * 128:(j + 1) * 128] = top
                rest[at:at + 2 * groups, j * 128:(j + 1) * 128] = (both - top.astype(jnp.float32)).astype(jnp.bfloat16)
    step = max(1, min(pieces, 128 // held))
    for k in range(0, pieces, step):
        some = put[k * held:(k + step) * held, :]
        total = split_dot(some, high[...]) + split_dot(some, rest[...])
        for i in range(step):
            ref, at = target[k + i]
            ref[at * held:(at + 1) * held, :] = total[i * held:(i + 1) * held, :].astype(jnp.bfloat16)


def finish_kernel(half_ref, mine_ref, other_ref, core_ref, out_ref):
    wide = mine_ref.shape[1]
    own = pl.multiple_of(half_ref[0] * wide, wide)
    far = pl.multiple_of((1 - half_ref[0]) * wide, wide)
    out_ref[:, pl.ds(own, wide)] = core_ref[:, pl.ds(own, wide)].astype(jnp.float32) + mine_ref[...]
    out_ref[:, pl.ds(far, wide)] = core_ref[:, pl.ds(far, wide)].astype(jnp.float32) + other_ref[...]


def call(kernel, outs, count, scratch=(), scalars=0, flops=0, moved=0):
    specs = [pl.BlockSpec(memory_space=pltpu.VMEM)] * count
    specs = [pl.BlockSpec(memory_space=pltpu.SMEM)] * scalars + specs
    out_specs = jax.tree.map(lambda _: pl.BlockSpec(memory_space=pltpu.VMEM), outs)
    return pl.pallas_call(
        kernel,
        out_shape=outs,
        in_specs=specs,
        out_specs=out_specs,
        scratch_shapes=list(scratch),
        compiler_params=pltpu.CompilerParams(vmem_limit_bytes=VMEM_LIMIT),
        cost_estimate=pl.CostEstimate(flops=flops, bytes_accessed=moved, transcendentals=0),
    )


def swap(array, axis, count, step):
    return lax.ppermute(array, axis, [(i, i ^ step) for i in range(count)])


def per_device(basis_values, point_weights, slot_ids, fetch_rows, density_blocks, core_blocks):
    rows_z, rows_x = lax.axis_size("batch"), lax.axis_size("pair")
    z, x, half = lax.axis_index("batch"), lax.axis_index("pair"), lax.axis_index("orb")
    owners = rows_z * rows_x
    batches, points, columns = basis_values.shape
    groups, own_groups = slot_ids.shape[1], slot_ids.shape[2]
    held, square = density_blocks.shape
    capacity = fetch_rows.shape[3]
    wide = square // 2
    table_rows = owners * held
    entries = batches * groups * groups
    kept = columns // 2
    bf16, f32 = jnp.bfloat16, jnp.float32

    own_rows = call(
        functools.partial(index_kernel, held),
        jax.ShapeDtypeStruct((1, batches * own_groups * groups), jnp.int32),
        2,
    )(fetch_rows.reshape(owners, capacity), slot_ids.transpose(0, 2, 1).reshape(1, -1))
    other_rows = swap(own_rows, "orb", 2, 1)

    far = list(range(rows_z // 2, rows_z))
    near = list(range(1, rows_z // 2))
    side = list(range(1, rows_x))

    mine = lax.dynamic_slice_in_dim(density_blocks, half * wide, wide, 1)
    direct = {dz: swap(mine, "batch", rows_z, dz) for dz in far}
    beside = [swap(mine, "pair", rows_x, dx) for dx in side]
    *beside, own_rows = lax.optimization_barrier((*beside, own_rows))
    cluster = jnp.concatenate([mine, *beside], axis=0)
    arrays, places = [cluster], [list(range(rows_x))]
    for dz in near:
        arrays.append(swap(cluster, "batch", rows_z, dz))
        places.append(list(range(dz * rows_x, (dz + 1) * rows_x)))
    direct[far[0]], other_rows = lax.optimization_barrier((direct[far[0]], other_rows))
    for dz in far:
        arrays.append(direct[dz])
        places.append([dz * rows_x])
        for dx in side:
            arrays.append(swap(direct[dz], "pair", rows_x, dx))
            places.append([dz * rows_x + dx])

    half_at, _ = lax.optimization_barrier((half.reshape(1).astype(jnp.int32), direct[far[-1]]))
    left, left_t = call(
        prepare_kernel,
        (
            jax.ShapeDtypeStruct((batches, points, kept), bf16),
            jax.ShapeDtypeStruct((batches, kept, points), bf16),
        ),
        1,
        scalars=1,
        flops=4 * batches * points * columns * kept,
        moved=3 * batches * points * columns * 2,
    )(half_at, basis_values)

    place = (z * rows_x + x).reshape(1).astype(jnp.int32)
    core_at = half.reshape(1).astype(jnp.int32)

    partial = call(
        functools.partial(density_kernel, places),
        jax.ShapeDtypeStruct((batches, points), f32),
        len(arrays) + 4,
        scalars=2,
        scratch=(pltpu.VMEM((table_rows, wide), bf16), pltpu.VMEM((batches, kept, columns), bf16)),
        flops=2 * batches * points * columns * kept,
        moved=2 * batches * points * columns * 2,
    )(place, core_at, *arrays, own_rows, other_rows, left, basis_values)
    partial_other = swap(partial, "orb", 2, 1)

    out_places = [list(range(dz * rows_x, (dz + 1) * rows_x)) for dz in [0] + near]
    out_places += [[dz * rows_x + dx] for dz in far for dx in [0] + side]
    sums = call(
        functools.partial(scatter_kernel, out_places),
        [jax.ShapeDtypeStruct((held * len(blocks), wide), bf16) for blocks in out_places],
        7,
        scalars=2,
        scratch=(pltpu.VMEM((entries, wide), bf16), pltpu.VMEM((entries, wide), bf16)),
        flops=2 * batches * points * columns * kept,
        moved=2 * batches * points * columns * 2,
    )(place, core_at, partial, partial_other, point_weights, basis_values, left_t, own_rows, other_rows)

    clusters, singles = sums[:len(near) + 1], sums[len(near) + 1:]
    landed = []
    for i, dz in enumerate(far):
        joined = singles[i * rows_x].astype(f32)
        for dx in side:
            joined = joined + swap(singles[i * rows_x + dx], "pair", rows_x, dx).astype(f32)
        landed.append(swap(joined.astype(bf16), "batch", rows_z, dz).astype(f32))
    cluster = clusters[0].astype(f32)
    for dz, array in zip(near, clusters[1:]):
        cluster = cluster + swap(array, "batch", rows_z, dz).astype(f32)
    total = cluster[:held]
    for dx in side:
        total = total + swap(cluster[dx * held:(dx + 1) * held].astype(bf16), "pair", rows_x, dx).astype(f32)
    for term in landed:
        total = total + term
    total_other = swap(total, "orb", 2, 1)
    return call(
        finish_kernel, jax.ShapeDtypeStruct((held, square), f32), 3, scalars=1, moved=held * square * 12
    )(half_at, total, total_other, core_blocks)


def solution(mesh):
    placed = (
        P(("groups", "batch", "pair"), None, None),
        P(("groups", "batch", "pair"), None),
        P(("groups", "batch", "pair"), None, "orb"),
        P(("groups", "batch", "pair"), "orb", None, None),
        P(("groups", "batch", "pair"), None),
        P(("groups", "batch", "pair"), None),
    )
    return jax.shard_map(
        per_device,
        mesh=mesh,
        in_specs=placed,
        out_specs=P(("groups", "batch", "pair"), None),
        check_vma=False,
    )
```

```python
import functools

import jax
import jax.numpy as jnp
from jax import lax
from jax.experimental import pallas as pl
from jax.experimental.pallas import tpu as pltpu
from jax.sharding import PartitionSpec as P

GO = 64
VMEM_LIMIT = 50 * 1024 * 1024
NT = (((1,), (1,)), ((), ()))
TN = (((0,), (0,)), ((), ()))


def split_dot(left, right, dims=None):
    if dims is None:
        return jnp.dot(left, right, preferred_element_type=jnp.float32)
    return lax.dot_general(left, right, dims, preferred_element_type=jnp.float32)


def three_parts(values):
    top = values.astype(jnp.bfloat16)
    left = values - top.astype(jnp.float32)
    middle = left.astype(jnp.bfloat16)
    return top, middle, (left - middle.astype(jnp.float32)).astype(jnp.bfloat16)


def prepare_kernel(place_ref, half_ref, values_ref, own_ref, other_ref, left_ref, left_t_ref, pick_ref, put_ref):
    batches, points, columns = values_ref.shape
    groups = columns // GO
    kept = left_ref.shape[2]
    first = half_ref[0] * (kept // groups)
    at = lax.broadcasted_iota(jnp.int32, (kept, columns), 0)
    lane = lax.broadcasted_iota(jnp.int32, (kept, columns), 1)
    wanted = (at % groups) * GO + first + at // groups
    select = jnp.where(lane == wanted, 1.0, 0.0).astype(jnp.bfloat16)
    for t in range(batches):
        left_ref[t] = split_dot(values_ref[t], select, NT).astype(jnp.bfloat16)
        left_t_ref[t] = split_dot(select, values_ref[t], NT).astype(jnp.bfloat16)
    hot = row_table(place_ref, half_ref, own_ref, other_ref, put_ref.shape[0])
    put_ref[...] = hot.astype(jnp.bfloat16)
    pick_ref[...] = hot.T.astype(jnp.bfloat16)


def index_kernel(held, fetch_ref, slots_ref, rows_ref):
    owners, capacity = fetch_ref.shape
    slots = slots_ref[...]
    entries = slots.shape[1]
    owner = slots // capacity
    owner_hot = jnp.where(lax.broadcasted_iota(jnp.int32, (owners, entries), 0) == owner, 1.0, 0.0)
    stored = fetch_ref[...].astype(jnp.float32).T.astype(jnp.bfloat16)
    listed = split_dot(stored, owner_hot.astype(jnp.bfloat16)).astype(jnp.int32)
    at = lax.broadcasted_iota(jnp.int32, (capacity, entries), 0)
    chosen = jnp.where(at == slots - owner * capacity, listed, 0)
    rows_ref[...] = jnp.sum(chosen, axis=0, keepdims=True) + owner * held


def row_table(place_ref, core_ref, own_ref, other_ref, table_rows):
    low = core_ref[0] == 0
    rows = jnp.concatenate(
        [jnp.where(low, own_ref[...], other_ref[...]), jnp.where(low, other_ref[...], own_ref[...])], axis=1
    )
    rows = lax.bitwise_xor(rows, place_ref[0])
    row = lax.broadcasted_iota(jnp.int32, (table_rows, rows.shape[1]), 0)
    return jnp.where(row == rows, 1.0, 0.0)


def density_kernel(places, *refs):
    piece_refs = refs[:len(places)]
    pick_ref, left_ref, values_ref, out_ref, table, dense = refs[len(places):]
    batches, points, columns = values_ref.shape
    groups = columns // GO
    owners = sum(len(blocks) for blocks in places)
    held = table.shape[0] // owners
    for ref, blocks in zip(piece_refs, places):
        table[blocks[0] * held:(blocks[-1] + 1) * held, :] = ref[...]
    low = lax.broadcasted_iota(jnp.int32, (1, 1, 1, groups, 128), 4) < GO
    for chunk in range(table.shape[1] // 256):
        wide = split_dot(pick_ref[...], table[:, chunk * 256:(chunk + 1) * 256])
        for j in (2 * chunk, 2 * chunk + 1):
            got = wide[:, (j % 2) * 128:(j % 2 + 1) * 128].reshape(2, batches, groups // 4, 2, groups, 128)
            even, odd = got[:, :, :, 0], got[:, :, :, 1]
            first = jnp.where(low, even, pltpu.roll(odd, GO, 4))
            second = jnp.where(low, pltpu.roll(even, GO, 4), odd)
            for t in range(batches):
                for q in range(groups // 2):
                    at = (q // (groups // 4), t, q % (groups // 4))
                    both = jnp.concatenate([first[at], second[at]], axis=0)
                    dense[t, j * 2 * groups:(j + 1) * 2 * groups, q * 128:(q + 1) * 128] = both.astype(jnp.bfloat16)
    ones = jnp.ones((8, 128), jnp.bfloat16)
    for t in range(batches):
        product = split_dot(left_ref[t], dense[t]) * values_ref[t].astype(jnp.float32)
        folded = product[:, :128]
        for q in range(1, columns // 128):
            folded = folded + product[:, q * 128:(q + 1) * 128]
        top, middle, last = [split_dot(ones, part, NT) for part in three_parts(folded)]
        out_ref[t:t + 1, :] = (top + middle + last)[:1]


def scatter_kernel(places, *refs):
    mine_ref, far_ref, weight_ref, values_ref, left_t_ref, put_ref = refs[:6]
    out_refs = refs[6:-2]
    high, rest = refs[-2:]
    target = {k: (ref, i) for ref, blocks in zip(out_refs, places) for i, k in enumerate(blocks)}
    pieces = len(target)
    held = out_refs[0].shape[0] // len(places[0])
    batches, points, columns = values_ref.shape
    groups = columns // GO
    kept = left_t_ref.shape[1]
    steps = kept // (2 * groups)
    potential = weight_ref[...] * jnp.tanh(mine_ref[...] + far_ref[...])
    low = lax.broadcasted_iota(jnp.int32, (1, groups, 128), 2) < GO
    row = lax.broadcasted_iota(jnp.int32, (8, points), 0)
    ones = jnp.ones((8, 128), jnp.bfloat16)
    for t in range(batches):
        top, middle, last = [part.astype(jnp.float32) for part in three_parts(potential[t:t + 1, :])]
        stacked = jnp.where(row == 0, top, jnp.where(row == 1, middle, jnp.where(row == 2, last, 0.0)))
        factor = split_dot(stacked.astype(jnp.bfloat16), ones, TN)
        factor = jnp.concatenate([factor] * (columns // 128), axis=1)
        weighted = (values_ref[t].astype(jnp.float32) * factor).astype(jnp.bfloat16)
        part = split_dot(left_t_ref[t], weighted)
        for q in range(groups // 2):
            cut = part[:, q * 128:(q + 1) * 128].reshape(steps, 2, groups, 128)
            first, second = cut[:, 0], cut[:, 1]
            even = jnp.where(low, first, pltpu.roll(second, GO, 2))
            odd = jnp.where(low, pltpu.roll(first, GO, 2), second)
            side, pair = q // (groups // 4), q % (groups // 4)
            at = ((side * batches + t) * (groups // 2) + 2 * pair) * groups
            for j in range(steps):
                both = jnp.concatenate([even[j], odd[j]], axis=0)
                top = both.astype(jnp.bfloat16)
                high[at:at + 2 * groups, j * 128:(j + 1) * 128] = top
                rest[at:at + 2 * groups, j * 128:(j + 1) * 128] = (both - top.astype(jnp.float32)).astype(jnp.bfloat16)
    step = max(1, min(pieces, 128 // held))
    for k in range(0, pieces, step):
        some = put_ref[k * held:(k + step) * held, :]
        total = split_dot(some, high[...]) + split_dot(some, rest[...])
        for i in range(step):
            ref, at = target[k + i]
            ref[at * held:(at + 1) * held, :] = total[i * held:(i + 1) * held, :].astype(jnp.bfloat16)


def finish_kernel(half_ref, mine_ref, other_ref, core_ref, out_ref):
    wide = mine_ref.shape[1]
    own = pl.multiple_of(half_ref[0] * wide, wide)
    far = pl.multiple_of((1 - half_ref[0]) * wide, wide)
    out_ref[:, pl.ds(own, wide)] = core_ref[:, pl.ds(own, wide)].astype(jnp.float32) + mine_ref[...]
    out_ref[:, pl.ds(far, wide)] = core_ref[:, pl.ds(far, wide)].astype(jnp.float32) + other_ref[...]


def call(kernel, outs, count, scratch=(), scalars=0, flops=0, moved=0):
    specs = [pl.BlockSpec(memory_space=pltpu.VMEM)] * count
    specs = [pl.BlockSpec(memory_space=pltpu.SMEM)] * scalars + specs
    out_specs = jax.tree.map(lambda _: pl.BlockSpec(memory_space=pltpu.VMEM), outs)
    return pl.pallas_call(
        kernel,
        out_shape=outs,
        in_specs=specs,
        out_specs=out_specs,
        scratch_shapes=list(scratch),
        compiler_params=pltpu.CompilerParams(vmem_limit_bytes=VMEM_LIMIT),
        cost_estimate=pl.CostEstimate(flops=flops, bytes_accessed=moved, transcendentals=0),
    )


def swap(array, axis, count, step):
    return lax.ppermute(array, axis, [(i, i ^ step) for i in range(count)])


def per_device(basis_values, point_weights, slot_ids, fetch_rows, density_blocks, core_blocks):
    rows_z, rows_x = lax.axis_size("batch"), lax.axis_size("pair")
    z, x, half = lax.axis_index("batch"), lax.axis_index("pair"), lax.axis_index("orb")
    owners = rows_z * rows_x
    batches, points, columns = basis_values.shape
    groups, own_groups = slot_ids.shape[1], slot_ids.shape[2]
    held, square = density_blocks.shape
    capacity = fetch_rows.shape[3]
    wide = square // 2
    table_rows = owners * held
    entries = batches * groups * groups
    kept = columns // 2
    bf16, f32 = jnp.bfloat16, jnp.float32

    own_rows = call(
        functools.partial(index_kernel, held),
        jax.ShapeDtypeStruct((1, batches * own_groups * groups), jnp.int32),
        2,
    )(fetch_rows.reshape(owners, capacity), slot_ids.transpose(0, 2, 1).reshape(1, -1))
    other_rows = swap(own_rows, "orb", 2, 1)

    far = list(range(rows_z // 2, rows_z))
    near = list(range(1, rows_z // 2))
    side = list(range(1, rows_x))

    mine = lax.dynamic_slice_in_dim(density_blocks, half * wide, wide, 1)
    direct = {dz: swap(mine, "batch", rows_z, dz) for dz in far}
    beside = [swap(mine, "pair", rows_x, dx) for dx in side]
    *beside, own_rows = lax.optimization_barrier((*beside, own_rows))
    cluster = jnp.concatenate([mine, *beside], axis=0)
    arrays, places = [cluster], [list(range(rows_x))]
    for dz in near:
        arrays.append(swap(cluster, "batch", rows_z, dz))
        places.append(list(range(dz * rows_x, (dz + 1) * rows_x)))
    direct[far[0]], other_rows = lax.optimization_barrier((direct[far[0]], other_rows))
    for dz in far:
        arrays.append(direct[dz])
        places.append([dz * rows_x])
        for dx in side:
            arrays.append(swap(direct[dz], "pair", rows_x, dx))
            places.append([dz * rows_x + dx])

    half_at, _ = lax.optimization_barrier((half.reshape(1).astype(jnp.int32), direct[far[-1]]))
    place = ((z * rows_x + x) * held).reshape(1).astype(jnp.int32)
    left, left_t, pick, put = call(
        prepare_kernel,
        (
            jax.ShapeDtypeStruct((batches, points, kept), bf16),
            jax.ShapeDtypeStruct((batches, kept, points), bf16),
            jax.ShapeDtypeStruct((entries, table_rows), bf16),
            jax.ShapeDtypeStruct((table_rows, entries), bf16),
        ),
        3,
        scalars=2,
        flops=4 * batches * points * columns * kept,
        moved=3 * batches * points * columns * 2,
    )(place, half_at, basis_values, own_rows, other_rows)


    partial = call(
        functools.partial(density_kernel, places),
        jax.ShapeDtypeStruct((batches, points), f32),
        len(arrays) + 3,
        scratch=(pltpu.VMEM((table_rows, wide), bf16), pltpu.VMEM((batches, kept, columns), bf16)),
        flops=2 * batches * points * columns * kept,
        moved=2 * batches * points * columns * 2,
    )(*arrays, pick, left, basis_values)
    partial_other = swap(partial, "orb", 2, 1)

    out_places = [list(range(dz * rows_x, (dz + 1) * rows_x)) for dz in [0] + near]
    out_places += [[dz * rows_x + dx] for dz in far for dx in [0] + side]
    sums = call(
        functools.partial(scatter_kernel, out_places),
        [jax.ShapeDtypeStruct((held * len(blocks), wide), bf16) for blocks in out_places],
        6,
        scratch=(pltpu.VMEM((entries, wide), bf16), pltpu.VMEM((entries, wide), bf16)),
        flops=2 * batches * points * columns * kept,
        moved=2 * batches * points * columns * 2,
    )(partial, partial_other, point_weights, basis_values, left_t, put)

    clusters, singles = sums[:len(near) + 1], sums[len(near) + 1:]
    landed = []
    for i, dz in enumerate(far):
        joined = singles[i * rows_x].astype(f32)
        for dx in side:
            joined = joined + swap(singles[i * rows_x + dx], "pair", rows_x, dx).astype(f32)
        landed.append(swap(joined.astype(bf16), "batch", rows_z, dz).astype(f32))
    cluster = clusters[0].astype(f32)
    for dz, array in zip(near, clusters[1:]):
        cluster = cluster + swap(array, "batch", rows_z, dz).astype(f32)
    total = cluster[:held]
    for dx in side:
        total = total + swap(cluster[dx * held:(dx + 1) * held].astype(bf16), "pair", rows_x, dx).astype(f32)
    for term in landed:
        total = total + term
    total_other = swap(total, "orb", 2, 1)
    return call(
        finish_kernel, jax.ShapeDtypeStruct((held, square), f32), 3, scalars=1, moved=held * square * 12
    )(half_at, total, total_other, core_blocks)


def solution(mesh):
    placed = (
        P(("groups", "batch", "pair"), None, None),
        P(("groups", "batch", "pair"), None),
        P(("groups", "batch", "pair"), None, "orb"),
        P(("groups", "batch", "pair"), "orb", None, None),
        P(("groups", "batch", "pair"), None),
        P(("groups", "batch", "pair"), None),
    )
    return jax.shard_map(
        per_device,
        mesh=mesh,
        in_specs=placed,
        out_specs=P(("groups", "batch", "pair"), None),
        check_vma=False,
    )
```

```python
import functools

import jax
import jax.numpy as jnp
from jax import lax
from jax.experimental import pallas as pl
from jax.experimental.pallas import tpu as pltpu
from jax.sharding import PartitionSpec as P

GO = 64
VMEM_LIMIT = 50 * 1024 * 1024
NT = (((1,), (1,)), ((), ()))


def split_dot(left, right, dims=None):
    if dims is None:
        return jnp.dot(left, right, preferred_element_type=jnp.float32)
    return lax.dot_general(left, right, dims, preferred_element_type=jnp.float32)


def prepare_kernel(half_ref, values_ref, left_ref, left_t_ref):
    batches, points, columns = values_ref.shape
    groups = columns // GO
    kept = left_ref.shape[2]
    first = half_ref[0] * (kept // groups)
    at = lax.broadcasted_iota(jnp.int32, (kept, columns), 0)
    lane = lax.broadcasted_iota(jnp.int32, (kept, columns), 1)
    wanted = (at % groups) * GO + first + at // groups
    select = jnp.where(lane == wanted, 1.0, 0.0).astype(jnp.bfloat16)
    for t in range(batches):
        left_ref[t] = split_dot(values_ref[t], select, NT).astype(jnp.bfloat16)
        left_t_ref[t] = split_dot(select, values_ref[t], NT).astype(jnp.bfloat16)


def index_kernel(held, fetch_ref, slots_ref, rows_ref):
    owners, capacity = fetch_ref.shape
    slots = slots_ref[...]
    entries = slots.shape[1]
    owner = slots // capacity
    owner_hot = jnp.where(lax.broadcasted_iota(jnp.int32, (owners, entries), 0) == owner, 1.0, 0.0)
    stored = fetch_ref[...].astype(jnp.float32).T.astype(jnp.bfloat16)
    listed = split_dot(stored, owner_hot.astype(jnp.bfloat16)).astype(jnp.int32)
    at = lax.broadcasted_iota(jnp.int32, (capacity, entries), 0)
    chosen = jnp.where(at == slots - owner * capacity, listed, 0)
    rows_ref[...] = jnp.sum(chosen, axis=0, keepdims=True) + owner * held


def row_table(place_ref, core_ref, own_ref, other_ref, held, owners):
    low = core_ref[0] == 0
    rows = jnp.concatenate(
        [jnp.where(low, own_ref[...], other_ref[...]), jnp.where(low, other_ref[...], own_ref[...])], axis=1
    )
    rows = lax.bitwise_xor(rows, place_ref[0] * held)
    row = lax.broadcasted_iota(jnp.int32, (owners * held, rows.shape[1]), 0)
    return jnp.where(row == rows, 1.0, 0.0)


def density_kernel(places, place_ref, core_ref, *refs):
    piece_refs = refs[:len(places)]
    own_ref, other_ref, left_ref, values_ref, out_ref, table, dense = refs[len(places):]
    batches, points, columns = values_ref.shape
    groups = columns // GO
    owners = sum(len(blocks) for blocks in places)
    held = table.shape[0] // owners
    for ref, blocks in zip(piece_refs, places):
        table[blocks[0] * held:(blocks[-1] + 1) * held, :] = ref[...]
    pick = row_table(place_ref, core_ref, own_ref, other_ref, held, owners).T.astype(jnp.bfloat16)
    low = lax.broadcasted_iota(jnp.int32, (1, 1, 1, groups, 128), 4) < GO
    for chunk in range(table.shape[1] // 256):
        wide = split_dot(pick, table[:, chunk * 256:(chunk + 1) * 256])
        for j in (2 * chunk, 2 * chunk + 1):
            got = wide[:, (j % 2) * 128:(j % 2 + 1) * 128].reshape(2, batches, groups // 4, 2, groups, 128)
            even, odd = got[:, :, :, 0], got[:, :, :, 1]
            first = jnp.where(low, even, pltpu.roll(odd, GO, 4))
            second = jnp.where(low, pltpu.roll(even, GO, 4), odd)
            for t in range(batches):
                for q in range(groups // 2):
                    at = (q // (groups // 4), t, q % (groups // 4))
                    both = jnp.concatenate([first[at], second[at]], axis=0)
                    dense[t, j * 2 * groups:(j + 1) * 2 * groups, q * 128:(q + 1) * 128] = both.astype(jnp.bfloat16)
    for t in range(batches):
        product = split_dot(left_ref[t], dense[t]) * values_ref[t].astype(jnp.float32)
        folded = product[:, :128]
        for q in range(1, columns // 128):
            folded = folded + product[:, q * 128:(q + 1) * 128]
        out_ref[t:t + 1, :] = jnp.sum(folded.T, axis=0, keepdims=True)


def scatter_kernel(places, place_ref, core_ref, *refs):
    mine_ref, far_ref, weight_ref, values_ref, left_t_ref, own_ref, other_ref = refs[:7]
    out_refs = refs[7:-2]
    high, rest = refs[-2:]
    target = {k: (ref, i) for ref, blocks in zip(out_refs, places) for i, k in enumerate(blocks)}
    pieces = len(target)
    held = out_refs[0].shape[0] // len(places[0])
    put = row_table(place_ref, core_ref, own_ref, other_ref, held, pieces).astype(jnp.bfloat16)
    batches, points, columns = values_ref.shape
    groups = columns // GO
    kept = left_t_ref.shape[1]
    steps = kept // (2 * groups)
    potential = weight_ref[...] * jnp.tanh(mine_ref[...] + far_ref[...])
    low = lax.broadcasted_iota(jnp.int32, (1, groups, 128), 2) < GO
    for t in range(batches):
        factor = jnp.broadcast_to(potential[t:t + 1, :], (128, points)).T
        factor = jnp.concatenate([factor] * (columns // 128), axis=1)
        weighted = (values_ref[t].astype(jnp.float32) * factor).astype(jnp.bfloat16)
        part = split_dot(left_t_ref[t], weighted)
        for q in range(groups // 2):
            cut = part[:, q * 128:(q + 1) * 128].reshape(steps, 2, groups, 128)
            first, second = cut[:, 0], cut[:, 1]
            even = jnp.where(low, first, pltpu.roll(second, GO, 2))
            odd = jnp.where(low, pltpu.roll(first, GO, 2), second)
            side, pair = q // (groups // 4), q % (groups // 4)
            at = ((side * batches + t) * (groups // 2) + 2 * pair) * groups
            for j in range(steps):
                both = jnp.concatenate([even[j], odd[j]], axis=0)
                top = both.astype(jnp.bfloat16)
                high[at:at + 2 * groups, j * 128:(j + 1) * 128] = top
                rest[at:at + 2 * groups, j * 128:(j + 1) * 128] = (both - top.astype(jnp.float32)).astype(jnp.bfloat16)
    step = max(1, min(pieces, 128 // held))
    for k in range(0, pieces, step):
        some = put[k * held:(k + step) * held, :]
        total = split_dot(some, high[...]) + split_dot(some, rest[...])
        for i in range(step):
            ref, at = target[k + i]
            ref[at * held:(at + 1) * held, :] = total[i * held:(i + 1) * held, :].astype(jnp.bfloat16)


def finish_kernel(half_ref, mine_ref, other_ref, core_ref, out_ref):
    wide = mine_ref.shape[1]
    own = pl.multiple_of(half_ref[0] * wide, wide)
    far = pl.multiple_of((1 - half_ref[0]) * wide, wide)
    out_ref[:, pl.ds(own, wide)] = core_ref[:, pl.ds(own, wide)].astype(jnp.float32) + mine_ref[...]
    out_ref[:, pl.ds(far, wide)] = core_ref[:, pl.ds(far, wide)].astype(jnp.float32) + other_ref[...]


def call(kernel, outs, count, scratch=(), scalars=0, flops=0, moved=0):
    specs = [pl.BlockSpec(memory_space=pltpu.VMEM)] * count
    specs = [pl.BlockSpec(memory_space=pltpu.SMEM)] * scalars + specs
    out_specs = jax.tree.map(lambda _: pl.BlockSpec(memory_space=pltpu.VMEM), outs)
    return pl.pallas_call(
        kernel,
        out_shape=outs,
        in_specs=specs,
        out_specs=out_specs,
        scratch_shapes=list(scratch),
        compiler_params=pltpu.CompilerParams(vmem_limit_bytes=VMEM_LIMIT),
        cost_estimate=pl.CostEstimate(flops=flops, bytes_accessed=moved, transcendentals=0),
    )


def swap(array, axis, count, step):
    return lax.ppermute(array, axis, [(i, i ^ step) for i in range(count)])


def per_device(basis_values, point_weights, slot_ids, fetch_rows, density_blocks, core_blocks):
    rows_z, rows_x = lax.axis_size("batch"), lax.axis_size("pair")
    z, x, half = lax.axis_index("batch"), lax.axis_index("pair"), lax.axis_index("orb")
    owners = rows_z * rows_x
    batches, points, columns = basis_values.shape
    groups, own_groups = slot_ids.shape[1], slot_ids.shape[2]
    held, square = density_blocks.shape
    capacity = fetch_rows.shape[3]
    wide = square // 2
    table_rows = owners * held
    entries = batches * groups * groups
    kept = columns // 2
    bf16, f32 = jnp.bfloat16, jnp.float32

    own_rows = call(
        functools.partial(index_kernel, held),
        jax.ShapeDtypeStruct((1, batches * own_groups * groups), jnp.int32),
        2,
    )(fetch_rows.reshape(owners, capacity), slot_ids.transpose(0, 2, 1).reshape(1, -1))
    other_rows = swap(own_rows, "orb", 2, 1)

    far = list(range(rows_z // 2, rows_z))
    near = list(range(1, rows_z // 2))
    side = list(range(1, rows_x))

    mine = lax.dynamic_slice_in_dim(density_blocks, half * wide, wide, 1)
    direct = {dz: swap(mine, "batch", rows_z, dz) for dz in far}
    beside = [swap(mine, "pair", rows_x, dx) for dx in side]
    *beside, own_rows = lax.optimization_barrier((*beside, own_rows))
    arrays, places = [mine, *beside], [[dx] for dx in range(rows_x)]
    for dz in near:
        for dx, piece in enumerate([mine, *beside]):
            arrays.append(swap(piece, "batch", rows_z, dz))
            places.append([dz * rows_x + dx])
    direct[far[0]], other_rows = lax.optimization_barrier((direct[far[0]], other_rows))
    for dz in far:
        arrays.append(direct[dz])
        places.append([dz * rows_x])
        for dx in side:
            arrays.append(swap(direct[dz], "pair", rows_x, dx))
            places.append([dz * rows_x + dx])

    half_at, _ = lax.optimization_barrier((half.reshape(1).astype(jnp.int32), direct[far[-1]]))
    left, left_t = call(
        prepare_kernel,
        (
            jax.ShapeDtypeStruct((batches, points, kept), bf16),
            jax.ShapeDtypeStruct((batches, kept, points), bf16),
        ),
        1,
        scalars=1,
        flops=4 * batches * points * columns * kept,
        moved=3 * batches * points * columns * 2,
    )(half_at, basis_values)

    place = (z * rows_x + x).reshape(1).astype(jnp.int32)
    core_at = half.reshape(1).astype(jnp.int32)

    partial = call(
        functools.partial(density_kernel, places),
        jax.ShapeDtypeStruct((batches, points), f32),
        len(arrays) + 4,
        scalars=2,
        scratch=(pltpu.VMEM((table_rows, wide), bf16), pltpu.VMEM((batches, kept, columns), bf16)),
        flops=2 * batches * points * columns * kept,
        moved=2 * batches * points * columns * 2,
    )(place, core_at, *arrays, own_rows, other_rows, left, basis_values)
    partial_other = swap(partial, "orb", 2, 1)

    out_places = [list(range(dz * rows_x, (dz + 1) * rows_x)) for dz in [0] + near]
    out_places += [[dz * rows_x + dx] for dz in far for dx in [0] + side]
    sums = call(
        functools.partial(scatter_kernel, out_places),
        [jax.ShapeDtypeStruct((held * len(blocks), wide), bf16) for blocks in out_places],
        7,
        scalars=2,
        scratch=(pltpu.VMEM((entries, wide), bf16), pltpu.VMEM((entries, wide), bf16)),
        flops=2 * batches * points * columns * kept,
        moved=2 * batches * points * columns * 2,
    )(place, core_at, partial, partial_other, point_weights, basis_values, left_t, own_rows, other_rows)

    clusters, singles = sums[:len(near) + 1], sums[len(near) + 1:]
    landed = []
    for i, dz in enumerate(far):
        joined = singles[i * rows_x].astype(f32)
        for dx in side:
            joined = joined + swap(singles[i * rows_x + dx], "pair", rows_x, dx).astype(f32)
        landed.append(swap(joined.astype(bf16), "batch", rows_z, dz).astype(f32))
    cluster = clusters[0].astype(f32)
    for dz, array in zip(near, clusters[1:]):
        cluster = cluster + swap(array, "batch", rows_z, dz).astype(f32)
    total = cluster[:held]
    for dx in side:
        total = total + swap(cluster[dx * held:(dx + 1) * held].astype(bf16), "pair", rows_x, dx).astype(f32)
    for term in landed:
        total = total + term
    total_other = swap(total, "orb", 2, 1)
    return call(
        finish_kernel, jax.ShapeDtypeStruct((held, square), f32), 3, scalars=1, moved=held * square * 12
    )(half_at, total, total_other, core_blocks)


def solution(mesh):
    placed = (
        P(("groups", "batch", "pair"), None, None),
        P(("groups", "batch", "pair"), None),
        P(("groups", "batch", "pair"), None, "orb"),
        P(("groups", "batch", "pair"), "orb", None, None),
        P(("groups", "batch", "pair"), None),
        P(("groups", "batch", "pair"), None),
    )
    return jax.shard_map(
        per_device,
        mesh=mesh,
        in_specs=placed,
        out_specs=P(("groups", "batch", "pair"), None),
        check_vma=False,
    )
```

```python
import functools

import jax
import jax.numpy as jnp
from jax import lax
from jax.experimental import pallas as pl
from jax.experimental.pallas import tpu as pltpu
from jax.sharding import PartitionSpec as P

GO = 64
VMEM_LIMIT = 50 * 1024 * 1024
NT = (((1,), (1,)), ((), ()))


def split_dot(left, right, dims=None):
    if dims is None:
        return jnp.dot(left, right, preferred_element_type=jnp.float32)
    return lax.dot_general(left, right, dims, preferred_element_type=jnp.float32)


def prepare_kernel(half_ref, values_ref, left_ref, left_t_ref):
    batches, points, columns = values_ref.shape
    groups = columns // GO
    kept = left_ref.shape[2]
    first = half_ref[0] * (kept // groups)
    at = lax.broadcasted_iota(jnp.int32, (kept, columns), 0)
    lane = lax.broadcasted_iota(jnp.int32, (kept, columns), 1)
    wanted = (at % groups) * GO + first + at // groups
    select = jnp.where(lane == wanted, 1.0, 0.0).astype(jnp.bfloat16)
    for t in range(batches):
        left_ref[t] = split_dot(values_ref[t], select, NT).astype(jnp.bfloat16)
        left_t_ref[t] = split_dot(select, values_ref[t], NT).astype(jnp.bfloat16)


def index_kernel(held, fetch_ref, slots_ref, rows_ref):
    owners, capacity = fetch_ref.shape
    slots = slots_ref[...]
    entries = slots.shape[1]
    owner = slots // capacity
    owner_hot = jnp.where(lax.broadcasted_iota(jnp.int32, (owners, entries), 0) == owner, 1.0, 0.0)
    stored = fetch_ref[...].astype(jnp.float32).T.astype(jnp.bfloat16)
    listed = split_dot(stored, owner_hot.astype(jnp.bfloat16)).astype(jnp.int32)
    at = lax.broadcasted_iota(jnp.int32, (capacity, entries), 0)
    chosen = jnp.where(at == slots - owner * capacity, listed, 0)
    rows_ref[...] = jnp.sum(chosen, axis=0, keepdims=True) + owner * held


def row_table(place_ref, core_ref, own_ref, other_ref, held, owners):
    low = core_ref[0] == 0
    rows = jnp.concatenate(
        [jnp.where(low, own_ref[...], other_ref[...]), jnp.where(low, other_ref[...], own_ref[...])], axis=1
    )
    rows = lax.bitwise_xor(rows, place_ref[0] * held)
    row = lax.broadcasted_iota(jnp.int32, (owners * held, rows.shape[1]), 0)
    return jnp.where(row == rows, 1.0, 0.0)


def density_kernel(places, place_ref, core_ref, *refs):
    piece_refs = refs[:len(places)]
    own_ref, other_ref, left_ref, values_ref, out_ref, table, dense = refs[len(places):]
    batches, points, columns = values_ref.shape
    groups = columns // GO
    owners = sum(len(blocks) for blocks in places)
    held = table.shape[0] // owners
    for ref, blocks in zip(piece_refs, places):
        table[blocks[0] * held:(blocks[-1] + 1) * held, :] = ref[...]
    pick = row_table(place_ref, core_ref, own_ref, other_ref, held, owners).T.astype(jnp.bfloat16)
    low = lax.broadcasted_iota(jnp.int32, (1, 1, 1, groups, 128), 4) < GO
    for chunk in range(table.shape[1] // 256):
        wide = split_dot(pick, table[:, chunk * 256:(chunk + 1) * 256])
        for j in (2 * chunk, 2 * chunk + 1):
            got = wide[:, (j % 2) * 128:(j % 2 + 1) * 128].reshape(2, batches, groups // 4, 2, groups, 128)
            even, odd = got[:, :, :, 0], got[:, :, :, 1]
            first = jnp.where(low, even, pltpu.roll(odd, GO, 4))
            second = jnp.where(low, pltpu.roll(even, GO, 4), odd)
            for t in range(batches):
                for q in range(groups // 2):
                    at = (q // (groups // 4), t, q % (groups // 4))
                    both = jnp.concatenate([first[at], second[at]], axis=0)
                    dense[t, j * 2 * groups:(j + 1) * 2 * groups, q * 128:(q + 1) * 128] = both.astype(jnp.bfloat16)
    for t in range(batches):
        product = split_dot(left_ref[t], dense[t]) * values_ref[t].astype(jnp.float32)
        folded = product[:, :128]
        for q in range(1, columns // 128):
            folded = folded + product[:, q * 128:(q + 1) * 128]
        out_ref[t:t + 1, :] = jnp.sum(folded.T, axis=0, keepdims=True)


def scatter_kernel(places, place_ref, core_ref, *refs):
    mine_ref, far_ref, weight_ref, values_ref, left_t_ref, own_ref, other_ref = refs[:7]
    out_refs = refs[7:-2]
    high, rest = refs[-2:]
    target = {k: (ref, i) for ref, blocks in zip(out_refs, places) for i, k in enumerate(blocks)}
    pieces = len(target)
    held = out_refs[0].shape[0] // len(places[0])
    put = row_table(place_ref, core_ref, own_ref, other_ref, held, pieces).astype(jnp.bfloat16)
    batches, points, columns = values_ref.shape
    groups = columns // GO
    kept = left_t_ref.shape[1]
    steps = kept // (2 * groups)
    potential = weight_ref[...] * jnp.tanh(mine_ref[...] + far_ref[...])
    low = lax.broadcasted_iota(jnp.int32, (1, groups, 128), 2) < GO
    for t in range(batches):
        factor = jnp.broadcast_to(potential[t:t + 1, :], (128, points)).T
        factor = jnp.concatenate([factor] * (columns // 128), axis=1)
        weighted = (values_ref[t].astype(jnp.float32) * factor).astype(jnp.bfloat16)
        part = split_dot(left_t_ref[t], weighted)
        for q in range(groups // 2):
            cut = part[:, q * 128:(q + 1) * 128].reshape(steps, 2, groups, 128)
            first, second = cut[:, 0], cut[:, 1]
            even = jnp.where(low, first, pltpu.roll(second, GO, 2))
            odd = jnp.where(low, pltpu.roll(first, GO, 2), second)
            side, pair = q // (groups // 4), q % (groups // 4)
            at = ((side * batches + t) * (groups // 2) + 2 * pair) * groups
            for j in range(steps):
                both = jnp.concatenate([even[j], odd[j]], axis=0)
                top = both.astype(jnp.bfloat16)
                high[at:at + 2 * groups, j * 128:(j + 1) * 128] = top
                rest[at:at + 2 * groups, j * 128:(j + 1) * 128] = (both - top.astype(jnp.float32)).astype(jnp.bfloat16)
    step = max(1, min(pieces, 128 // held))
    for k in range(0, pieces, step):
        some = put[k * held:(k + step) * held, :]
        total = split_dot(some, high[...]) + split_dot(some, rest[...])
        for i in range(step):
            ref, at = target[k + i]
            ref[at * held:(at + 1) * held, :] = total[i * held:(i + 1) * held, :].astype(jnp.bfloat16)


def finish_kernel(half_ref, mine_ref, other_ref, core_ref, out_ref):
    wide = mine_ref.shape[1]
    own = pl.multiple_of(half_ref[0] * wide, wide)
    far = pl.multiple_of((1 - half_ref[0]) * wide, wide)
    out_ref[:, pl.ds(own, wide)] = core_ref[:, pl.ds(own, wide)].astype(jnp.float32) + mine_ref[...]
    out_ref[:, pl.ds(far, wide)] = core_ref[:, pl.ds(far, wide)].astype(jnp.float32) + other_ref[...]


def call(kernel, outs, count, scratch=(), scalars=0, flops=0, moved=0):
    specs = [pl.BlockSpec(memory_space=pltpu.VMEM)] * count
    specs = [pl.BlockSpec(memory_space=pltpu.SMEM)] * scalars + specs
    out_specs = jax.tree.map(lambda _: pl.BlockSpec(memory_space=pltpu.VMEM), outs)
    return pl.pallas_call(
        kernel,
        out_shape=outs,
        in_specs=specs,
        out_specs=out_specs,
        scratch_shapes=list(scratch),
        compiler_params=pltpu.CompilerParams(vmem_limit_bytes=VMEM_LIMIT),
        cost_estimate=pl.CostEstimate(flops=flops, bytes_accessed=moved, transcendentals=0),
    )


def swap(array, axis, count, step):
    return lax.ppermute(array, axis, [(i, i ^ step) for i in range(count)])


def swap_both(array, sizes, dz, dx):
    step = dz * sizes[1] + dx
    return lax.ppermute(array, ("batch", "pair"), [(i, i ^ step) for i in range(sizes[0] * sizes[1])])


def per_device(basis_values, point_weights, slot_ids, fetch_rows, density_blocks, core_blocks):
    rows_z, rows_x = lax.axis_size("batch"), lax.axis_size("pair")
    z, x, half = lax.axis_index("batch"), lax.axis_index("pair"), lax.axis_index("orb")
    owners = rows_z * rows_x
    batches, points, columns = basis_values.shape
    groups, own_groups = slot_ids.shape[1], slot_ids.shape[2]
    held, square = density_blocks.shape
    capacity = fetch_rows.shape[3]
    wide = square // 2
    table_rows = owners * held
    entries = batches * groups * groups
    kept = columns // 2
    bf16, f32 = jnp.bfloat16, jnp.float32

    own_rows = call(
        functools.partial(index_kernel, held),
        jax.ShapeDtypeStruct((1, batches * own_groups * groups), jnp.int32),
        2,
    )(fetch_rows.reshape(owners, capacity), slot_ids.transpose(0, 2, 1).reshape(1, -1))
    other_rows = swap(own_rows, "orb", 2, 1)

    far = list(range(rows_z // 2, rows_z))
    near = list(range(1, rows_z // 2))
    side = list(range(1, rows_x))

    mine = lax.dynamic_slice_in_dim(density_blocks, half * wide, wide, 1)
    direct = {dz: swap(mine, "batch", rows_z, dz) for dz in far}
    beside = [swap(mine, "pair", rows_x, dx) for dx in side]
    *beside, own_rows = lax.optimization_barrier((*beside, own_rows))
    cluster = jnp.concatenate([mine, *beside], axis=0)
    arrays, places = [cluster], [list(range(rows_x))]
    for dz in near:
        arrays.append(swap(cluster, "batch", rows_z, dz))
        places.append(list(range(dz * rows_x, (dz + 1) * rows_x)))
    direct[far[0]], other_rows = lax.optimization_barrier((direct[far[0]], other_rows))
    arrays.append(direct[far[0]])
    places.append([far[0] * rows_x])
    for dx in side:
        arrays.append(swap(direct[far[0]], "pair", rows_x, dx))
        places.append([far[0] * rows_x + dx])
    for dz in far[1:]:
        for dx in [0] + side:
            arrays.append(direct[dz] if dx == 0 else swap_both(mine, (rows_z, rows_x), dz, dx))
            places.append([dz * rows_x + dx])

    half_at, _ = lax.optimization_barrier((half.reshape(1).astype(jnp.int32), direct[far[-1]]))
    left, left_t = call(
        prepare_kernel,
        (
            jax.ShapeDtypeStruct((batches, points, kept), bf16),
            jax.ShapeDtypeStruct((batches, kept, points), bf16),
        ),
        1,
        scalars=1,
        flops=4 * batches * points * columns * kept,
        moved=3 * batches * points * columns * 2,
    )(half_at, basis_values)

    place = (z * rows_x + x).reshape(1).astype(jnp.int32)
    core_at = half.reshape(1).astype(jnp.int32)

    partial = call(
        functools.partial(density_kernel, places),
        jax.ShapeDtypeStruct((batches, points), f32),
        len(arrays) + 4,
        scalars=2,
        scratch=(pltpu.VMEM((table_rows, wide), bf16), pltpu.VMEM((batches, kept, columns), bf16)),
        flops=2 * batches * points * columns * kept,
        moved=2 * batches * points * columns * 2,
    )(place, core_at, *arrays, own_rows, other_rows, left, basis_values)
    partial_other = swap(partial, "orb", 2, 1)

    out_places = [list(range(dz * rows_x, (dz + 1) * rows_x)) for dz in [0] + near]
    out_places += [[dz * rows_x + dx] for dz in far for dx in [0] + side]
    sums = call(
        functools.partial(scatter_kernel, out_places),
        [jax.ShapeDtypeStruct((held * len(blocks), wide), bf16) for blocks in out_places],
        7,
        scalars=2,
        scratch=(pltpu.VMEM((entries, wide), bf16), pltpu.VMEM((entries, wide), bf16)),
        flops=2 * batches * points * columns * kept,
        moved=2 * batches * points * columns * 2,
    )(place, core_at, partial, partial_other, point_weights, basis_values, left_t, own_rows, other_rows)

    clusters, singles = sums[:len(near) + 1], sums[len(near) + 1:]
    joined = singles[0].astype(f32)
    for dx in side:
        joined = joined + swap(singles[dx], "pair", rows_x, dx).astype(f32)
    landed = [swap(joined.astype(bf16), "batch", rows_z, far[0]).astype(f32)]
    for i, dz in enumerate(far[1:]):
        for dx in [0] + side:
            array = singles[(i + 1) * rows_x + dx]
            landed.append(swap_both(array, (rows_z, rows_x), dz, dx).astype(f32))
    cluster = clusters[0].astype(f32)
    for dz, array in zip(near, clusters[1:]):
        cluster = cluster + swap(array, "batch", rows_z, dz).astype(f32)
    total = cluster[:held]
    for dx in side:
        total = total + swap(cluster[dx * held:(dx + 1) * held].astype(bf16), "pair", rows_x, dx).astype(f32)
    for term in landed:
        total = total + term
    total_other = swap(total, "orb", 2, 1)
    return call(
        finish_kernel, jax.ShapeDtypeStruct((held, square), f32), 3, scalars=1, moved=held * square * 12
    )(half_at, total, total_other, core_blocks)


def solution(mesh):
    placed = (
        P(("groups", "batch", "pair"), None, None),
        P(("groups", "batch", "pair"), None),
        P(("groups", "batch", "pair"), None, "orb"),
        P(("groups", "batch", "pair"), "orb", None, None),
        P(("groups", "batch", "pair"), None),
        P(("groups", "batch", "pair"), None),
    )
    return jax.shard_map(
        per_device,
        mesh=mesh,
        in_specs=placed,
        out_specs=P(("groups", "batch", "pair"), None),
        check_vma=False,
    )
```

```python
import functools

import jax
import jax.numpy as jnp
from jax import lax
from jax.experimental import pallas as pl
from jax.experimental.pallas import tpu as pltpu
from jax.sharding import PartitionSpec as P

GO = 64
VMEM_LIMIT = 50 * 1024 * 1024
NT = (((1,), (1,)), ((), ()))


def split_dot(left, right, dims=None):
    if dims is None:
        return jnp.dot(left, right, preferred_element_type=jnp.float32)
    return lax.dot_general(left, right, dims, preferred_element_type=jnp.float32)


def prepare_kernel(half_ref, values_ref, left_ref, left_t_ref):
    batches, points, columns = values_ref.shape
    groups = columns // GO
    kept = left_ref.shape[2]
    first = half_ref[0] * (kept // groups)
    at = lax.broadcasted_iota(jnp.int32, (kept, columns), 0)
    lane = lax.broadcasted_iota(jnp.int32, (kept, columns), 1)
    wanted = (at % groups) * GO + first + at // groups
    select = jnp.where(lane == wanted, 1.0, 0.0).astype(jnp.bfloat16)

    @pl.loop(0, batches)
    def _(t):
        left_ref[t] = split_dot(values_ref[t], select, NT).astype(jnp.bfloat16)
        left_t_ref[t] = split_dot(select, values_ref[t], NT).astype(jnp.bfloat16)


def index_kernel(held, fetch_ref, slots_ref, rows_ref):
    owners, capacity = fetch_ref.shape
    slots = slots_ref[...]
    entries = slots.shape[1]
    owner = slots // capacity
    owner_hot = jnp.where(lax.broadcasted_iota(jnp.int32, (owners, entries), 0) == owner, 1.0, 0.0)
    stored = fetch_ref[...].astype(jnp.float32).T.astype(jnp.bfloat16)
    listed = split_dot(stored, owner_hot.astype(jnp.bfloat16)).astype(jnp.int32)
    at = lax.broadcasted_iota(jnp.int32, (capacity, entries), 0)
    chosen = jnp.where(at == slots - owner * capacity, listed, 0)
    rows_ref[...] = jnp.sum(chosen, axis=0, keepdims=True) + owner * held


def row_table(place_ref, core_ref, own_ref, other_ref, held, owners):
    low = core_ref[0] == 0
    rows = jnp.concatenate(
        [jnp.where(low, own_ref[...], other_ref[...]), jnp.where(low, other_ref[...], own_ref[...])], axis=1
    )
    rows = lax.bitwise_xor(rows, place_ref[0] * held)
    row = lax.broadcasted_iota(jnp.int32, (owners * held, rows.shape[1]), 0)
    return jnp.where(row == rows, 1.0, 0.0)


def density_kernel(places, place_ref, core_ref, *refs):
    piece_refs = refs[:len(places)]
    own_ref, other_ref, left_ref, values_ref, out_ref, table, dense = refs[len(places):]
    batches, points, columns = values_ref.shape
    groups = columns // GO
    owners = sum(len(blocks) for blocks in places)
    held = table.shape[0] // owners
    for ref, blocks in zip(piece_refs, places):
        table[blocks[0] * held:(blocks[-1] + 1) * held, :] = ref[...]
    pick = row_table(place_ref, core_ref, own_ref, other_ref, held, owners).T.astype(jnp.bfloat16)
    low = lax.broadcasted_iota(jnp.int32, (1, 1, 1, groups, 128), 4) < GO
    @pl.loop(0, table.shape[1] // 256)
    def _(chunk):
        wide = split_dot(pick, table[:, pl.ds(pl.multiple_of(chunk * 256, 256), 256)])
        for j in range(2):
            got = wide[:, j * 128:(j + 1) * 128].reshape(2, batches, groups // 4, 2, groups, 128)
            even, odd = got[:, :, :, 0], got[:, :, :, 1]
            first = jnp.where(low, even, pltpu.roll(odd, GO, 4))
            second = jnp.where(low, pltpu.roll(even, GO, 4), odd)
            rows = pl.ds(pl.multiple_of((2 * chunk + j) * 2 * groups, 2 * groups), 2 * groups)
            for t in range(batches):
                for q in range(groups // 2):
                    at = (q // (groups // 4), t, q % (groups // 4))
                    both = jnp.concatenate([first[at], second[at]], axis=0)
                    dense[t, rows, q * 128:(q + 1) * 128] = both.astype(jnp.bfloat16)

    @pl.loop(0, batches)
    def _(t):
        product = split_dot(left_ref[t], dense[t]) * values_ref[t].astype(jnp.float32)
        folded = product[:, :128]
        for q in range(1, columns // 128):
            folded = folded + product[:, q * 128:(q + 1) * 128]
        out_ref[pl.ds(t, 1), :] = jnp.sum(folded.T, axis=0, keepdims=True)


def scatter_kernel(places, place_ref, core_ref, *refs):
    mine_ref, far_ref, weight_ref, values_ref, left_t_ref, own_ref, other_ref = refs[:7]
    out_refs = refs[7:-3]
    high, rest, potential = refs[-3:]
    target = {k: (ref, i) for ref, blocks in zip(out_refs, places) for i, k in enumerate(blocks)}
    pieces = len(target)
    held = out_refs[0].shape[0] // len(places[0])
    put = row_table(place_ref, core_ref, own_ref, other_ref, held, pieces).astype(jnp.bfloat16)
    batches, points, columns = values_ref.shape
    groups = columns // GO
    kept = left_t_ref.shape[1]
    steps = kept // (2 * groups)
    potential[...] = weight_ref[...] * jnp.tanh(mine_ref[...] + far_ref[...])
    low = lax.broadcasted_iota(jnp.int32, (1, groups, 128), 2) < GO

    @pl.loop(0, batches)
    def _(t):
        factor = jnp.broadcast_to(potential[pl.ds(t, 1), :], (128, points)).T
        factor = jnp.concatenate([factor] * (columns // 128), axis=1)
        weighted = (values_ref[t].astype(jnp.float32) * factor).astype(jnp.bfloat16)
        part = split_dot(left_t_ref[t], weighted)
        for q in range(groups // 2):
            cut = part[:, q * 128:(q + 1) * 128].reshape(steps, 2, groups, 128)
            first, second = cut[:, 0], cut[:, 1]
            even = jnp.where(low, first, pltpu.roll(second, GO, 2))
            odd = jnp.where(low, pltpu.roll(first, GO, 2), second)
            side, pair = q // (groups // 4), q % (groups // 4)
            at = ((side * batches + t) * (groups // 2) + 2 * pair) * groups
            rows = pl.ds(pl.multiple_of(at, 2 * groups), 2 * groups)
            for j in range(steps):
                both = jnp.concatenate([even[j], odd[j]], axis=0)
                top = both.astype(jnp.bfloat16)
                high[rows, j * 128:(j + 1) * 128] = top
                rest[rows, j * 128:(j + 1) * 128] = (both - top.astype(jnp.float32)).astype(jnp.bfloat16)

    step = max(1, min(pieces, 128 // held))
    for k in range(0, pieces, step):

        @pl.loop(0, high.shape[1] // 512)
        def _(chunk):
            lanes = pl.ds(pl.multiple_of(chunk * 512, 512), 512)
            some = put[k * held:(k + step) * held, :]
            total = split_dot(some, high[:, lanes]) + split_dot(some, rest[:, lanes])
            for i in range(step):
                ref, at = target[k + i]
                ref[at * held:(at + 1) * held, lanes] = total[i * held:(i + 1) * held, :].astype(jnp.bfloat16)


def finish_kernel(half_ref, mine_ref, other_ref, core_ref, out_ref):
    wide = mine_ref.shape[1]
    own = pl.multiple_of(half_ref[0] * wide, wide)
    far = pl.multiple_of((1 - half_ref[0]) * wide, wide)
    out_ref[:, pl.ds(own, wide)] = core_ref[:, pl.ds(own, wide)].astype(jnp.float32) + mine_ref[...]
    out_ref[:, pl.ds(far, wide)] = core_ref[:, pl.ds(far, wide)].astype(jnp.float32) + other_ref[...]


def call(kernel, outs, count, scratch=(), scalars=0, flops=0, moved=0):
    specs = [pl.BlockSpec(memory_space=pltpu.VMEM)] * count
    specs = [pl.BlockSpec(memory_space=pltpu.SMEM)] * scalars + specs
    out_specs = jax.tree.map(lambda _: pl.BlockSpec(memory_space=pltpu.VMEM), outs)
    return pl.pallas_call(
        kernel,
        out_shape=outs,
        in_specs=specs,
        out_specs=out_specs,
        scratch_shapes=list(scratch),
        compiler_params=pltpu.CompilerParams(vmem_limit_bytes=VMEM_LIMIT),
        cost_estimate=pl.CostEstimate(flops=flops, bytes_accessed=moved, transcendentals=0),
    )


def swap(array, axis, count, step):
    return lax.ppermute(array, axis, [(i, i ^ step) for i in range(count)])


def per_device(basis_values, point_weights, slot_ids, fetch_rows, density_blocks, core_blocks):
    rows_z, rows_x = lax.axis_size("batch"), lax.axis_size("pair")
    z, x, half = lax.axis_index("batch"), lax.axis_index("pair"), lax.axis_index("orb")
    owners = rows_z * rows_x
    batches, points, columns = basis_values.shape
    groups, own_groups = slot_ids.shape[1], slot_ids.shape[2]
    held, square = density_blocks.shape
    capacity = fetch_rows.shape[3]
    wide = square // 2
    table_rows = owners * held
    entries = batches * groups * groups
    kept = columns // 2
    bf16, f32 = jnp.bfloat16, jnp.float32

    own_rows = call(
        functools.partial(index_kernel, held),
        jax.ShapeDtypeStruct((1, batches * own_groups * groups), jnp.int32),
        2,
    )(fetch_rows.reshape(owners, capacity), slot_ids.transpose(0, 2, 1).reshape(1, -1))
    other_rows = swap(own_rows, "orb", 2, 1)

    far = list(range(rows_z // 2, rows_z))
    near = list(range(1, rows_z // 2))
    side = list(range(1, rows_x))

    mine = lax.dynamic_slice_in_dim(density_blocks, half * wide, wide, 1)
    direct = {dz: swap(mine, "batch", rows_z, dz) for dz in far}
    beside = [swap(mine, "pair", rows_x, dx) for dx in side]
    *beside, own_rows = lax.optimization_barrier((*beside, own_rows))
    cluster = jnp.concatenate([mine, *beside], axis=0)
    arrays, places = [cluster], [list(range(rows_x))]
    for dz in near:
        arrays.append(swap(cluster, "batch", rows_z, dz))
        places.append(list(range(dz * rows_x, (dz + 1) * rows_x)))
    direct[far[0]], other_rows = lax.optimization_barrier((direct[far[0]], other_rows))
    for dz in far:
        arrays.append(direct[dz])
        places.append([dz * rows_x])
        for dx in side:
            arrays.append(swap(direct[dz], "pair", rows_x, dx))
            places.append([dz * rows_x + dx])

    half_at, _ = lax.optimization_barrier((half.reshape(1).astype(jnp.int32), direct[far[-1]]))
    left, left_t = call(
        prepare_kernel,
        (
            jax.ShapeDtypeStruct((batches, points, kept), bf16),
            jax.ShapeDtypeStruct((batches, kept, points), bf16),
        ),
        1,
        scalars=1,
        flops=4 * batches * points * columns * kept,
        moved=3 * batches * points * columns * 2,
    )(half_at, basis_values)

    place = (z * rows_x + x).reshape(1).astype(jnp.int32)
    core_at = half.reshape(1).astype(jnp.int32)

    partial = call(
        functools.partial(density_kernel, places),
        jax.ShapeDtypeStruct((batches, points), f32),
        len(arrays) + 4,
        scalars=2,
        scratch=(pltpu.VMEM((table_rows, wide), bf16), pltpu.VMEM((batches, kept, columns), bf16)),
        flops=2 * batches * points * columns * kept,
        moved=2 * batches * points * columns * 2,
    )(place, core_at, *arrays, own_rows, other_rows, left, basis_values)
    partial_other = swap(partial, "orb", 2, 1)

    out_places = [list(range(dz * rows_x, (dz + 1) * rows_x)) for dz in [0] + near]
    out_places += [[dz * rows_x + dx] for dz in far for dx in [0] + side]
    sums = call(
        functools.partial(scatter_kernel, out_places),
        [jax.ShapeDtypeStruct((held * len(blocks), wide), bf16) for blocks in out_places],
        7,
        scalars=2,
        scratch=(pltpu.VMEM((entries, wide), bf16), pltpu.VMEM((entries, wide), bf16), pltpu.VMEM((batches, points), f32)),
        flops=2 * batches * points * columns * kept,
        moved=2 * batches * points * columns * 2,
    )(place, core_at, partial, partial_other, point_weights, basis_values, left_t, own_rows, other_rows)

    clusters, singles = sums[:len(near) + 1], sums[len(near) + 1:]
    landed = []
    for i, dz in enumerate(far):
        joined = singles[i * rows_x].astype(f32)
        for dx in side:
            joined = joined + swap(singles[i * rows_x + dx], "pair", rows_x, dx).astype(f32)
        landed.append(swap(joined.astype(bf16), "batch", rows_z, dz).astype(f32))
    cluster = clusters[0].astype(f32)
    for dz, array in zip(near, clusters[1:]):
        cluster = cluster + swap(array, "batch", rows_z, dz).astype(f32)
    total = cluster[:held]
    for dx in side:
        total = total + swap(cluster[dx * held:(dx + 1) * held].astype(bf16), "pair", rows_x, dx).astype(f32)
    for term in landed:
        total = total + term
    total_other = swap(total, "orb", 2, 1)
    return call(
        finish_kernel, jax.ShapeDtypeStruct((held, square), f32), 3, scalars=1, moved=held * square * 12
    )(half_at, total, total_other, core_blocks)


def solution(mesh):
    placed = (
        P(("groups", "batch", "pair"), None, None),
        P(("groups", "batch", "pair"), None),
        P(("groups", "batch", "pair"), None, "orb"),
        P(("groups", "batch", "pair"), "orb", None, None),
        P(("groups", "batch", "pair"), None),
        P(("groups", "batch", "pair"), None),
    )
    return jax.shard_map(
        per_device,
        mesh=mesh,
        in_specs=placed,
        out_specs=P(("groups", "batch", "pair"), None),
        check_vma=False,
    )
```

```python
import functools

import jax
import jax.numpy as jnp
from jax import lax
from jax.experimental import pallas as pl
from jax.experimental.pallas import tpu as pltpu
from jax.sharding import PartitionSpec as P

GO = 64
VMEM_LIMIT = 50 * 1024 * 1024
NT = (((1,), (1,)), ((), ()))


def split_dot(left, right, dims=None):
    if dims is None:
        return jnp.dot(left, right, preferred_element_type=jnp.float32)
    return lax.dot_general(left, right, dims, preferred_element_type=jnp.float32)


def prepare_kernel(half_ref, values_ref, left_ref, left_t_ref):
    batches, points, columns = values_ref.shape
    groups = columns // GO
    kept = left_ref.shape[2]
    first = half_ref[0] * (kept // groups)
    at = lax.broadcasted_iota(jnp.int32, (kept, columns), 0)
    lane = lax.broadcasted_iota(jnp.int32, (kept, columns), 1)
    wanted = (at % groups) * GO + first + at // groups
    select = jnp.where(lane == wanted, 1.0, 0.0).astype(jnp.bfloat16)
    for t in range(batches):
        left_ref[t] = split_dot(values_ref[t], select, NT).astype(jnp.bfloat16)
        left_t_ref[t] = split_dot(select, values_ref[t], NT).astype(jnp.bfloat16)


def index_kernel(held, fetch_ref, slots_ref, rows_ref):
    owners, capacity = fetch_ref.shape
    slots = slots_ref[...]
    entries = slots.shape[1]
    owner = slots // capacity
    owner_hot = jnp.where(lax.broadcasted_iota(jnp.int32, (owners, entries), 0) == owner, 1.0, 0.0)
    stored = fetch_ref[...].astype(jnp.float32).T.astype(jnp.bfloat16)
    listed = split_dot(stored, owner_hot.astype(jnp.bfloat16)).astype(jnp.int32)
    at = lax.broadcasted_iota(jnp.int32, (capacity, entries), 0)
    chosen = jnp.where(at == slots - owner * capacity, listed, 0)
    rows_ref[...] = jnp.sum(chosen, axis=0, keepdims=True) + owner * held


def row_table(place_ref, core_ref, own_ref, other_ref, held, owners):
    low = core_ref[0] == 0
    rows = jnp.concatenate(
        [jnp.where(low, own_ref[...], other_ref[...]), jnp.where(low, other_ref[...], own_ref[...])], axis=1
    )
    rows = lax.bitwise_xor(rows, place_ref[0] * held)
    row = lax.broadcasted_iota(jnp.int32, (owners * held, rows.shape[1]), 0)
    return jnp.where(row == rows, 1.0, 0.0)


def density_kernel(places, place_ref, core_ref, *refs):
    piece_refs = refs[:len(places)]
    own_ref, other_ref, left_ref, values_ref, out_ref, table, dense = refs[len(places):]
    batches, points, columns = values_ref.shape
    groups = columns // GO
    owners = sum(len(blocks) for blocks in places)
    held = table.shape[0] // owners
    for ref, blocks in zip(piece_refs, places):
        table[blocks[0] * held:(blocks[-1] + 1) * held, :] = ref[...]
    pick = row_table(place_ref, core_ref, own_ref, other_ref, held, owners).T.astype(jnp.bfloat16)
    low = lax.broadcasted_iota(jnp.int32, (1, 1, 1, groups, 128), 4) < GO
    for chunk in range(table.shape[1] // 256):
        wide = split_dot(pick, table[:, chunk * 256:(chunk + 1) * 256])
        for j in (2 * chunk, 2 * chunk + 1):
            got = wide[:, (j % 2) * 128:(j % 2 + 1) * 128].reshape(2, batches, groups // 4, 2, groups, 128)
            even, odd = got[:, :, :, 0], got[:, :, :, 1]
            first = jnp.where(low, even, pltpu.roll(odd, GO, 4))
            second = jnp.where(low, pltpu.roll(even, GO, 4), odd)
            for t in range(batches):
                for q in range(groups // 2):
                    at = (q // (groups // 4), t, q % (groups // 4))
                    both = jnp.concatenate([first[at], second[at]], axis=0)
                    dense[t, j * 2 * groups:(j + 1) * 2 * groups, q * 128:(q + 1) * 128] = both.astype(jnp.bfloat16)
    for t in range(batches):
        product = split_dot(left_ref[t], dense[t]) * values_ref[t].astype(jnp.float32)
        folded = product[:, :128]
        for q in range(1, columns // 128):
            folded = folded + product[:, q * 128:(q + 1) * 128]
        out_ref[t:t + 1, :] = jnp.sum(folded.T, axis=0, keepdims=True)


def scatter_kernel(places, place_ref, core_ref, *refs):
    mine_ref, far_ref, weight_ref, values_ref, left_t_ref, own_ref, other_ref = refs[:7]
    out_refs = refs[7:-2]
    high, rest = refs[-2:]
    target = {k: (ref, i) for ref, blocks in zip(out_refs, places) for i, k in enumerate(blocks)}
    pieces = len(target)
    held = out_refs[0].shape[0] // len(places[0])
    put = row_table(place_ref, core_ref, own_ref, other_ref, held, pieces).astype(jnp.bfloat16)
    batches, points, columns = values_ref.shape
    groups = columns // GO
    kept = left_t_ref.shape[1]
    steps = kept // (2 * groups)
    potential = weight_ref[...] * jnp.tanh(mine_ref[...] + far_ref[...])
    low = lax.broadcasted_iota(jnp.int32, (1, groups, 128), 2) < GO
    for t in range(batches):
        factor = jnp.broadcast_to(potential[t:t + 1, :], (128, points)).T
        factor = jnp.concatenate([factor] * (columns // 128), axis=1)
        weighted = (values_ref[t].astype(jnp.float32) * factor).astype(jnp.bfloat16)
        part = split_dot(left_t_ref[t], weighted)
        for q in range(groups // 2):
            cut = part[:, q * 128:(q + 1) * 128].reshape(steps, 2, groups, 128)
            first, second = cut[:, 0], cut[:, 1]
            even = jnp.where(low, first, pltpu.roll(second, GO, 2))
            odd = jnp.where(low, pltpu.roll(first, GO, 2), second)
            side, pair = q // (groups // 4), q % (groups // 4)
            at = ((side * batches + t) * (groups // 2) + 2 * pair) * groups
            for j in range(steps):
                both = jnp.concatenate([even[j], odd[j]], axis=0)
                top = both.astype(jnp.bfloat16)
                high[at:at + 2 * groups, j * 128:(j + 1) * 128] = top
                rest[at:at + 2 * groups, j * 128:(j + 1) * 128] = (both - top.astype(jnp.float32)).astype(jnp.bfloat16)
    step = max(1, min(pieces, 128 // held))
    for k in range(0, pieces, step):
        some = put[k * held:(k + step) * held, :]
        total = split_dot(some, high[...]) + split_dot(some, rest[...])
        for i in range(step):
            ref, at = target[k + i]
            ref[at * held:(at + 1) * held, :] = total[i * held:(i + 1) * held, :].astype(jnp.bfloat16)


def finish_kernel(half_ref, mine_ref, other_ref, core_ref, out_ref):
    wide = mine_ref.shape[1]
    own = pl.multiple_of(half_ref[0] * wide, wide)
    far = pl.multiple_of((1 - half_ref[0]) * wide, wide)
    out_ref[:, pl.ds(own, wide)] = core_ref[:, pl.ds(own, wide)].astype(jnp.float32) + mine_ref[...]
    out_ref[:, pl.ds(far, wide)] = core_ref[:, pl.ds(far, wide)].astype(jnp.float32) + other_ref[...]


def call(kernel, outs, count, scratch=(), scalars=0, flops=0, moved=0):
    specs = [pl.BlockSpec(memory_space=pltpu.VMEM)] * count
    specs = [pl.BlockSpec(memory_space=pltpu.SMEM)] * scalars + specs
    out_specs = jax.tree.map(lambda _: pl.BlockSpec(memory_space=pltpu.VMEM), outs)
    return pl.pallas_call(
        kernel,
        out_shape=outs,
        in_specs=specs,
        out_specs=out_specs,
        scratch_shapes=list(scratch),
        compiler_params=pltpu.CompilerParams(vmem_limit_bytes=VMEM_LIMIT),
        cost_estimate=pl.CostEstimate(flops=flops, bytes_accessed=moved, transcendentals=0),
    )


def swap(array, axis, count, step):
    return lax.ppermute(array, axis, [(i, i ^ step) for i in range(count)])


def per_device(basis_values, point_weights, slot_ids, fetch_rows, density_blocks, core_blocks):
    rows_z, rows_x = lax.axis_size("batch"), lax.axis_size("pair")
    z, x, half = lax.axis_index("batch"), lax.axis_index("pair"), lax.axis_index("orb")
    owners = rows_z * rows_x
    batches, points, columns = basis_values.shape
    groups, own_groups = slot_ids.shape[1], slot_ids.shape[2]
    held, square = density_blocks.shape
    capacity = fetch_rows.shape[3]
    wide = square // 2
    table_rows = owners * held
    entries = batches * groups * groups
    kept = columns // 2
    bf16, f32 = jnp.bfloat16, jnp.float32

    own_rows = call(
        functools.partial(index_kernel, held),
        jax.ShapeDtypeStruct((1, batches * own_groups * groups), jnp.int32),
        2,
    )(fetch_rows.reshape(owners, capacity), slot_ids.transpose(0, 2, 1).reshape(1, -1))
    other_rows = swap(own_rows, "orb", 2, 1)

    far = list(range(rows_z // 2, rows_z))
    near = list(range(1, rows_z // 2))
    side = list(range(1, rows_x))

    mine = lax.dynamic_slice_in_dim(density_blocks, half * wide, wide, 1)
    direct = {dz: swap(mine, "batch", rows_z, dz) for dz in far}
    beside = [swap(mine, "pair", rows_x, dx) for dx in side]
    *beside, own_rows = lax.optimization_barrier((*beside, own_rows))
    cluster = jnp.concatenate([mine, *beside], axis=0)
    arrays, places = [cluster], [list(range(rows_x))]
    for dz in near:
        arrays.append(swap(cluster, "batch", rows_z, dz))
        places.append(list(range(dz * rows_x, (dz + 1) * rows_x)))
    direct[far[0]], other_rows = lax.optimization_barrier((direct[far[0]], other_rows))
    for dz in far:
        arrays.append(direct[dz])
        places.append([dz * rows_x])
        for dx in side:
            arrays.append(swap(direct[dz], "pair", rows_x, dx))
            places.append([dz * rows_x + dx])

    half_at, _ = lax.optimization_barrier((half.reshape(1).astype(jnp.int32), direct[far[-1]]))
    left, left_t = call(
        prepare_kernel,
        (
            jax.ShapeDtypeStruct((batches, points, kept), bf16),
            jax.ShapeDtypeStruct((batches, kept, points), bf16),
        ),
        1,
        scalars=1,
        flops=4 * batches * points * columns * kept,
        moved=3 * batches * points * columns * 2,
    )(half_at, basis_values)

    place = (z * rows_x + x).reshape(1).astype(jnp.int32)
    core_at = half.reshape(1).astype(jnp.int32)

    partial = call(
        functools.partial(density_kernel, places),
        jax.ShapeDtypeStruct((batches, points), f32),
        len(arrays) + 4,
        scalars=2,
        scratch=(pltpu.VMEM((table_rows, wide), bf16), pltpu.VMEM((batches, kept, columns), bf16)),
        flops=2 * batches * points * columns * kept,
        moved=2 * batches * points * columns * 2,
    )(place, core_at, *arrays, own_rows, other_rows, left, basis_values)
    partial_other = swap(partial, "orb", 2, 1)

    out_places = [list(range(dz * rows_x, (dz + 1) * rows_x)) for dz in [0] + near]
    out_places += [[dz * rows_x + dx for dz in far] for dx in [0] + side]
    sums = call(
        functools.partial(scatter_kernel, out_places),
        [jax.ShapeDtypeStruct((held * len(blocks), wide), bf16) for blocks in out_places],
        7,
        scalars=2,
        scratch=(pltpu.VMEM((entries, wide), bf16), pltpu.VMEM((entries, wide), bf16)),
        flops=2 * batches * points * columns * kept,
        moved=2 * batches * points * columns * 2,
    )(place, core_at, partial, partial_other, point_weights, basis_values, left_t, own_rows, other_rows)

    clusters, middles = sums[:len(near) + 1], sums[len(near) + 1:]
    joined = middles[0].astype(f32)
    for dx in side:
        joined = joined + swap(middles[dx], "pair", rows_x, dx).astype(f32)
    joined = joined.astype(bf16)
    joined, cluster = lax.optimization_barrier((joined, clusters[0]))
    landed = [swap(joined[i * held:(i + 1) * held], "batch", rows_z, dz).astype(f32) for i, dz in enumerate(far)]
    cluster = cluster.astype(f32)
    for dz, array in zip(near, clusters[1:]):
        cluster = cluster + swap(array, "batch", rows_z, dz).astype(f32)
    total = cluster[:held]
    for dx in side:
        total = total + swap(cluster[dx * held:(dx + 1) * held].astype(bf16), "pair", rows_x, dx).astype(f32)
    for term in landed:
        total = total + term
    total_other = swap(total, "orb", 2, 1)
    return call(
        finish_kernel, jax.ShapeDtypeStruct((held, square), f32), 3, scalars=1, moved=held * square * 12
    )(half_at, total, total_other, core_blocks)


def solution(mesh):
    placed = (
        P(("groups", "batch", "pair"), None, None),
        P(("groups", "batch", "pair"), None),
        P(("groups", "batch", "pair"), None, "orb"),
        P(("groups", "batch", "pair"), "orb", None, None),
        P(("groups", "batch", "pair"), None),
        P(("groups", "batch", "pair"), None),
    )
    return jax.shard_map(
        per_device,
        mesh=mesh,
        in_specs=placed,
        out_specs=P(("groups", "batch", "pair"), None),
        check_vma=False,
    )
```

```python
import functools

import jax
import jax.numpy as jnp
from jax import lax
from jax.experimental import pallas as pl
from jax.experimental.pallas import tpu as pltpu
from jax.sharding import PartitionSpec as P

GO = 64
VMEM_LIMIT = 50 * 1024 * 1024
NT = (((1,), (1,)), ((), ()))


def split_dot(left, right, dims=None):
    if dims is None:
        return jnp.dot(left, right, preferred_element_type=jnp.float32)
    return lax.dot_general(left, right, dims, preferred_element_type=jnp.float32)


def prepare_kernel(half_ref, values_ref, left_ref, left_t_ref):
    batches, points, columns = values_ref.shape
    groups = columns // GO
    kept = left_ref.shape[2]
    first = half_ref[0] * (kept // groups)
    at = lax.broadcasted_iota(jnp.int32, (kept, columns), 0)
    lane = lax.broadcasted_iota(jnp.int32, (kept, columns), 1)
    wanted = (at % groups) * GO + first + at // groups
    select = jnp.where(lane == wanted, 1.0, 0.0).astype(jnp.bfloat16)
    for t in range(batches):
        left_ref[t] = split_dot(values_ref[t], select, NT).astype(jnp.bfloat16)
        left_t_ref[t] = split_dot(select, values_ref[t], NT).astype(jnp.bfloat16)


def index_kernel(held, fetch_ref, slots_ref, rows_ref):
    owners, capacity = fetch_ref.shape
    slots = slots_ref[...]
    entries = slots.shape[1]
    owner = slots // capacity
    owner_hot = jnp.where(lax.broadcasted_iota(jnp.int32, (owners, entries), 0) == owner, 1.0, 0.0)
    stored = fetch_ref[...].astype(jnp.float32).T.astype(jnp.bfloat16)
    listed = split_dot(stored, owner_hot.astype(jnp.bfloat16)).astype(jnp.int32)
    at = lax.broadcasted_iota(jnp.int32, (capacity, entries), 0)
    chosen = jnp.where(at == slots - owner * capacity, listed, 0)
    rows_ref[...] = jnp.sum(chosen, axis=0, keepdims=True) + owner * held


def row_table(place_ref, core_ref, own_ref, other_ref, held, owners):
    low = core_ref[0] == 0
    rows = jnp.concatenate(
        [jnp.where(low, own_ref[...], other_ref[...]), jnp.where(low, other_ref[...], own_ref[...])], axis=1
    )
    rows = lax.bitwise_xor(rows, place_ref[0] * held)
    row = lax.broadcasted_iota(jnp.int32, (owners * held, rows.shape[1]), 0)
    return jnp.where(row == rows, 1.0, 0.0)


def density_kernel(places, place_ref, core_ref, *refs):
    piece_refs = refs[:len(places)]
    own_ref, other_ref, left_ref, values_ref, out_ref, table, dense = refs[len(places):]
    batches, points, columns = values_ref.shape
    groups = columns // GO
    owners = sum(len(blocks) for blocks in places)
    held = table.shape[0] // owners
    for ref, blocks in zip(piece_refs, places):
        table[blocks[0] * held:(blocks[-1] + 1) * held, :] = ref[...]
    pick = row_table(place_ref, core_ref, own_ref, other_ref, held, owners).T.astype(jnp.bfloat16)
    low = lax.broadcasted_iota(jnp.int32, (1, 1, 1, groups, 128), 4) < GO
    for chunk in range(table.shape[1] // 256):
        wide = split_dot(pick, table[:, chunk * 256:(chunk + 1) * 256])
        for j in (2 * chunk, 2 * chunk + 1):
            got = wide[:, (j % 2) * 128:(j % 2 + 1) * 128].reshape(2, batches, groups // 4, 2, groups, 128)
            even, odd = got[:, :, :, 0], got[:, :, :, 1]
            first = jnp.where(low, even, pltpu.roll(odd, GO, 4))
            second = jnp.where(low, pltpu.roll(even, GO, 4), odd)
            for t in range(batches):
                for q in range(groups // 2):
                    at = (q // (groups // 4), t, q % (groups // 4))
                    both = jnp.concatenate([first[at], second[at]], axis=0)
                    dense[t, j * 2 * groups:(j + 1) * 2 * groups, q * 128:(q + 1) * 128] = both.astype(jnp.bfloat16)
    for t in range(batches):
        product = split_dot(left_ref[t], dense[t]) * values_ref[t].astype(jnp.float32)
        folded = product[:, :128]
        for q in range(1, columns // 128):
            folded = folded + product[:, q * 128:(q + 1) * 128]
        out_ref[t:t + 1, :] = jnp.sum(folded.T, axis=0, keepdims=True)


def scatter_kernel(places, owners, place_ref, core_ref, *refs):
    mine_ref, far_ref, weight_ref, values_ref, left_t_ref, own_ref, other_ref = refs[:7]
    out_refs = refs[7:-2]
    high, rest = refs[-2:]
    target = {k: (ref, i) for ref, blocks in zip(out_refs, places) for i, k in enumerate(blocks)}
    held = out_refs[0].shape[0] // len(places[0])
    pieces = owners
    put = row_table(place_ref, core_ref, own_ref, other_ref, held, pieces).astype(jnp.bfloat16)
    batches, points, columns = values_ref.shape
    groups = columns // GO
    kept = left_t_ref.shape[1]
    steps = kept // (2 * groups)
    potential = weight_ref[...] * jnp.tanh(mine_ref[...] + far_ref[...])
    low = lax.broadcasted_iota(jnp.int32, (1, groups, 128), 2) < GO
    for t in range(batches):
        factor = jnp.broadcast_to(potential[t:t + 1, :], (128, points)).T
        factor = jnp.concatenate([factor] * (columns // 128), axis=1)
        weighted = (values_ref[t].astype(jnp.float32) * factor).astype(jnp.bfloat16)
        part = split_dot(left_t_ref[t], weighted)
        for q in range(groups // 2):
            cut = part[:, q * 128:(q + 1) * 128].reshape(steps, 2, groups, 128)
            first, second = cut[:, 0], cut[:, 1]
            even = jnp.where(low, first, pltpu.roll(second, GO, 2))
            odd = jnp.where(low, pltpu.roll(first, GO, 2), second)
            side, pair = q // (groups // 4), q % (groups // 4)
            at = ((side * batches + t) * (groups // 2) + 2 * pair) * groups
            for j in range(steps):
                both = jnp.concatenate([even[j], odd[j]], axis=0)
                top = both.astype(jnp.bfloat16)
                high[at:at + 2 * groups, j * 128:(j + 1) * 128] = top
                rest[at:at + 2 * groups, j * 128:(j + 1) * 128] = (both - top.astype(jnp.float32)).astype(jnp.bfloat16)
    step = max(1, min(pieces, 128 // held))
    for k in range(0, pieces, step):
        some = put[k * held:(k + step) * held, :]
        total = split_dot(some, high[...]) + split_dot(some, rest[...])
        for i in range(step):
            if k + i in target:
                ref, at = target[k + i]
                ref[at * held:(at + 1) * held, :] = total[i * held:(i + 1) * held, :].astype(jnp.bfloat16)


def late_kernel(first, place_ref, core_ref, high_ref, rest_ref, own_ref, other_ref, *out_refs):
    held = out_refs[0].shape[0]
    owners = first + len(out_refs)
    put = row_table(place_ref, core_ref, own_ref, other_ref, held, owners)[first * held:].astype(jnp.bfloat16)
    total = split_dot(put, high_ref[...]) + split_dot(put, rest_ref[...])
    for i, ref in enumerate(out_refs):
        ref[...] = total[i * held:(i + 1) * held, :].astype(jnp.bfloat16)


def finish_kernel(half_ref, mine_ref, other_ref, core_ref, out_ref):
    wide = mine_ref.shape[1]
    own = pl.multiple_of(half_ref[0] * wide, wide)
    far = pl.multiple_of((1 - half_ref[0]) * wide, wide)
    out_ref[:, pl.ds(own, wide)] = core_ref[:, pl.ds(own, wide)].astype(jnp.float32) + mine_ref[...]
    out_ref[:, pl.ds(far, wide)] = core_ref[:, pl.ds(far, wide)].astype(jnp.float32) + other_ref[...]


def call(kernel, outs, count, scratch=(), scalars=0, flops=0, moved=0):
    specs = [pl.BlockSpec(memory_space=pltpu.VMEM)] * count
    specs = [pl.BlockSpec(memory_space=pltpu.SMEM)] * scalars + specs
    out_specs = jax.tree.map(lambda _: pl.BlockSpec(memory_space=pltpu.VMEM), outs)
    return pl.pallas_call(
        kernel,
        out_shape=outs,
        in_specs=specs,
        out_specs=out_specs,
        scratch_shapes=list(scratch),
        compiler_params=pltpu.CompilerParams(vmem_limit_bytes=VMEM_LIMIT),
        cost_estimate=pl.CostEstimate(flops=flops, bytes_accessed=moved, transcendentals=0),
    )


def swap(array, axis, count, step):
    return lax.ppermute(array, axis, [(i, i ^ step) for i in range(count)])


def per_device(basis_values, point_weights, slot_ids, fetch_rows, density_blocks, core_blocks):
    rows_z, rows_x = lax.axis_size("batch"), lax.axis_size("pair")
    z, x, half = lax.axis_index("batch"), lax.axis_index("pair"), lax.axis_index("orb")
    owners = rows_z * rows_x
    batches, points, columns = basis_values.shape
    groups, own_groups = slot_ids.shape[1], slot_ids.shape[2]
    held, square = density_blocks.shape
    capacity = fetch_rows.shape[3]
    wide = square // 2
    table_rows = owners * held
    entries = batches * groups * groups
    kept = columns // 2
    bf16, f32 = jnp.bfloat16, jnp.float32

    own_rows = call(
        functools.partial(index_kernel, held),
        jax.ShapeDtypeStruct((1, batches * own_groups * groups), jnp.int32),
        2,
    )(fetch_rows.reshape(owners, capacity), slot_ids.transpose(0, 2, 1).reshape(1, -1))
    other_rows = swap(own_rows, "orb", 2, 1)

    far = list(range(rows_z // 2, rows_z))
    near = list(range(1, rows_z // 2))
    side = list(range(1, rows_x))

    mine = lax.dynamic_slice_in_dim(density_blocks, half * wide, wide, 1)
    direct = {dz: swap(mine, "batch", rows_z, dz) for dz in far}
    beside = [swap(mine, "pair", rows_x, dx) for dx in side]
    *beside, own_rows = lax.optimization_barrier((*beside, own_rows))
    cluster = jnp.concatenate([mine, *beside], axis=0)
    arrays, places = [cluster], [list(range(rows_x))]
    for dz in near:
        arrays.append(swap(cluster, "batch", rows_z, dz))
        places.append(list(range(dz * rows_x, (dz + 1) * rows_x)))
    direct[far[0]], other_rows = lax.optimization_barrier((direct[far[0]], other_rows))
    for dz in far:
        arrays.append(direct[dz])
        places.append([dz * rows_x])
        for dx in side:
            arrays.append(swap(direct[dz], "pair", rows_x, dx))
            places.append([dz * rows_x + dx])

    half_at, _ = lax.optimization_barrier((half.reshape(1).astype(jnp.int32), direct[far[-1]]))
    left, left_t = call(
        prepare_kernel,
        (
            jax.ShapeDtypeStruct((batches, points, kept), bf16),
            jax.ShapeDtypeStruct((batches, kept, points), bf16),
        ),
        1,
        scalars=1,
        flops=4 * batches * points * columns * kept,
        moved=3 * batches * points * columns * 2,
    )(half_at, basis_values)

    place = (z * rows_x + x).reshape(1).astype(jnp.int32)
    core_at = half.reshape(1).astype(jnp.int32)

    partial = call(
        functools.partial(density_kernel, places),
        jax.ShapeDtypeStruct((batches, points), f32),
        len(arrays) + 4,
        scalars=2,
        scratch=(pltpu.VMEM((table_rows, wide), bf16), pltpu.VMEM((batches, kept, columns), bf16)),
        flops=2 * batches * points * columns * kept,
        moved=2 * batches * points * columns * 2,
    )(place, core_at, *arrays, own_rows, other_rows, left, basis_values)
    partial_other = swap(partial, "orb", 2, 1)

    out_places = [list(range(dz * rows_x, (dz + 1) * rows_x)) for dz in [0] + near]
    out_places += [[dz * rows_x + dx] for dz in far[:-1] for dx in [0] + side]
    outs = [jax.ShapeDtypeStruct((held * len(blocks), wide), bf16) for blocks in out_places]
    *sums, high, rest = call(
        functools.partial(scatter_kernel, out_places, owners),
        outs + [jax.ShapeDtypeStruct((entries, wide), bf16)] * 2,
        7,
        scalars=2,
        flops=2 * batches * points * columns * kept,
        moved=2 * batches * points * columns * 2,
    )(place, core_at, partial, partial_other, point_weights, basis_values, left_t, own_rows, other_rows)
    sums += call(
        functools.partial(late_kernel, owners - rows_x),
        [jax.ShapeDtypeStruct((held, wide), bf16)] * rows_x,
        4,
        scalars=2,
        flops=4 * rows_x * held * entries * wide,
        moved=2 * entries * wide * 2,
    )(place, core_at, high, rest, own_rows, other_rows)

    clusters, singles = sums[:len(near) + 1], sums[len(near) + 1:]
    landed = []
    for i, dz in enumerate(far):
        joined = singles[i * rows_x].astype(f32)
        for dx in side:
            joined = joined + swap(singles[i * rows_x + dx], "pair", rows_x, dx).astype(f32)
        landed.append(swap(joined.astype(bf16), "batch", rows_z, dz).astype(f32))
    cluster = clusters[0].astype(f32)
    for dz, array in zip(near, clusters[1:]):
        cluster = cluster + swap(array, "batch", rows_z, dz).astype(f32)
    total = cluster[:held]
    for dx in side:
        total = total + swap(cluster[dx * held:(dx + 1) * held].astype(bf16), "pair", rows_x, dx).astype(f32)
    for term in landed:
        total = total + term
    total_other = swap(total, "orb", 2, 1)
    return call(
        finish_kernel, jax.ShapeDtypeStruct((held, square), f32), 3, scalars=1, moved=held * square * 12
    )(half_at, total, total_other, core_blocks)


def solution(mesh):
    placed = (
        P(("groups", "batch", "pair"), None, None),
        P(("groups", "batch", "pair"), None),
        P(("groups", "batch", "pair"), None, "orb"),
        P(("groups", "batch", "pair"), "orb", None, None),
        P(("groups", "batch", "pair"), None),
        P(("groups", "batch", "pair"), None),
    )
    return jax.shard_map(
        per_device,
        mesh=mesh,
        in_specs=placed,
        out_specs=P(("groups", "batch", "pair"), None),
        check_vma=False,
    )
```

```python
import functools

import jax
import jax.numpy as jnp
from jax import lax
from jax.experimental import pallas as pl
from jax.experimental.pallas import tpu as pltpu
from jax.sharding import PartitionSpec as P

GO = 64
VMEM_LIMIT = 50 * 1024 * 1024
NT = (((1,), (1,)), ((), ()))


def split_dot(left, right, dims=None):
    if dims is None:
        return jnp.dot(left, right, preferred_element_type=jnp.float32)
    return lax.dot_general(left, right, dims, preferred_element_type=jnp.float32)


def prepare_kernel(half_ref, values_ref, left_ref, left_t_ref):
    batches, points, columns = values_ref.shape
    groups = columns // GO
    kept = left_ref.shape[2]
    first = half_ref[0] * (kept // groups)
    at = lax.broadcasted_iota(jnp.int32, (kept, columns), 0)
    lane = lax.broadcasted_iota(jnp.int32, (kept, columns), 1)
    wanted = (at % groups) * GO + first + at // groups
    select = jnp.where(lane == wanted, 1.0, 0.0).astype(jnp.bfloat16)
    for t in range(batches):
        left_ref[t] = split_dot(values_ref[t], select, NT).astype(jnp.bfloat16)
        left_t_ref[t] = split_dot(select, values_ref[t], NT).astype(jnp.bfloat16)


def index_kernel(held, fetch_ref, slots_ref, rows_ref):
    owners, capacity = fetch_ref.shape
    slots = slots_ref[...]
    entries = slots.shape[1]
    owner = slots // capacity
    owner_hot = jnp.where(lax.broadcasted_iota(jnp.int32, (owners, entries), 0) == owner, 1.0, 0.0)
    stored = fetch_ref[...].astype(jnp.float32).T.astype(jnp.bfloat16)
    listed = split_dot(stored, owner_hot.astype(jnp.bfloat16)).astype(jnp.int32)
    at = lax.broadcasted_iota(jnp.int32, (capacity, entries), 0)
    chosen = jnp.where(at == slots - owner * capacity, listed, 0)
    rows_ref[...] = jnp.sum(chosen, axis=0, keepdims=True) + owner * held


def row_table(place_ref, core_ref, own_ref, other_ref, held, owners):
    low = core_ref[0] == 0
    rows = jnp.concatenate(
        [jnp.where(low, own_ref[...], other_ref[...]), jnp.where(low, other_ref[...], own_ref[...])], axis=1
    )
    rows = lax.bitwise_xor(rows, place_ref[0] * held)
    row = lax.broadcasted_iota(jnp.int32, (owners * held, rows.shape[1]), 0)
    return jnp.where(row == rows, 1.0, 0.0)


def density_kernel(places, place_ref, core_ref, *refs):
    piece_refs = refs[:len(places)]
    own_ref, other_ref, left_ref, values_ref, out_ref, table, dense = refs[len(places):]
    batches, points, columns = values_ref.shape
    groups = columns // GO
    owners = sum(len(blocks) for blocks in places)
    held = table.shape[0] // owners
    for ref, blocks in zip(piece_refs, places):
        table[blocks[0] * held:(blocks[-1] + 1) * held, :] = ref[...]
    pick = row_table(place_ref, core_ref, own_ref, other_ref, held, owners).T.astype(jnp.bfloat16)
    low = lax.broadcasted_iota(jnp.int32, (1, 1, 1, groups, 128), 4) < GO
    for chunk in range(table.shape[1] // 256):
        wide = split_dot(pick, table[:, chunk * 256:(chunk + 1) * 256])
        for j in (2 * chunk, 2 * chunk + 1):
            got = wide[:, (j % 2) * 128:(j % 2 + 1) * 128].reshape(2, batches, groups // 4, 2, groups, 128)
            even, odd = got[:, :, :, 0], got[:, :, :, 1]
            first = jnp.where(low, even, pltpu.roll(odd, GO, 4))
            second = jnp.where(low, pltpu.roll(even, GO, 4), odd)
            for t in range(batches):
                for q in range(groups // 2):
                    at = (q // (groups // 4), t, q % (groups // 4))
                    both = jnp.concatenate([first[at], second[at]], axis=0)
                    dense[t, j * 2 * groups:(j + 1) * 2 * groups, q * 128:(q + 1) * 128] = both.astype(jnp.bfloat16)
    for t in range(batches):
        product = split_dot(left_ref[t], dense[t]) * values_ref[t].astype(jnp.float32)
        folded = product[:, :128]
        for q in range(1, columns // 128):
            folded = folded + product[:, q * 128:(q + 1) * 128]
        out_ref[t:t + 1, :] = jnp.sum(folded.T, axis=0, keepdims=True)


def scatter_kernel(places, place_ref, core_ref, *refs):
    mine_ref, far_ref, weight_ref, values_ref, left_t_ref, own_ref, other_ref = refs[:7]
    out_refs = refs[7:-2]
    high, rest = refs[-2:]
    target = {k: (ref, i) for ref, blocks in zip(out_refs, places) for i, k in enumerate(blocks)}
    pieces = len(target)
    held = out_refs[0].shape[0] // len(places[0])
    put = row_table(place_ref, core_ref, own_ref, other_ref, held, pieces).astype(jnp.bfloat16)
    batches, points, columns = values_ref.shape
    groups = columns // GO
    kept = left_t_ref.shape[1]
    steps = kept // (2 * groups)
    potential = weight_ref[...] * jnp.tanh(mine_ref[...] + far_ref[...])
    low = lax.broadcasted_iota(jnp.int32, (1, groups, 128), 2) < GO
    for t in range(batches):
        factor = jnp.broadcast_to(potential[t:t + 1, :], (128, points)).T
        factor = jnp.concatenate([factor] * (columns // 128), axis=1)
        weighted = (values_ref[t].astype(jnp.float32) * factor).astype(jnp.bfloat16)
        part = split_dot(left_t_ref[t], weighted)
        for q in range(groups // 2):
            cut = part[:, q * 128:(q + 1) * 128].reshape(steps, 2, groups, 128)
            first, second = cut[:, 0], cut[:, 1]
            even = jnp.where(low, first, pltpu.roll(second, GO, 2))
            odd = jnp.where(low, pltpu.roll(first, GO, 2), second)
            side, pair = q // (groups // 4), q % (groups // 4)
            at = ((side * batches + t) * (groups // 2) + 2 * pair) * groups
            for j in range(steps):
                both = jnp.concatenate([even[j], odd[j]], axis=0)
                top = both.astype(jnp.bfloat16)
                high[at:at + 2 * groups, j * 128:(j + 1) * 128] = top
                rest[at:at + 2 * groups, j * 128:(j + 1) * 128] = (both - top.astype(jnp.float32)).astype(jnp.bfloat16)
    step = max(1, min(pieces, 128 // held))
    for k in range(0, pieces, step):
        some = put[k * held:(k + step) * held, :]
        total = split_dot(some, high[...]) + split_dot(some, rest[...])
        for i in range(step):
            ref, at = target[k + i]
            ref[at * held:(at + 1) * held, :] = total[i * held:(i + 1) * held, :].astype(jnp.bfloat16)


def finish_kernel(half_ref, mine_ref, other_ref, core_ref, out_ref):
    wide = mine_ref.shape[1]
    own = pl.multiple_of(half_ref[0] * wide, wide)
    far = pl.multiple_of((1 - half_ref[0]) * wide, wide)
    out_ref[:, pl.ds(own, wide)] = core_ref[:, pl.ds(own, wide)].astype(jnp.float32) + mine_ref[...]
    out_ref[:, pl.ds(far, wide)] = core_ref[:, pl.ds(far, wide)].astype(jnp.float32) + other_ref[...]


def call(kernel, outs, count, scratch=(), scalars=0, flops=0, moved=0):
    specs = [pl.BlockSpec(memory_space=pltpu.VMEM)] * count
    specs = [pl.BlockSpec(memory_space=pltpu.SMEM)] * scalars + specs
    out_specs = jax.tree.map(lambda _: pl.BlockSpec(memory_space=pltpu.VMEM), outs)
    return pl.pallas_call(
        kernel,
        out_shape=outs,
        in_specs=specs,
        out_specs=out_specs,
        scratch_shapes=list(scratch),
        compiler_params=pltpu.CompilerParams(vmem_limit_bytes=VMEM_LIMIT),
        cost_estimate=pl.CostEstimate(flops=flops, bytes_accessed=moved, transcendentals=0),
    )


def swap(array, axis, count, step):
    return lax.ppermute(array, axis, [(i, i ^ step) for i in range(count)])


def per_device(basis_values, point_weights, slot_ids, fetch_rows, density_blocks, core_blocks):
    rows_z, rows_x = lax.axis_size("batch"), lax.axis_size("pair")
    z, x, half = lax.axis_index("batch"), lax.axis_index("pair"), lax.axis_index("orb")
    owners = rows_z * rows_x
    batches, points, columns = basis_values.shape
    groups, own_groups = slot_ids.shape[1], slot_ids.shape[2]
    held, square = density_blocks.shape
    capacity = fetch_rows.shape[3]
    wide = square // 2
    table_rows = owners * held
    entries = batches * groups * groups
    kept = columns // 2
    bf16, f32 = jnp.bfloat16, jnp.float32

    own_rows = call(
        functools.partial(index_kernel, held),
        jax.ShapeDtypeStruct((1, batches * own_groups * groups), jnp.int32),
        2,
    )(fetch_rows.reshape(owners, capacity), slot_ids.transpose(0, 2, 1).reshape(1, -1))
    other_rows = swap(own_rows, "orb", 2, 1)

    far = list(range(rows_z // 2, rows_z))
    near = list(range(1, rows_z // 2))
    side = list(range(1, rows_x))

    mine = lax.dynamic_slice_in_dim(density_blocks, half * wide, wide, 1)
    direct = {dz: swap(mine, "batch", rows_z, dz) for dz in far}
    beside = [swap(mine, "pair", rows_x, dx) for dx in side]
    *beside, own_rows = lax.optimization_barrier((*beside, own_rows))
    cluster = jnp.concatenate([mine, *beside], axis=0)
    arrays, places = [cluster], [list(range(rows_x))]
    for dz in near:
        arrays.append(swap(cluster, "batch", rows_z, dz))
        places.append(list(range(dz * rows_x, (dz + 1) * rows_x)))
    direct[far[0]], other_rows = lax.optimization_barrier((direct[far[0]], other_rows))
    for dz in far:
        arrays.append(direct[dz])
        places.append([dz * rows_x])
        for dx in side:
            arrays.append(swap(direct[dz], "pair", rows_x, dx))
            places.append([dz * rows_x + dx])

    half_at, _ = lax.optimization_barrier((half.reshape(1).astype(jnp.int32), direct[far[-1]]))
    left, left_t = call(
        prepare_kernel,
        (
            jax.ShapeDtypeStruct((batches, points, kept), bf16),
            jax.ShapeDtypeStruct((batches, kept, points), bf16),
        ),
        1,
        scalars=1,
        flops=4 * batches * points * columns * kept,
        moved=3 * batches * points * columns * 2,
    )(half_at, basis_values)

    place = (z * rows_x + x).reshape(1).astype(jnp.int32)
    core_at = half.reshape(1).astype(jnp.int32)

    partial = call(
        functools.partial(density_kernel, places),
        jax.ShapeDtypeStruct((batches, points), f32),
        len(arrays) + 4,
        scalars=2,
        scratch=(pltpu.VMEM((table_rows, wide), bf16), pltpu.VMEM((batches, kept, columns), bf16)),
        flops=2 * batches * points * columns * kept,
        moved=2 * batches * points * columns * 2,
    )(place, core_at, *arrays, own_rows, other_rows, left, basis_values)
    partial_other = swap(partial, "orb", 2, 1)

    out_places = [list(range(dz * rows_x, (dz + 1) * rows_x)) for dz in [0] + near]
    out_places += [[dz * rows_x + dx] for dz in far for dx in [0] + side]
    sums = call(
        functools.partial(scatter_kernel, out_places),
        [jax.ShapeDtypeStruct((held * len(blocks), wide), bf16) for blocks in out_places],
        7,
        scalars=2,
        scratch=(pltpu.VMEM((entries, wide), bf16), pltpu.VMEM((entries, wide), bf16)),
        flops=2 * batches * points * columns * kept,
        moved=2 * batches * points * columns * 2,
    )(place, core_at, partial, partial_other, point_weights, basis_values, left_t, own_rows, other_rows)

    clusters, singles = sums[:len(near) + 1], sums[len(near) + 1:]
    landed = []
    for i, dz in enumerate(far):
        joined = singles[i * rows_x].astype(f32)
        for dx in side:
            joined = joined + swap(singles[i * rows_x + dx], "pair", rows_x, dx).astype(f32)
        landed.append(swap(joined.astype(bf16), "batch", rows_z, dz).astype(f32))
    cluster = clusters[0].astype(f32)
    for dz, array in zip(near, clusters[1:]):
        cluster = cluster + swap(array, "batch", rows_z, dz).astype(f32)
    mine_total = cluster[:held]
    for dx in side:
        mine_total = mine_total + swap(cluster[dx * held:(dx + 1) * held].astype(bf16), "pair", rows_x, dx).astype(f32)
    total = mine_total + landed[1] + landed[0]
    total_other = swap(total, "orb", 2, 1)
    return call(
        finish_kernel, jax.ShapeDtypeStruct((held, square), f32), 3, scalars=1, moved=held * square * 12
    )(half_at, total, total_other, core_blocks)


def solution(mesh):
    placed = (
        P(("groups", "batch", "pair"), None, None),
        P(("groups", "batch", "pair"), None),
        P(("groups", "batch", "pair"), None, "orb"),
        P(("groups", "batch", "pair"), "orb", None, None),
        P(("groups", "batch", "pair"), None),
        P(("groups", "batch", "pair"), None),
    )
    return jax.shard_map(
        per_device,
        mesh=mesh,
        in_specs=placed,
        out_specs=P(("groups", "batch", "pair"), None),
        check_vma=False,
    )
```

```python
import functools

import jax
import jax.numpy as jnp
from jax import lax
from jax.experimental import pallas as pl
from jax.experimental.pallas import tpu as pltpu
from jax.sharding import PartitionSpec as P

GO = 64
VMEM_LIMIT = 50 * 1024 * 1024
NT = (((1,), (1,)), ((), ()))


def split_dot(left, right, dims=None):
    if dims is None:
        return jnp.dot(left, right, preferred_element_type=jnp.float32)
    return lax.dot_general(left, right, dims, preferred_element_type=jnp.float32)


def prepare_kernel(half_ref, values_ref, left_ref, left_t_ref):
    batches, points, columns = values_ref.shape
    groups = columns // GO
    kept = left_ref.shape[2]
    first = half_ref[0] * (kept // groups)
    at = lax.broadcasted_iota(jnp.int32, (kept, columns), 0)
    lane = lax.broadcasted_iota(jnp.int32, (kept, columns), 1)
    wanted = (at % groups) * GO + first + at // groups
    select = jnp.where(lane == wanted, 1.0, 0.0).astype(jnp.bfloat16)
    for t in range(batches):
        left_ref[t] = split_dot(values_ref[t], select, NT).astype(jnp.bfloat16)
        left_t_ref[t] = split_dot(select, values_ref[t], NT).astype(jnp.bfloat16)


def index_kernel(held, fetch_ref, slots_ref, rows_ref):
    owners, capacity = fetch_ref.shape
    slots = slots_ref[...]
    entries = slots.shape[1]
    owner = slots // capacity
    owner_hot = jnp.where(lax.broadcasted_iota(jnp.int32, (owners, entries), 0) == owner, 1.0, 0.0)
    stored = fetch_ref[...].astype(jnp.float32).T.astype(jnp.bfloat16)
    listed = split_dot(stored, owner_hot.astype(jnp.bfloat16)).astype(jnp.int32)
    at = lax.broadcasted_iota(jnp.int32, (capacity, entries), 0)
    chosen = jnp.where(at == slots - owner * capacity, listed, 0)
    rows_ref[...] = jnp.sum(chosen, axis=0, keepdims=True) + owner * held


def row_table(place_ref, core_ref, own_ref, other_ref, held, owners):
    low = core_ref[0] == 0
    rows = jnp.concatenate(
        [jnp.where(low, own_ref[...], other_ref[...]), jnp.where(low, other_ref[...], own_ref[...])], axis=1
    )
    rows = lax.bitwise_xor(rows, place_ref[0] * held)
    row = lax.broadcasted_iota(jnp.int32, (owners * held, rows.shape[1]), 0)
    return jnp.where(row == rows, 1.0, 0.0)


def density_kernel(places, place_ref, core_ref, *refs):
    piece_refs = refs[:len(places)]
    own_ref, other_ref, left_ref, values_ref, out_ref, table, dense = refs[len(places):]
    batches, points, columns = values_ref.shape
    groups = columns // GO
    owners = sum(len(blocks) for blocks in places)
    held = table.shape[0] // owners
    for ref, blocks in zip(piece_refs, places):
        table[blocks[0] * held:(blocks[-1] + 1) * held, :] = ref[...]
    pick = row_table(place_ref, core_ref, own_ref, other_ref, held, owners).T.astype(jnp.bfloat16)
    low = lax.broadcasted_iota(jnp.int32, (1, 1, 1, groups, 128), 4) < GO
    for chunk in range(table.shape[1] // 256):
        wide = split_dot(pick, table[:, chunk * 256:(chunk + 1) * 256])
        for j in (2 * chunk, 2 * chunk + 1):
            got = wide[:, (j % 2) * 128:(j % 2 + 1) * 128].reshape(2, batches, groups // 4, 2, groups, 128)
            even, odd = got[:, :, :, 0], got[:, :, :, 1]
            first = jnp.where(low, even, pltpu.roll(odd, GO, 4))
            second = jnp.where(low, pltpu.roll(even, GO, 4), odd)
            for t in range(batches):
                for q in range(groups // 2):
                    at = (q // (groups // 4), t, q % (groups // 4))
                    both = jnp.concatenate([first[at], second[at]], axis=0)
                    dense[t, j * 2 * groups:(j + 1) * 2 * groups, q * 128:(q + 1) * 128] = both.astype(jnp.bfloat16)
    for t in range(batches):
        product = split_dot(left_ref[t], dense[t]) * values_ref[t].astype(jnp.float32)
        folded = product[:, :128]
        for q in range(1, columns // 128):
            folded = folded + product[:, q * 128:(q + 1) * 128]
        out_ref[t:t + 1, :] = jnp.sum(folded.T, axis=0, keepdims=True)


def scatter_kernel(places, place_ref, core_ref, *refs):
    mine_ref, far_ref, weight_ref, values_ref, left_t_ref, own_ref, other_ref = refs[:7]
    out_refs = refs[7:-2]
    high, rest = refs[-2:]
    target = {k: (ref, i) for ref, blocks in zip(out_refs, places) for i, k in enumerate(blocks)}
    pieces = len(target)
    held = out_refs[0].shape[0] // len(places[0])
    put = row_table(place_ref, core_ref, own_ref, other_ref, held, pieces).astype(jnp.bfloat16)
    batches, points, columns = values_ref.shape
    groups = columns // GO
    kept = left_t_ref.shape[1]
    steps = kept // (2 * groups)
    potential = weight_ref[...] * jnp.tanh(mine_ref[...] + far_ref[...])
    low = lax.broadcasted_iota(jnp.int32, (1, groups, 128), 2) < GO
    for t in range(batches):
        factor = jnp.broadcast_to(potential[t:t + 1, :], (128, points)).T
        factor = jnp.concatenate([factor] * (columns // 128), axis=1)
        weighted = (values_ref[t].astype(jnp.float32) * factor).astype(jnp.bfloat16)
        part = split_dot(left_t_ref[t], weighted)
        for q in range(groups // 2):
            cut = part[:, q * 128:(q + 1) * 128].reshape(steps, 2, groups, 128)
            first, second = cut[:, 0], cut[:, 1]
            even = jnp.where(low, first, pltpu.roll(second, GO, 2))
            odd = jnp.where(low, pltpu.roll(first, GO, 2), second)
            side, pair = q // (groups // 4), q % (groups // 4)
            at = ((side * batches + t) * (groups // 2) + 2 * pair) * groups
            for j in range(steps):
                both = jnp.concatenate([even[j], odd[j]], axis=0)
                top = both.astype(jnp.bfloat16)
                high[at:at + 2 * groups, j * 128:(j + 1) * 128] = top
                rest[at:at + 2 * groups, j * 128:(j + 1) * 128] = (both - top.astype(jnp.float32)).astype(jnp.bfloat16)
    step = max(1, min(pieces, 128 // held))
    for k in range(0, pieces, step):
        some = put[k * held:(k + step) * held, :]
        total = split_dot(some, high[...]) + split_dot(some, rest[...])
        for i in range(step):
            ref, at = target[k + i]
            ref[at * held:(at + 1) * held, :] = total[i * held:(i + 1) * held, :].astype(jnp.bfloat16)


def finish_kernel(half_ref, mine_ref, other_ref, core_ref, out_ref):
    wide = mine_ref.shape[1]
    own = pl.multiple_of(half_ref[0] * wide, wide)
    far = pl.multiple_of((1 - half_ref[0]) * wide, wide)
    out_ref[:, pl.ds(own, wide)] = core_ref[:, pl.ds(own, wide)].astype(jnp.float32) + mine_ref[...]
    out_ref[:, pl.ds(far, wide)] = core_ref[:, pl.ds(far, wide)].astype(jnp.float32) + other_ref[...]


def call(kernel, outs, count, scratch=(), scalars=0, flops=0, moved=0):
    specs = [pl.BlockSpec(memory_space=pltpu.VMEM)] * count
    specs = [pl.BlockSpec(memory_space=pltpu.SMEM)] * scalars + specs
    out_specs = jax.tree.map(lambda _: pl.BlockSpec(memory_space=pltpu.VMEM), outs)
    return pl.pallas_call(
        kernel,
        out_shape=outs,
        in_specs=specs,
        out_specs=out_specs,
        scratch_shapes=list(scratch),
        compiler_params=pltpu.CompilerParams(vmem_limit_bytes=VMEM_LIMIT),
        cost_estimate=pl.CostEstimate(flops=flops, bytes_accessed=moved, transcendentals=0),
    )


def swap(array, axis, count, step):
    return lax.ppermute(array, axis, [(i, i ^ step) for i in range(count)])


def per_device(basis_values, point_weights, slot_ids, fetch_rows, density_blocks, core_blocks):
    rows_z, rows_x = lax.axis_size("batch"), lax.axis_size("pair")
    z, x, half = lax.axis_index("batch"), lax.axis_index("pair"), lax.axis_index("orb")
    owners = rows_z * rows_x
    batches, points, columns = basis_values.shape
    groups, own_groups = slot_ids.shape[1], slot_ids.shape[2]
    held, square = density_blocks.shape
    capacity = fetch_rows.shape[3]
    wide = square // 2
    table_rows = owners * held
    entries = batches * groups * groups
    kept = columns // 2
    bf16, f32 = jnp.bfloat16, jnp.float32

    own_rows = call(
        functools.partial(index_kernel, held),
        jax.ShapeDtypeStruct((1, batches * own_groups * groups), jnp.int32),
        2,
    )(fetch_rows.reshape(owners, capacity), slot_ids.transpose(0, 2, 1).reshape(1, -1))
    other_rows = swap(own_rows, "orb", 2, 1)

    far = list(range(rows_z // 2, rows_z))
    near = list(range(1, rows_z // 2))
    side = list(range(1, rows_x))

    mine = lax.dynamic_slice_in_dim(density_blocks, half * wide, wide, 1)
    direct = {dz: swap(mine, "batch", rows_z, dz) for dz in far}
    beside = [
        lax.dynamic_slice_in_dim(swap(density_blocks, "pair", rows_x, dx), half * wide, wide, 1) for dx in side
    ]
    *beside, own_rows = lax.optimization_barrier((*beside, own_rows))
    cluster = jnp.concatenate([mine, *beside], axis=0)
    arrays, places = [cluster], [list(range(rows_x))]
    for dz in near:
        arrays.append(swap(cluster, "batch", rows_z, dz))
        places.append(list(range(dz * rows_x, (dz + 1) * rows_x)))
    direct[far[0]], other_rows = lax.optimization_barrier((direct[far[0]], other_rows))
    for dz in far:
        arrays.append(direct[dz])
        places.append([dz * rows_x])
        for dx in side:
            arrays.append(swap(direct[dz], "pair", rows_x, dx))
            places.append([dz * rows_x + dx])

    half_at, _ = lax.optimization_barrier((half.reshape(1).astype(jnp.int32), direct[far[-1]]))
    left, left_t = call(
        prepare_kernel,
        (
            jax.ShapeDtypeStruct((batches, points, kept), bf16),
            jax.ShapeDtypeStruct((batches, kept, points), bf16),
        ),
        1,
        scalars=1,
        flops=4 * batches * points * columns * kept,
        moved=3 * batches * points * columns * 2,
    )(half_at, basis_values)

    place = (z * rows_x + x).reshape(1).astype(jnp.int32)
    core_at = half.reshape(1).astype(jnp.int32)

    partial = call(
        functools.partial(density_kernel, places),
        jax.ShapeDtypeStruct((batches, points), f32),
        len(arrays) + 4,
        scalars=2,
        scratch=(pltpu.VMEM((table_rows, wide), bf16), pltpu.VMEM((batches, kept, columns), bf16)),
        flops=2 * batches * points * columns * kept,
        moved=2 * batches * points * columns * 2,
    )(place, core_at, *arrays, own_rows, other_rows, left, basis_values)
    partial_other = swap(partial, "orb", 2, 1)

    out_places = [list(range(dz * rows_x, (dz + 1) * rows_x)) for dz in [0] + near]
    out_places += [[dz * rows_x + dx] for dz in far for dx in [0] + side]
    sums = call(
        functools.partial(scatter_kernel, out_places),
        [jax.ShapeDtypeStruct((held * len(blocks), wide), bf16) for blocks in out_places],
        7,
        scalars=2,
        scratch=(pltpu.VMEM((entries, wide), bf16), pltpu.VMEM((entries, wide), bf16)),
        flops=2 * batches * points * columns * kept,
        moved=2 * batches * points * columns * 2,
    )(place, core_at, partial, partial_other, point_weights, basis_values, left_t, own_rows, other_rows)

    clusters, singles = sums[:len(near) + 1], sums[len(near) + 1:]
    landed = []
    for i, dz in enumerate(far):
        joined = singles[i * rows_x].astype(f32)
        for dx in side:
            joined = joined + swap(singles[i * rows_x + dx], "pair", rows_x, dx).astype(f32)
        landed.append(swap(joined.astype(bf16), "batch", rows_z, dz).astype(f32))
    cluster = clusters[0].astype(f32)
    for dz, array in zip(near, clusters[1:]):
        cluster = cluster + swap(array, "batch", rows_z, dz).astype(f32)
    total = cluster[:held]
    for dx in side:
        total = total + swap(cluster[dx * held:(dx + 1) * held].astype(bf16), "pair", rows_x, dx).astype(f32)
    for term in landed:
        total = total + term
    total_other = swap(total, "orb", 2, 1)
    return call(
        finish_kernel, jax.ShapeDtypeStruct((held, square), f32), 3, scalars=1, moved=held * square * 12
    )(half_at, total, total_other, core_blocks)


def solution(mesh):
    placed = (
        P(("groups", "batch", "pair"), None, None),
        P(("groups", "batch", "pair"), None),
        P(("groups", "batch", "pair"), None, "orb"),
        P(("groups", "batch", "pair"), "orb", None, None),
        P(("groups", "batch", "pair"), None),
        P(("groups", "batch", "pair"), None),
    )
    return jax.shard_map(
        per_device,
        mesh=mesh,
        in_specs=placed,
        out_specs=P(("groups", "batch", "pair"), None),
        check_vma=False,
    )
```

```python
import functools

import jax
import jax.numpy as jnp
from jax import lax
from jax.experimental import pallas as pl
from jax.experimental.pallas import tpu as pltpu
from jax.sharding import PartitionSpec as P

GO = 64
VMEM_LIMIT = 50 * 1024 * 1024
NT = (((1,), (1,)), ((), ()))


def split_dot(left, right, dims=None):
    if dims is None:
        return jnp.dot(left, right, preferred_element_type=jnp.float32)
    return lax.dot_general(left, right, dims, preferred_element_type=jnp.float32)


def prepare_kernel(half_ref, values_ref, left_ref, left_t_ref):
    batches, points, columns = values_ref.shape
    groups = columns // GO
    kept = left_ref.shape[2]
    first = half_ref[0] * (kept // groups)
    at = lax.broadcasted_iota(jnp.int32, (kept, columns), 0)
    lane = lax.broadcasted_iota(jnp.int32, (kept, columns), 1)
    wanted = (at % groups) * GO + first + at // groups
    select = jnp.where(lane == wanted, 1.0, 0.0).astype(jnp.bfloat16)
    for t in range(batches):
        left_ref[t] = split_dot(values_ref[t], select, NT).astype(jnp.bfloat16)
        left_t_ref[t] = split_dot(select, values_ref[t], NT).astype(jnp.bfloat16)


def index_kernel(held, fetch_ref, slots_ref, rows_ref):
    owners, capacity = fetch_ref.shape
    slots = slots_ref[...]
    entries = slots.shape[1]
    owner = slots // capacity
    owner_hot = jnp.where(lax.broadcasted_iota(jnp.int32, (owners, entries), 0) == owner, 1.0, 0.0)
    stored = fetch_ref[...].astype(jnp.float32).T.astype(jnp.bfloat16)
    listed = split_dot(stored, owner_hot.astype(jnp.bfloat16)).astype(jnp.int32)
    at = lax.broadcasted_iota(jnp.int32, (capacity, entries), 0)
    chosen = jnp.where(at == slots - owner * capacity, listed, 0)
    rows_ref[...] = jnp.sum(chosen, axis=0, keepdims=True) + owner * held


def row_table(place_ref, core_ref, own_ref, other_ref, held, owners):
    low = core_ref[0] == 0
    rows = jnp.concatenate(
        [jnp.where(low, own_ref[...], other_ref[...]), jnp.where(low, other_ref[...], own_ref[...])], axis=1
    )
    rows = lax.bitwise_xor(rows, place_ref[0] * held)
    row = lax.broadcasted_iota(jnp.int32, (owners * held, rows.shape[1]), 0)
    return jnp.where(row == rows, 1.0, 0.0)


def density_kernel(places, place_ref, core_ref, *refs):
    piece_refs = refs[:len(places)]
    own_ref, other_ref, left_ref, values_ref, out_ref, table, dense = refs[len(places):]
    batches, points, columns = values_ref.shape
    groups = columns // GO
    owners = sum(len(blocks) for blocks in places)
    held = table.shape[0] // owners
    for ref, blocks in zip(piece_refs, places):
        for i, k in enumerate(blocks):
            table[k * held:(k + 1) * held, :] = ref[i * held:(i + 1) * held, :]
    pick = row_table(place_ref, core_ref, own_ref, other_ref, held, owners).T.astype(jnp.bfloat16)
    low = lax.broadcasted_iota(jnp.int32, (1, 1, 1, groups, 128), 4) < GO
    for chunk in range(table.shape[1] // 256):
        wide = split_dot(pick, table[:, chunk * 256:(chunk + 1) * 256])
        for j in (2 * chunk, 2 * chunk + 1):
            got = wide[:, (j % 2) * 128:(j % 2 + 1) * 128].reshape(2, batches, groups // 4, 2, groups, 128)
            even, odd = got[:, :, :, 0], got[:, :, :, 1]
            first = jnp.where(low, even, pltpu.roll(odd, GO, 4))
            second = jnp.where(low, pltpu.roll(even, GO, 4), odd)
            for t in range(batches):
                for q in range(groups // 2):
                    at = (q // (groups // 4), t, q % (groups // 4))
                    both = jnp.concatenate([first[at], second[at]], axis=0)
                    dense[t, j * 2 * groups:(j + 1) * 2 * groups, q * 128:(q + 1) * 128] = both.astype(jnp.bfloat16)
    for t in range(batches):
        product = split_dot(left_ref[t], dense[t]) * values_ref[t].astype(jnp.float32)
        folded = product[:, :128]
        for q in range(1, columns // 128):
            folded = folded + product[:, q * 128:(q + 1) * 128]
        out_ref[t:t + 1, :] = jnp.sum(folded.T, axis=0, keepdims=True)


def scatter_kernel(places, place_ref, core_ref, *refs):
    mine_ref, far_ref, weight_ref, values_ref, left_t_ref, own_ref, other_ref = refs[:7]
    out_refs = refs[7:-2]
    high, rest = refs[-2:]
    target = {k: (ref, i) for ref, blocks in zip(out_refs, places) for i, k in enumerate(blocks)}
    pieces = len(target)
    held = out_refs[0].shape[0] // len(places[0])
    put = row_table(place_ref, core_ref, own_ref, other_ref, held, pieces).astype(jnp.bfloat16)
    batches, points, columns = values_ref.shape
    groups = columns // GO
    kept = left_t_ref.shape[1]
    steps = kept // (2 * groups)
    potential = weight_ref[...] * jnp.tanh(mine_ref[...] + far_ref[...])
    low = lax.broadcasted_iota(jnp.int32, (1, groups, 128), 2) < GO
    for t in range(batches):
        factor = jnp.broadcast_to(potential[t:t + 1, :], (128, points)).T
        factor = jnp.concatenate([factor] * (columns // 128), axis=1)
        weighted = (values_ref[t].astype(jnp.float32) * factor).astype(jnp.bfloat16)
        part = split_dot(left_t_ref[t], weighted)
        for q in range(groups // 2):
            cut = part[:, q * 128:(q + 1) * 128].reshape(steps, 2, groups, 128)
            first, second = cut[:, 0], cut[:, 1]
            even = jnp.where(low, first, pltpu.roll(second, GO, 2))
            odd = jnp.where(low, pltpu.roll(first, GO, 2), second)
            side, pair = q // (groups // 4), q % (groups // 4)
            at = ((side * batches + t) * (groups // 2) + 2 * pair) * groups
            for j in range(steps):
                both = jnp.concatenate([even[j], odd[j]], axis=0)
                top = both.astype(jnp.bfloat16)
                high[at:at + 2 * groups, j * 128:(j + 1) * 128] = top
                rest[at:at + 2 * groups, j * 128:(j + 1) * 128] = (both - top.astype(jnp.float32)).astype(jnp.bfloat16)
    step = max(1, min(pieces, 128 // held))
    for k in range(0, pieces, step):
        some = put[k * held:(k + step) * held, :]
        total = split_dot(some, high[...]) + split_dot(some, rest[...])
        for i in range(step):
            ref, at = target[k + i]
            ref[at * held:(at + 1) * held, :] = total[i * held:(i + 1) * held, :].astype(jnp.bfloat16)


def finish_kernel(half_ref, mine_ref, other_ref, core_ref, out_ref):
    wide = mine_ref.shape[1]
    own = pl.multiple_of(half_ref[0] * wide, wide)
    far = pl.multiple_of((1 - half_ref[0]) * wide, wide)
    out_ref[:, pl.ds(own, wide)] = core_ref[:, pl.ds(own, wide)].astype(jnp.float32) + mine_ref[...]
    out_ref[:, pl.ds(far, wide)] = core_ref[:, pl.ds(far, wide)].astype(jnp.float32) + other_ref[...]


def call(kernel, outs, count, scratch=(), scalars=0, flops=0, moved=0):
    specs = [pl.BlockSpec(memory_space=pltpu.VMEM)] * count
    specs = [pl.BlockSpec(memory_space=pltpu.SMEM)] * scalars + specs
    out_specs = jax.tree.map(lambda _: pl.BlockSpec(memory_space=pltpu.VMEM), outs)
    return pl.pallas_call(
        kernel,
        out_shape=outs,
        in_specs=specs,
        out_specs=out_specs,
        scratch_shapes=list(scratch),
        compiler_params=pltpu.CompilerParams(vmem_limit_bytes=VMEM_LIMIT),
        cost_estimate=pl.CostEstimate(flops=flops, bytes_accessed=moved, transcendentals=0),
    )


def swap(array, axis, count, step):
    return lax.ppermute(array, axis, [(i, i ^ step) for i in range(count)])


def per_device(basis_values, point_weights, slot_ids, fetch_rows, density_blocks, core_blocks):
    rows_z, rows_x = lax.axis_size("batch"), lax.axis_size("pair")
    z, x, half = lax.axis_index("batch"), lax.axis_index("pair"), lax.axis_index("orb")
    owners = rows_z * rows_x
    batches, points, columns = basis_values.shape
    groups, own_groups = slot_ids.shape[1], slot_ids.shape[2]
    held, square = density_blocks.shape
    capacity = fetch_rows.shape[3]
    wide = square // 2
    table_rows = owners * held
    entries = batches * groups * groups
    kept = columns // 2
    bf16, f32 = jnp.bfloat16, jnp.float32

    own_rows = call(
        functools.partial(index_kernel, held),
        jax.ShapeDtypeStruct((1, batches * own_groups * groups), jnp.int32),
        2,
    )(fetch_rows.reshape(owners, capacity), slot_ids.transpose(0, 2, 1).reshape(1, -1))
    other_rows = swap(own_rows, "orb", 2, 1)

    far = list(range(rows_z // 2, rows_z))
    near = list(range(1, rows_z // 2))
    side = list(range(1, rows_x))

    mine = lax.dynamic_slice_in_dim(density_blocks, half * wide, wide, 1)
    direct = {dz: swap(mine, "batch", rows_z, dz) for dz in far}
    beside = [swap(mine, "pair", rows_x, dx) for dx in side]
    *beside, own_rows = lax.optimization_barrier((*beside, own_rows))
    cluster = jnp.concatenate([mine, *beside], axis=0)
    arrays, places = [cluster], [list(range(rows_x))]
    for dz in near:
        arrays.append(swap(cluster, "batch", rows_z, dz))
        places.append(list(range(dz * rows_x, (dz + 1) * rows_x)))
    middle = jnp.concatenate([direct[dz] for dz in far], axis=0)
    for dx in [0] + side:
        arrays.append(middle if dx == 0 else swap(middle, "pair", rows_x, dx))
        places.append([dz * rows_x + dx for dz in far])

    half_at, _ = lax.optimization_barrier((half.reshape(1).astype(jnp.int32), arrays[len(near)]))
    left, left_t = call(
        prepare_kernel,
        (
            jax.ShapeDtypeStruct((batches, points, kept), bf16),
            jax.ShapeDtypeStruct((batches, kept, points), bf16),
        ),
        1,
        scalars=1,
        flops=4 * batches * points * columns * kept,
        moved=3 * batches * points * columns * 2,
    )(half_at, basis_values)

    place = (z * rows_x + x).reshape(1).astype(jnp.int32)
    core_at = half.reshape(1).astype(jnp.int32)

    partial = call(
        functools.partial(density_kernel, places),
        jax.ShapeDtypeStruct((batches, points), f32),
        len(arrays) + 4,
        scalars=2,
        scratch=(pltpu.VMEM((table_rows, wide), bf16), pltpu.VMEM((batches, kept, columns), bf16)),
        flops=2 * batches * points * columns * kept,
        moved=2 * batches * points * columns * 2,
    )(place, core_at, *arrays, own_rows, other_rows, left, basis_values)
    partial_other = swap(partial, "orb", 2, 1)

    out_places = [list(range(dz * rows_x, (dz + 1) * rows_x)) for dz in [0] + near]
    out_places += [[dz * rows_x + dx] for dz in far for dx in [0] + side]
    sums = call(
        functools.partial(scatter_kernel, out_places),
        [jax.ShapeDtypeStruct((held * len(blocks), wide), bf16) for blocks in out_places],
        7,
        scalars=2,
        scratch=(pltpu.VMEM((entries, wide), bf16), pltpu.VMEM((entries, wide), bf16)),
        flops=2 * batches * points * columns * kept,
        moved=2 * batches * points * columns * 2,
    )(place, core_at, partial, partial_other, point_weights, basis_values, left_t, own_rows, other_rows)

    clusters, singles = sums[:len(near) + 1], sums[len(near) + 1:]
    landed = []
    for i, dz in enumerate(far):
        joined = singles[i * rows_x].astype(f32)
        for dx in side:
            joined = joined + swap(singles[i * rows_x + dx], "pair", rows_x, dx).astype(f32)
        landed.append(swap(joined.astype(bf16), "batch", rows_z, dz).astype(f32))
    cluster = clusters[0].astype(f32)
    for dz, array in zip(near, clusters[1:]):
        cluster = cluster + swap(array, "batch", rows_z, dz).astype(f32)
    total = cluster[:held]
    for dx in side:
        total = total + swap(cluster[dx * held:(dx + 1) * held].astype(bf16), "pair", rows_x, dx).astype(f32)
    for term in landed:
        total = total + term
    total_other = swap(total, "orb", 2, 1)
    return call(
        finish_kernel, jax.ShapeDtypeStruct((held, square), f32), 3, scalars=1, moved=held * square * 12
    )(half_at, total, total_other, core_blocks)


def solution(mesh):
    placed = (
        P(("groups", "batch", "pair"), None, None),
        P(("groups", "batch", "pair"), None),
        P(("groups", "batch", "pair"), None, "orb"),
        P(("groups", "batch", "pair"), "orb", None, None),
        P(("groups", "batch", "pair"), None),
        P(("groups", "batch", "pair"), None),
    )
    return jax.shard_map(
        per_device,
        mesh=mesh,
        in_specs=placed,
        out_specs=P(("groups", "batch", "pair"), None),
        check_vma=False,
    )
```

```python
import functools

import jax
import jax.numpy as jnp
from jax import lax
from jax.experimental import pallas as pl
from jax.experimental.pallas import tpu as pltpu
from jax.sharding import PartitionSpec as P

GO = 64
VMEM_LIMIT = 50 * 1024 * 1024
NT = (((1,), (1,)), ((), ()))


def split_dot(left, right, dims=None):
    if dims is None:
        return jnp.dot(left, right, preferred_element_type=jnp.float32)
    return lax.dot_general(left, right, dims, preferred_element_type=jnp.float32)


def prepare_kernel(half_ref, values_ref, left_ref, left_t_ref):
    batches, points, columns = values_ref.shape
    groups = columns // GO
    kept = left_ref.shape[2]
    first = half_ref[0] * (kept // groups)
    at = lax.broadcasted_iota(jnp.int32, (kept, columns), 0)
    lane = lax.broadcasted_iota(jnp.int32, (kept, columns), 1)
    wanted = (at % groups) * GO + first + at // groups
    select = jnp.where(lane == wanted, 1.0, 0.0).astype(jnp.bfloat16)
    for t in range(batches):
        left_ref[t] = split_dot(values_ref[t], select, NT).astype(jnp.bfloat16)
        left_t_ref[t] = split_dot(select, values_ref[t], NT).astype(jnp.bfloat16)


def index_kernel(held, fetch_ref, slots_ref, rows_ref):
    owners, capacity = fetch_ref.shape
    slots = slots_ref[...]
    entries = slots.shape[1]
    owner = slots // capacity
    owner_hot = jnp.where(lax.broadcasted_iota(jnp.int32, (owners, entries), 0) == owner, 1.0, 0.0)
    stored = fetch_ref[...].astype(jnp.float32).T.astype(jnp.bfloat16)
    listed = split_dot(stored, owner_hot.astype(jnp.bfloat16)).astype(jnp.int32)
    at = lax.broadcasted_iota(jnp.int32, (capacity, entries), 0)
    chosen = jnp.where(at == slots - owner * capacity, listed, 0)
    rows_ref[...] = jnp.sum(chosen, axis=0, keepdims=True) + owner * held


def row_table(place_ref, core_ref, own_ref, other_ref, held, owners):
    low = core_ref[0] == 0
    rows = jnp.concatenate(
        [jnp.where(low, own_ref[...], other_ref[...]), jnp.where(low, other_ref[...], own_ref[...])], axis=1
    )
    rows = lax.bitwise_xor(rows, place_ref[0] * held)
    row = lax.broadcasted_iota(jnp.int32, (owners * held, rows.shape[1]), 0)
    return jnp.where(row == rows, 1.0, 0.0)


def density_kernel(places, place_ref, core_ref, *refs):
    piece_refs = refs[:len(places)]
    own_ref, other_ref, left_ref, values_ref, out_ref, table, dense = refs[len(places):]
    batches, points, columns = values_ref.shape
    groups = columns // GO
    owners = sum(len(blocks) for blocks in places)
    held = table.shape[0] // owners
    for ref, blocks in zip(piece_refs, places):
        table[blocks[0] * held:(blocks[-1] + 1) * held, :] = ref[...]
    pick = row_table(place_ref, core_ref, own_ref, other_ref, held, owners).T.astype(jnp.bfloat16)
    low = lax.broadcasted_iota(jnp.int32, (1, 1, 1, groups, 128), 4) < GO
    for chunk in range(table.shape[1] // 256):
        wide = split_dot(pick, table[:, chunk * 256:(chunk + 1) * 256])
        for j in (2 * chunk, 2 * chunk + 1):
            got = wide[:, (j % 2) * 128:(j % 2 + 1) * 128].reshape(2, batches, groups // 4, 2, groups, 128)
            even, odd = got[:, :, :, 0], got[:, :, :, 1]
            first = jnp.where(low, even, pltpu.roll(odd, GO, 4))
            second = jnp.where(low, pltpu.roll(even, GO, 4), odd)
            for t in range(batches):
                for q in range(groups // 2):
                    at = (q // (groups // 4), t, q % (groups // 4))
                    both = jnp.concatenate([first[at], second[at]], axis=0)
                    dense[t, j * 2 * groups:(j + 1) * 2 * groups, q * 128:(q + 1) * 128] = both.astype(jnp.bfloat16)
    for t in range(batches):
        product = split_dot(left_ref[t], dense[t]) * values_ref[t].astype(jnp.float32)
        folded = product[:, :128]
        for q in range(1, columns // 128):
            folded = folded + product[:, q * 128:(q + 1) * 128]
        out_ref[t:t + 1, :] = jnp.sum(folded.T, axis=0, keepdims=True)


def scatter_kernel(places, place_ref, core_ref, *refs):
    mine_ref, far_ref, weight_ref, values_ref, left_t_ref, own_ref, other_ref = refs[:7]
    out_refs = refs[7:-2]
    high, rest = refs[-2:]
    target = {k: (ref, i) for ref, blocks in zip(out_refs, places) for i, k in enumerate(blocks)}
    pieces = len(target)
    held = out_refs[0].shape[0] // len(places[0])
    put = row_table(place_ref, core_ref, own_ref, other_ref, held, pieces).astype(jnp.bfloat16)
    batches, points, columns = values_ref.shape
    groups = columns // GO
    kept = left_t_ref.shape[1]
    steps = kept // (2 * groups)
    potential = weight_ref[...] * jnp.tanh(mine_ref[...] + far_ref[...])
    low = lax.broadcasted_iota(jnp.int32, (1, groups, 128), 2) < GO
    for t in range(batches):
        factor = jnp.broadcast_to(potential[t:t + 1, :], (128, points)).T
        factor = jnp.concatenate([factor] * (columns // 128), axis=1)
        weighted = (values_ref[t].astype(jnp.float32) * factor).astype(jnp.bfloat16)
        part = split_dot(left_t_ref[t], weighted)
        for q in range(groups // 2):
            cut = part[:, q * 128:(q + 1) * 128].reshape(steps, 2, groups, 128)
            first, second = cut[:, 0], cut[:, 1]
            even = jnp.where(low, first, pltpu.roll(second, GO, 2))
            odd = jnp.where(low, pltpu.roll(first, GO, 2), second)
            side, pair = q // (groups // 4), q % (groups // 4)
            at = ((side * batches + t) * (groups // 2) + 2 * pair) * groups
            for j in range(steps):
                both = jnp.concatenate([even[j], odd[j]], axis=0)
                top = both.astype(jnp.bfloat16)
                high[at:at + 2 * groups, j * 128:(j + 1) * 128] = top
                rest[at:at + 2 * groups, j * 128:(j + 1) * 128] = (both - top.astype(jnp.float32)).astype(jnp.bfloat16)
    step = max(1, min(pieces, 128 // held))
    for k in range(0, pieces, step):
        some = put[k * held:(k + step) * held, :]
        total = split_dot(some, high[...]) + split_dot(some, rest[...])
        for i in range(step):
            ref, at = target[k + i]
            ref[at * held:(at + 1) * held, :] = total[i * held:(i + 1) * held, :].astype(jnp.bfloat16)


def finish_kernel(half_ref, mine_ref, other_ref, core_ref, out_hbm, total, sent):
    wide = mine_ref.shape[1]
    size = wide // 2
    own = half_ref[0] * wide
    far = (1 - half_ref[0]) * wide
    copies = []
    for first, term_ref in ((own, mine_ref), (far, other_ref)):
        for i in range(2):
            lanes = pl.ds(pl.multiple_of(first + i * size, size), size)
            total[:, lanes] = core_ref[:, lanes].astype(jnp.float32) + term_ref[:, i * size:(i + 1) * size]
            copy = pltpu.make_async_copy(total.at[:, lanes], out_hbm.at[:, lanes], sent.at[len(copies)])
            copy.start()
            copies.append(copy)
    for copy in copies:
        copy.wait()


def call(kernel, outs, count, scratch=(), scalars=0, flops=0, moved=0):
    specs = [pl.BlockSpec(memory_space=pltpu.VMEM)] * count
    specs = [pl.BlockSpec(memory_space=pltpu.SMEM)] * scalars + specs
    out_specs = jax.tree.map(lambda _: pl.BlockSpec(memory_space=pltpu.VMEM), outs)
    return pl.pallas_call(
        kernel,
        out_shape=outs,
        in_specs=specs,
        out_specs=out_specs,
        scratch_shapes=list(scratch),
        compiler_params=pltpu.CompilerParams(vmem_limit_bytes=VMEM_LIMIT),
        cost_estimate=pl.CostEstimate(flops=flops, bytes_accessed=moved, transcendentals=0),
    )


def swap(array, axis, count, step):
    return lax.ppermute(array, axis, [(i, i ^ step) for i in range(count)])


def per_device(basis_values, point_weights, slot_ids, fetch_rows, density_blocks, core_blocks):
    rows_z, rows_x = lax.axis_size("batch"), lax.axis_size("pair")
    z, x, half = lax.axis_index("batch"), lax.axis_index("pair"), lax.axis_index("orb")
    owners = rows_z * rows_x
    batches, points, columns = basis_values.shape
    groups, own_groups = slot_ids.shape[1], slot_ids.shape[2]
    held, square = density_blocks.shape
    capacity = fetch_rows.shape[3]
    wide = square // 2
    table_rows = owners * held
    entries = batches * groups * groups
    kept = columns // 2
    bf16, f32 = jnp.bfloat16, jnp.float32

    own_rows = call(
        functools.partial(index_kernel, held),
        jax.ShapeDtypeStruct((1, batches * own_groups * groups), jnp.int32),
        2,
    )(fetch_rows.reshape(owners, capacity), slot_ids.transpose(0, 2, 1).reshape(1, -1))
    other_rows = swap(own_rows, "orb", 2, 1)

    far = list(range(rows_z // 2, rows_z))
    near = list(range(1, rows_z // 2))
    side = list(range(1, rows_x))

    mine = lax.dynamic_slice_in_dim(density_blocks, half * wide, wide, 1)
    direct = {dz: swap(mine, "batch", rows_z, dz) for dz in far}
    beside = [swap(mine, "pair", rows_x, dx) for dx in side]
    *beside, own_rows = lax.optimization_barrier((*beside, own_rows))
    cluster = jnp.concatenate([mine, *beside], axis=0)
    arrays, places = [cluster], [list(range(rows_x))]
    for dz in near:
        arrays.append(swap(cluster, "batch", rows_z, dz))
        places.append(list(range(dz * rows_x, (dz + 1) * rows_x)))
    direct[far[0]], other_rows = lax.optimization_barrier((direct[far[0]], other_rows))
    for dz in far:
        arrays.append(direct[dz])
        places.append([dz * rows_x])
        for dx in side:
            arrays.append(swap(direct[dz], "pair", rows_x, dx))
            places.append([dz * rows_x + dx])

    half_at, _ = lax.optimization_barrier((half.reshape(1).astype(jnp.int32), direct[far[-1]]))
    left, left_t = call(
        prepare_kernel,
        (
            jax.ShapeDtypeStruct((batches, points, kept), bf16),
            jax.ShapeDtypeStruct((batches, kept, points), bf16),
        ),
        1,
        scalars=1,
        flops=4 * batches * points * columns * kept,
        moved=3 * batches * points * columns * 2,
    )(half_at, basis_values)

    place = (z * rows_x + x).reshape(1).astype(jnp.int32)
    core_at = half.reshape(1).astype(jnp.int32)

    partial = call(
        functools.partial(density_kernel, places),
        jax.ShapeDtypeStruct((batches, points), f32),
        len(arrays) + 4,
        scalars=2,
        scratch=(pltpu.VMEM((table_rows, wide), bf16), pltpu.VMEM((batches, kept, columns), bf16)),
        flops=2 * batches * points * columns * kept,
        moved=2 * batches * points * columns * 2,
    )(place, core_at, *arrays, own_rows, other_rows, left, basis_values)
    partial_other = swap(partial, "orb", 2, 1)

    out_places = [list(range(dz * rows_x, (dz + 1) * rows_x)) for dz in [0] + near]
    out_places += [[dz * rows_x + dx] for dz in far for dx in [0] + side]
    sums = call(
        functools.partial(scatter_kernel, out_places),
        [jax.ShapeDtypeStruct((held * len(blocks), wide), bf16) for blocks in out_places],
        7,
        scalars=2,
        scratch=(pltpu.VMEM((entries, wide), bf16), pltpu.VMEM((entries, wide), bf16)),
        flops=2 * batches * points * columns * kept,
        moved=2 * batches * points * columns * 2,
    )(place, core_at, partial, partial_other, point_weights, basis_values, left_t, own_rows, other_rows)

    clusters, singles = sums[:len(near) + 1], sums[len(near) + 1:]
    landed = []
    for i, dz in enumerate(far):
        joined = singles[i * rows_x].astype(f32)
        for dx in side:
            joined = joined + swap(singles[i * rows_x + dx], "pair", rows_x, dx).astype(f32)
        landed.append(swap(joined.astype(bf16), "batch", rows_z, dz).astype(f32))
    cluster = clusters[0].astype(f32)
    for dz, array in zip(near, clusters[1:]):
        cluster = cluster + swap(array, "batch", rows_z, dz).astype(f32)
    total = cluster[:held]
    for dx in side:
        total = total + swap(cluster[dx * held:(dx + 1) * held].astype(bf16), "pair", rows_x, dx).astype(f32)
    for term in landed:
        total = total + term
    total_other = swap(total, "orb", 2, 1)
    return pl.pallas_call(
        finish_kernel,
        out_shape=jax.ShapeDtypeStruct((held, square), f32),
        in_specs=[pl.BlockSpec(memory_space=pltpu.SMEM)] + [pl.BlockSpec(memory_space=pltpu.VMEM)] * 3,
        out_specs=pl.BlockSpec(memory_space=pl.ANY),
        scratch_shapes=[pltpu.VMEM((held, square), f32), pltpu.SemaphoreType.DMA((4,))],
        compiler_params=pltpu.CompilerParams(vmem_limit_bytes=VMEM_LIMIT),
        cost_estimate=pl.CostEstimate(flops=0, bytes_accessed=held * square * 12, transcendentals=0),
    )(half_at, total, total_other, core_blocks)


def solution(mesh):
    placed = (
        P(("groups", "batch", "pair"), None, None),
        P(("groups", "batch", "pair"), None),
        P(("groups", "batch", "pair"), None, "orb"),
        P(("groups", "batch", "pair"), "orb", None, None),
        P(("groups", "batch", "pair"), None),
        P(("groups", "batch", "pair"), None),
    )
    return jax.shard_map(
        per_device,
        mesh=mesh,
        in_specs=placed,
        out_specs=P(("groups", "batch", "pair"), None),
        check_vma=False,
    )
```

```python
import functools

import jax
import jax.numpy as jnp
from jax import lax
from jax.experimental import pallas as pl
from jax.experimental.pallas import tpu as pltpu
from jax.sharding import PartitionSpec as P

GO = 64
VMEM_LIMIT = 50 * 1024 * 1024
NT = (((1,), (1,)), ((), ()))


def split_dot(left, right, dims=None):
    if dims is None:
        return jnp.dot(left, right, preferred_element_type=jnp.float32)
    return lax.dot_general(left, right, dims, preferred_element_type=jnp.float32)


def prepare_kernel(half_ref, values_ref, left_ref, left_t_ref):
    batches, points, columns = values_ref.shape
    groups = columns // GO
    kept = left_ref.shape[2]
    first = half_ref[0] * (kept // groups)
    at = lax.broadcasted_iota(jnp.int32, (kept, columns), 0)
    lane = lax.broadcasted_iota(jnp.int32, (kept, columns), 1)
    wanted = (at % groups) * GO + first + at // groups
    select = jnp.where(lane == wanted, 1.0, 0.0).astype(jnp.bfloat16)
    for t in range(batches):
        left_ref[t] = split_dot(values_ref[t], select, NT).astype(jnp.bfloat16)
        left_t_ref[t] = split_dot(select, values_ref[t], NT).astype(jnp.bfloat16)


def index_kernel(held, fetch_ref, slots_ref, rows_ref):
    owners, capacity = fetch_ref.shape
    slots = slots_ref[...]
    entries = slots.shape[1]
    owner = slots // capacity
    owner_hot = jnp.where(lax.broadcasted_iota(jnp.int32, (owners, entries), 0) == owner, 1.0, 0.0)
    stored = fetch_ref[...].astype(jnp.float32).T.astype(jnp.bfloat16)
    listed = split_dot(stored, owner_hot.astype(jnp.bfloat16)).astype(jnp.int32)
    at = lax.broadcasted_iota(jnp.int32, (capacity, entries), 0)
    chosen = jnp.where(at == slots - owner * capacity, listed, 0)
    rows_ref[...] = jnp.sum(chosen, axis=0, keepdims=True) + owner * held


def row_table(place_ref, core_ref, own_ref, other_ref, held, owners):
    low = core_ref[0] == 0
    rows = jnp.concatenate(
        [jnp.where(low, own_ref[...], other_ref[...]), jnp.where(low, other_ref[...], own_ref[...])], axis=1
    )
    rows = lax.bitwise_xor(rows, place_ref[0] * held)
    row = lax.broadcasted_iota(jnp.int32, (owners * held, rows.shape[1]), 0)
    return jnp.where(row == rows, 1.0, 0.0)


def density_kernel(places, place_ref, core_ref, *refs):
    piece_refs = refs[:len(places)]
    own_ref, other_ref, left_ref, values_ref, out_ref, table, dense = refs[len(places):]
    batches, points, columns = values_ref.shape
    groups = columns // GO
    owners = sum(len(blocks) for blocks in places)
    held = table.shape[0] // owners
    for ref, blocks in zip(piece_refs, places):
        table[blocks[0] * held:(blocks[-1] + 1) * held, :] = ref[...]
    pick = row_table(place_ref, core_ref, own_ref, other_ref, held, owners).T.astype(jnp.bfloat16)
    low = lax.broadcasted_iota(jnp.int32, (1, 1, 1, groups, 128), 4) < GO
    for chunk in range(table.shape[1] // 256):
        wide = split_dot(pick, table[:, chunk * 256:(chunk + 1) * 256])
        for j in (2 * chunk, 2 * chunk + 1):
            got = wide[:, (j % 2) * 128:(j % 2 + 1) * 128].reshape(2, batches, groups // 4, 2, groups, 128)
            even, odd = got[:, :, :, 0], got[:, :, :, 1]
            first = jnp.where(low, even, pltpu.roll(odd, GO, 4))
            second = jnp.where(low, pltpu.roll(even, GO, 4), odd)
            for t in range(batches):
                for q in range(groups // 2):
                    at = (q // (groups // 4), t, q % (groups // 4))
                    both = jnp.concatenate([first[at], second[at]], axis=0)
                    dense[t, j * 2 * groups:(j + 1) * 2 * groups, q * 128:(q + 1) * 128] = both.astype(jnp.bfloat16)
    at_lane = lax.broadcasted_iota(jnp.int32, (points, 128), 1)
    columns_out = jnp.zeros((points, 128), jnp.float32)
    for t in range(batches):
        product = split_dot(left_ref[t], dense[t]) * values_ref[t].astype(jnp.float32)
        folded = product[:, :128]
        for q in range(1, columns // 128):
            folded = folded + product[:, q * 128:(q + 1) * 128]
        columns_out = jnp.where(at_lane == t, jnp.sum(folded, axis=1, keepdims=True), columns_out)
    out_ref[...] = columns_out.T[:batches]


def scatter_kernel(places, place_ref, core_ref, *refs):
    mine_ref, far_ref, weight_ref, values_ref, left_t_ref, own_ref, other_ref = refs[:7]
    out_refs = refs[7:-2]
    high, rest = refs[-2:]
    target = {k: (ref, i) for ref, blocks in zip(out_refs, places) for i, k in enumerate(blocks)}
    pieces = len(target)
    held = out_refs[0].shape[0] // len(places[0])
    put = row_table(place_ref, core_ref, own_ref, other_ref, held, pieces).astype(jnp.bfloat16)
    batches, points, columns = values_ref.shape
    groups = columns // GO
    kept = left_t_ref.shape[1]
    steps = kept // (2 * groups)
    potential = weight_ref[...] * jnp.tanh(mine_ref[...] + far_ref[...])
    low = lax.broadcasted_iota(jnp.int32, (1, groups, 128), 2) < GO
    upright = jnp.concatenate([potential] * (8 // batches), axis=0).T
    for t in range(batches):
        factor = jnp.broadcast_to(upright[:, t:t + 1], (points, 128))
        factor = jnp.concatenate([factor] * (columns // 128), axis=1)
        weighted = (values_ref[t].astype(jnp.float32) * factor).astype(jnp.bfloat16)
        part = split_dot(left_t_ref[t], weighted)
        for q in range(groups // 2):
            cut = part[:, q * 128:(q + 1) * 128].reshape(steps, 2, groups, 128)
            first, second = cut[:, 0], cut[:, 1]
            even = jnp.where(low, first, pltpu.roll(second, GO, 2))
            odd = jnp.where(low, pltpu.roll(first, GO, 2), second)
            side, pair = q // (groups // 4), q % (groups // 4)
            at = ((side * batches + t) * (groups // 2) + 2 * pair) * groups
            for j in range(steps):
                both = jnp.concatenate([even[j], odd[j]], axis=0)
                top = both.astype(jnp.bfloat16)
                high[at:at + 2 * groups, j * 128:(j + 1) * 128] = top
                rest[at:at + 2 * groups, j * 128:(j + 1) * 128] = (both - top.astype(jnp.float32)).astype(jnp.bfloat16)
    step = max(1, min(pieces, 128 // held))
    for k in range(0, pieces, step):
        some = put[k * held:(k + step) * held, :]
        total = split_dot(some, high[...]) + split_dot(some, rest[...])
        for i in range(step):
            ref, at = target[k + i]
            ref[at * held:(at + 1) * held, :] = total[i * held:(i + 1) * held, :].astype(jnp.bfloat16)


def finish_kernel(half_ref, mine_ref, other_ref, core_ref, out_ref):
    wide = mine_ref.shape[1]
    own = pl.multiple_of(half_ref[0] * wide, wide)
    far = pl.multiple_of((1 - half_ref[0]) * wide, wide)
    out_ref[:, pl.ds(own, wide)] = core_ref[:, pl.ds(own, wide)].astype(jnp.float32) + mine_ref[...]
    out_ref[:, pl.ds(far, wide)] = core_ref[:, pl.ds(far, wide)].astype(jnp.float32) + other_ref[...]


def call(kernel, outs, count, scratch=(), scalars=0, flops=0, moved=0):
    specs = [pl.BlockSpec(memory_space=pltpu.VMEM)] * count
    specs = [pl.BlockSpec(memory_space=pltpu.SMEM)] * scalars + specs
    out_specs = jax.tree.map(lambda _: pl.BlockSpec(memory_space=pltpu.VMEM), outs)
    return pl.pallas_call(
        kernel,
        out_shape=outs,
        in_specs=specs,
        out_specs=out_specs,
        scratch_shapes=list(scratch),
        compiler_params=pltpu.CompilerParams(vmem_limit_bytes=VMEM_LIMIT),
        cost_estimate=pl.CostEstimate(flops=flops, bytes_accessed=moved, transcendentals=0),
    )


def swap(array, axis, count, step):
    return lax.ppermute(array, axis, [(i, i ^ step) for i in range(count)])


def per_device(basis_values, point_weights, slot_ids, fetch_rows, density_blocks, core_blocks):
    rows_z, rows_x = lax.axis_size("batch"), lax.axis_size("pair")
    z, x, half = lax.axis_index("batch"), lax.axis_index("pair"), lax.axis_index("orb")
    owners = rows_z * rows_x
    batches, points, columns = basis_values.shape
    groups, own_groups = slot_ids.shape[1], slot_ids.shape[2]
    held, square = density_blocks.shape
    capacity = fetch_rows.shape[3]
    wide = square // 2
    table_rows = owners * held
    entries = batches * groups * groups
    kept = columns // 2
    bf16, f32 = jnp.bfloat16, jnp.float32

    own_rows = call(
        functools.partial(index_kernel, held),
        jax.ShapeDtypeStruct((1, batches * own_groups * groups), jnp.int32),
        2,
    )(fetch_rows.reshape(owners, capacity), slot_ids.transpose(0, 2, 1).reshape(1, -1))
    other_rows = swap(own_rows, "orb", 2, 1)

    far = list(range(rows_z // 2, rows_z))
    near = list(range(1, rows_z // 2))
    side = list(range(1, rows_x))

    mine = lax.dynamic_slice_in_dim(density_blocks, half * wide, wide, 1)
    direct = {dz: swap(mine, "batch", rows_z, dz) for dz in far}
    beside = [swap(mine, "pair", rows_x, dx) for dx in side]
    *beside, own_rows = lax.optimization_barrier((*beside, own_rows))
    cluster = jnp.concatenate([mine, *beside], axis=0)
    arrays, places = [cluster], [list(range(rows_x))]
    for dz in near:
        arrays.append(swap(cluster, "batch", rows_z, dz))
        places.append(list(range(dz * rows_x, (dz + 1) * rows_x)))
    direct[far[0]], other_rows = lax.optimization_barrier((direct[far[0]], other_rows))
    for dz in far:
        arrays.append(direct[dz])
        places.append([dz * rows_x])
        for dx in side:
            arrays.append(swap(direct[dz], "pair", rows_x, dx))
            places.append([dz * rows_x + dx])

    half_at, _ = lax.optimization_barrier((half.reshape(1).astype(jnp.int32), direct[far[-1]]))
    left, left_t = call(
        prepare_kernel,
        (
            jax.ShapeDtypeStruct((batches, points, kept), bf16),
            jax.ShapeDtypeStruct((batches, kept, points), bf16),
        ),
        1,
        scalars=1,
        flops=4 * batches * points * columns * kept,
        moved=3 * batches * points * columns * 2,
    )(half_at, basis_values)

    place = (z * rows_x + x).reshape(1).astype(jnp.int32)
    core_at = half.reshape(1).astype(jnp.int32)

    partial = call(
        functools.partial(density_kernel, places),
        jax.ShapeDtypeStruct((batches, points), f32),
        len(arrays) + 4,
        scalars=2,
        scratch=(pltpu.VMEM((table_rows, wide), bf16), pltpu.VMEM((batches, kept, columns), bf16)),
        flops=2 * batches * points * columns * kept,
        moved=2 * batches * points * columns * 2,
    )(place, core_at, *arrays, own_rows, other_rows, left, basis_values)
    partial_other = swap(partial, "orb", 2, 1)

    out_places = [list(range(dz * rows_x, (dz + 1) * rows_x)) for dz in [0] + near]
    out_places += [[dz * rows_x + dx] for dz in far for dx in [0] + side]
    sums = call(
        functools.partial(scatter_kernel, out_places),
        [jax.ShapeDtypeStruct((held * len(blocks), wide), bf16) for blocks in out_places],
        7,
        scalars=2,
        scratch=(pltpu.VMEM((entries, wide), bf16), pltpu.VMEM((entries, wide), bf16)),
        flops=2 * batches * points * columns * kept,
        moved=2 * batches * points * columns * 2,
    )(place, core_at, partial, partial_other, point_weights, basis_values, left_t, own_rows, other_rows)

    clusters, singles = sums[:len(near) + 1], sums[len(near) + 1:]
    landed = []
    for i, dz in enumerate(far):
        joined = singles[i * rows_x].astype(f32)
        for dx in side:
            joined = joined + swap(singles[i * rows_x + dx], "pair", rows_x, dx).astype(f32)
        landed.append(swap(joined.astype(bf16), "batch", rows_z, dz).astype(f32))
    cluster = clusters[0].astype(f32)
    for dz, array in zip(near, clusters[1:]):
        cluster = cluster + swap(array, "batch", rows_z, dz).astype(f32)
    total = cluster[:held]
    for dx in side:
        total = total + swap(cluster[dx * held:(dx + 1) * held].astype(bf16), "pair", rows_x, dx).astype(f32)
    for term in landed:
        total = total + term
    total_other = swap(total, "orb", 2, 1)
    return call(
        finish_kernel, jax.ShapeDtypeStruct((held, square), f32), 3, scalars=1, moved=held * square * 12
    )(half_at, total, total_other, core_blocks)


def solution(mesh):
    placed = (
        P(("groups", "batch", "pair"), None, None),
        P(("groups", "batch", "pair"), None),
        P(("groups", "batch", "pair"), None, "orb"),
        P(("groups", "batch", "pair"), "orb", None, None),
        P(("groups", "batch", "pair"), None),
        P(("groups", "batch", "pair"), None),
    )
    return jax.shard_map(
        per_device,
        mesh=mesh,
        in_specs=placed,
        out_specs=P(("groups", "batch", "pair"), None),
        check_vma=False,
    )
```

```python
import functools

import jax
import jax.numpy as jnp
from jax import lax
from jax.experimental import pallas as pl
from jax.experimental.pallas import tpu as pltpu
from jax.sharding import PartitionSpec as P

GO = 64
VMEM_LIMIT = 50 * 1024 * 1024
NT = (((1,), (1,)), ((), ()))


def split_dot(left, right, dims=None):
    if dims is None:
        return jnp.dot(left, right, preferred_element_type=jnp.float32)
    return lax.dot_general(left, right, dims, preferred_element_type=jnp.float32)


def prepare_kernel(half_ref, values_ref, left_ref, left_t_ref):
    batches, points, columns = values_ref.shape
    groups = columns // GO
    kept = left_ref.shape[2]
    first = half_ref[0] * (kept // groups)
    at = lax.broadcasted_iota(jnp.int32, (kept, columns), 0)
    lane = lax.broadcasted_iota(jnp.int32, (kept, columns), 1)
    wanted = (at % groups) * GO + first + at // groups
    select = jnp.where(lane == wanted, 1.0, 0.0).astype(jnp.bfloat16)
    for t in range(batches):
        left_ref[t] = split_dot(values_ref[t], select, NT).astype(jnp.bfloat16)
        left_t_ref[t] = split_dot(select, values_ref[t], NT).astype(jnp.bfloat16)


def index_kernel(held, fetch_ref, slots_ref, rows_ref):
    owners, capacity = fetch_ref.shape
    slots = slots_ref[...]
    entries = slots.shape[1]
    owner = slots // capacity
    owner_hot = jnp.where(lax.broadcasted_iota(jnp.int32, (owners, entries), 0) == owner, 1.0, 0.0)
    stored = fetch_ref[...].astype(jnp.float32).T.astype(jnp.bfloat16)
    listed = split_dot(stored, owner_hot.astype(jnp.bfloat16)).astype(jnp.int32)
    at = lax.broadcasted_iota(jnp.int32, (capacity, entries), 0)
    chosen = jnp.where(at == slots - owner * capacity, listed, 0)
    rows_ref[...] = jnp.sum(chosen, axis=0, keepdims=True) + owner * held


def row_table(place_ref, core_ref, own_ref, other_ref, held, owners):
    low = core_ref[0] == 0
    rows = jnp.concatenate(
        [jnp.where(low, own_ref[...], other_ref[...]), jnp.where(low, other_ref[...], own_ref[...])], axis=1
    )
    rows = lax.bitwise_xor(rows, place_ref[0] * held)
    row = lax.broadcasted_iota(jnp.int32, (owners * held, rows.shape[1]), 0)
    return jnp.where(row == rows, 1.0, 0.0)


def density_kernel(places, place_ref, core_ref, *refs):
    piece_refs = refs[:len(places)]
    own_ref, other_ref, left_ref, values_ref, out_ref, table, dense = refs[len(places):]
    batches, points, columns = values_ref.shape
    groups = columns // GO
    owners = sum(len(blocks) for blocks in places)
    held = table.shape[0] // owners
    for ref, blocks in zip(piece_refs, places):
        table[blocks[0] * held:(blocks[-1] + 1) * held, :] = ref[...]
    pick = row_table(place_ref, core_ref, own_ref, other_ref, held, owners).T.astype(jnp.bfloat16)
    low = lax.broadcasted_iota(jnp.int32, (1, 1, 1, groups, 128), 4) < GO
    for chunk in range(table.shape[1] // 512):
        wide = split_dot(pick, table[:, chunk * 512:(chunk + 1) * 512])
        for j in range(4 * chunk, 4 * chunk + 4):
            got = wide[:, (j % 4) * 128:(j % 4 + 1) * 128].reshape(2, batches, groups // 4, 2, groups, 128)
            even, odd = got[:, :, :, 0], got[:, :, :, 1]
            first = jnp.where(low, even, pltpu.roll(odd, GO, 4))
            second = jnp.where(low, pltpu.roll(even, GO, 4), odd)
            for t in range(batches):
                for q in range(groups // 2):
                    at = (q // (groups // 4), t, q % (groups // 4))
                    both = jnp.concatenate([first[at], second[at]], axis=0)
                    dense[t, j * 2 * groups:(j + 1) * 2 * groups, q * 128:(q + 1) * 128] = both.astype(jnp.bfloat16)
    for t in range(batches):
        product = split_dot(left_ref[t], dense[t]) * values_ref[t].astype(jnp.float32)
        folded = product[:, :128]
        for q in range(1, columns // 128):
            folded = folded + product[:, q * 128:(q + 1) * 128]
        out_ref[t:t + 1, :] = jnp.sum(folded.T, axis=0, keepdims=True)


def scatter_kernel(places, place_ref, core_ref, *refs):
    mine_ref, far_ref, weight_ref, values_ref, left_t_ref, own_ref, other_ref = refs[:7]
    out_refs = refs[7:-1]
    terms = refs[-1]
    target = {k: (ref, i) for ref, blocks in zip(out_refs, places) for i, k in enumerate(blocks)}
    pieces = len(target)
    held = out_refs[0].shape[0] // len(places[0])
    put = row_table(place_ref, core_ref, own_ref, other_ref, held, pieces).astype(jnp.bfloat16)
    batches, points, columns = values_ref.shape
    groups = columns // GO
    kept = left_t_ref.shape[1]
    steps = kept // (2 * groups)
    entries = batches * groups * groups
    potential = weight_ref[...] * jnp.tanh(mine_ref[...] + far_ref[...])
    low = lax.broadcasted_iota(jnp.int32, (1, groups, 128), 2) < GO
    for t in range(batches):
        factor = jnp.broadcast_to(potential[t:t + 1, :], (128, points)).T
        factor = jnp.concatenate([factor] * (columns // 128), axis=1)
        weighted = (values_ref[t].astype(jnp.float32) * factor).astype(jnp.bfloat16)
        part = split_dot(left_t_ref[t], weighted)
        for q in range(groups // 2):
            cut = part[:, q * 128:(q + 1) * 128].reshape(steps, 2, groups, 128)
            first, second = cut[:, 0], cut[:, 1]
            even = jnp.where(low, first, pltpu.roll(second, GO, 2))
            odd = jnp.where(low, pltpu.roll(first, GO, 2), second)
            side, pair = q // (groups // 4), q % (groups // 4)
            at = ((side * batches + t) * (groups // 2) + 2 * pair) * groups
            for j in range(steps):
                both = jnp.concatenate([even[j], odd[j]], axis=0)
                top = both.astype(jnp.bfloat16)
                terms[at:at + 2 * groups, j * 128:(j + 1) * 128] = top
                left = (both - top.astype(jnp.float32)).astype(jnp.bfloat16)
                terms[entries + at:entries + at + 2 * groups, j * 128:(j + 1) * 128] = left
    put = jnp.concatenate([put, put], axis=1)
    step = max(1, min(pieces, 128 // held))
    for k in range(0, pieces, step):
        some = put[k * held:(k + step) * held, :]
        total = split_dot(some, terms[...])
        for i in range(step):
            ref, at = target[k + i]
            ref[at * held:(at + 1) * held, :] = total[i * held:(i + 1) * held, :].astype(jnp.bfloat16)


def finish_kernel(half_ref, mine_ref, other_ref, core_ref, out_ref):
    wide = mine_ref.shape[1]
    own = pl.multiple_of(half_ref[0] * wide, wide)
    far = pl.multiple_of((1 - half_ref[0]) * wide, wide)
    out_ref[:, pl.ds(own, wide)] = core_ref[:, pl.ds(own, wide)].astype(jnp.float32) + mine_ref[...]
    out_ref[:, pl.ds(far, wide)] = core_ref[:, pl.ds(far, wide)].astype(jnp.float32) + other_ref[...]


def call(kernel, outs, count, scratch=(), scalars=0, flops=0, moved=0):
    specs = [pl.BlockSpec(memory_space=pltpu.VMEM)] * count
    specs = [pl.BlockSpec(memory_space=pltpu.SMEM)] * scalars + specs
    out_specs = jax.tree.map(lambda _: pl.BlockSpec(memory_space=pltpu.VMEM), outs)
    return pl.pallas_call(
        kernel,
        out_shape=outs,
        in_specs=specs,
        out_specs=out_specs,
        scratch_shapes=list(scratch),
        compiler_params=pltpu.CompilerParams(vmem_limit_bytes=VMEM_LIMIT),
        cost_estimate=pl.CostEstimate(flops=flops, bytes_accessed=moved, transcendentals=0),
    )


def swap(array, axis, count, step):
    return lax.ppermute(array, axis, [(i, i ^ step) for i in range(count)])


def per_device(basis_values, point_weights, slot_ids, fetch_rows, density_blocks, core_blocks):
    rows_z, rows_x = lax.axis_size("batch"), lax.axis_size("pair")
    z, x, half = lax.axis_index("batch"), lax.axis_index("pair"), lax.axis_index("orb")
    owners = rows_z * rows_x
    batches, points, columns = basis_values.shape
    groups, own_groups = slot_ids.shape[1], slot_ids.shape[2]
    held, square = density_blocks.shape
    capacity = fetch_rows.shape[3]
    wide = square // 2
    table_rows = owners * held
    entries = batches * groups * groups
    kept = columns // 2
    bf16, f32 = jnp.bfloat16, jnp.float32

    own_rows = call(
        functools.partial(index_kernel, held),
        jax.ShapeDtypeStruct((1, batches * own_groups * groups), jnp.int32),
        2,
    )(fetch_rows.reshape(owners, capacity), slot_ids.transpose(0, 2, 1).reshape(1, -1))
    other_rows = swap(own_rows, "orb", 2, 1)

    far = list(range(rows_z // 2, rows_z))
    near = list(range(1, rows_z // 2))
    side = list(range(1, rows_x))

    mine = lax.dynamic_slice_in_dim(density_blocks, half * wide, wide, 1)
    direct = {dz: swap(mine, "batch", rows_z, dz) for dz in far}
    beside = [swap(mine, "pair", rows_x, dx) for dx in side]
    *beside, own_rows = lax.optimization_barrier((*beside, own_rows))
    cluster = jnp.concatenate([mine, *beside], axis=0)
    arrays, places = [cluster], [list(range(rows_x))]
    for dz in near:
        arrays.append(swap(cluster, "batch", rows_z, dz))
        places.append(list(range(dz * rows_x, (dz + 1) * rows_x)))
    direct[far[0]], other_rows = lax.optimization_barrier((direct[far[0]], other_rows))
    for dz in far:
        arrays.append(direct[dz])
        places.append([dz * rows_x])
        for dx in side:
            arrays.append(swap(direct[dz], "pair", rows_x, dx))
            places.append([dz * rows_x + dx])

    half_at, _ = lax.optimization_barrier((half.reshape(1).astype(jnp.int32), direct[far[-1]]))
    left, left_t = call(
        prepare_kernel,
        (
            jax.ShapeDtypeStruct((batches, points, kept), bf16),
            jax.ShapeDtypeStruct((batches, kept, points), bf16),
        ),
        1,
        scalars=1,
        flops=4 * batches * points * columns * kept,
        moved=3 * batches * points * columns * 2,
    )(half_at, basis_values)

    place = (z * rows_x + x).reshape(1).astype(jnp.int32)
    core_at = half.reshape(1).astype(jnp.int32)

    partial = call(
        functools.partial(density_kernel, places),
        jax.ShapeDtypeStruct((batches, points), f32),
        len(arrays) + 4,
        scalars=2,
        scratch=(pltpu.VMEM((table_rows, wide), bf16), pltpu.VMEM((batches, kept, columns), bf16)),
        flops=2 * batches * points * columns * kept,
        moved=2 * batches * points * columns * 2,
    )(place, core_at, *arrays, own_rows, other_rows, left, basis_values)
    partial_other = swap(partial, "orb", 2, 1)

    out_places = [list(range(dz * rows_x, (dz + 1) * rows_x)) for dz in [0] + near]
    out_places += [[dz * rows_x + dx] for dz in far for dx in [0] + side]
    sums = call(
        functools.partial(scatter_kernel, out_places),
        [jax.ShapeDtypeStruct((held * len(blocks), wide), bf16) for blocks in out_places],
        7,
        scalars=2,
        scratch=(pltpu.VMEM((2 * entries, wide), bf16),),
        flops=2 * batches * points * columns * kept,
        moved=2 * batches * points * columns * 2,
    )(place, core_at, partial, partial_other, point_weights, basis_values, left_t, own_rows, other_rows)

    clusters, singles = sums[:len(near) + 1], sums[len(near) + 1:]
    landed = []
    for i, dz in enumerate(far):
        joined = singles[i * rows_x].astype(f32)
        for dx in side:
            joined = joined + swap(singles[i * rows_x + dx], "pair", rows_x, dx).astype(f32)
        landed.append(swap(joined.astype(bf16), "batch", rows_z, dz).astype(f32))
    cluster = clusters[0].astype(f32)
    for dz, array in zip(near, clusters[1:]):
        cluster = cluster + swap(array, "batch", rows_z, dz).astype(f32)
    total = cluster[:held]
    for dx in side:
        total = total + swap(cluster[dx * held:(dx + 1) * held].astype(bf16), "pair", rows_x, dx).astype(f32)
    for term in landed:
        total = total + term
    total_other = swap(total, "orb", 2, 1)
    return call(
        finish_kernel, jax.ShapeDtypeStruct((held, square), f32), 3, scalars=1, moved=held * square * 12
    )(half_at, total, total_other, core_blocks)


def solution(mesh):
    placed = (
        P(("groups", "batch", "pair"), None, None),
        P(("groups", "batch", "pair"), None),
        P(("groups", "batch", "pair"), None, "orb"),
        P(("groups", "batch", "pair"), "orb", None, None),
        P(("groups", "batch", "pair"), None),
        P(("groups", "batch", "pair"), None),
    )
    return jax.shard_map(
        per_device,
        mesh=mesh,
        in_specs=placed,
        out_specs=P(("groups", "batch", "pair"), None),
        check_vma=False,
    )
```

```python
import functools

import jax
import jax.numpy as jnp
from jax import lax
from jax.experimental import pallas as pl
from jax.experimental.pallas import tpu as pltpu
from jax.sharding import PartitionSpec as P

GO = 64
VMEM_LIMIT = 50 * 1024 * 1024
NT = (((1,), (1,)), ((), ()))


def split_dot(left, right, dims=None):
    if dims is None:
        return jnp.dot(left, right, preferred_element_type=jnp.float32)
    return lax.dot_general(left, right, dims, preferred_element_type=jnp.float32)


def prepare_kernel(place_ref, half_ref, values_ref, own_ref, other_ref, left_ref, left_t_ref, pick_ref, put_ref):
    batches, points, columns = values_ref.shape
    groups = columns // GO
    kept = left_ref.shape[2]
    first = half_ref[0] * (kept // groups)
    at = lax.broadcasted_iota(jnp.int32, (kept, columns), 0)
    lane = lax.broadcasted_iota(jnp.int32, (kept, columns), 1)
    wanted = (at % groups) * GO + first + at // groups
    select = jnp.where(lane == wanted, 1.0, 0.0).astype(jnp.bfloat16)
    for t in range(batches):
        left_ref[t] = split_dot(values_ref[t], select, NT).astype(jnp.bfloat16)
        left_t_ref[t] = split_dot(select, values_ref[t], NT).astype(jnp.bfloat16)
    hot = row_table(place_ref, half_ref, own_ref, other_ref, put_ref.shape[0])
    pick_ref[...] = hot.T.astype(jnp.bfloat16)
    hot = hot.astype(jnp.bfloat16)
    put_ref[...] = jnp.concatenate([hot, hot], axis=1)


def index_kernel(held, fetch_ref, slots_ref, rows_ref):
    owners, capacity = fetch_ref.shape
    slots = slots_ref[...]
    entries = slots.shape[1]
    owner = slots // capacity
    owner_hot = jnp.where(lax.broadcasted_iota(jnp.int32, (owners, entries), 0) == owner, 1.0, 0.0)
    stored = fetch_ref[...].astype(jnp.float32).T.astype(jnp.bfloat16)
    listed = split_dot(stored, owner_hot.astype(jnp.bfloat16)).astype(jnp.int32)
    at = lax.broadcasted_iota(jnp.int32, (capacity, entries), 0)
    chosen = jnp.where(at == slots - owner * capacity, listed, 0)
    rows_ref[...] = jnp.sum(chosen, axis=0, keepdims=True) + owner * held


def row_table(place_ref, core_ref, own_ref, other_ref, table_rows):
    low = core_ref[0] == 0
    rows = jnp.concatenate(
        [jnp.where(low, own_ref[...], other_ref[...]), jnp.where(low, other_ref[...], own_ref[...])], axis=1
    )
    rows = lax.bitwise_xor(rows, place_ref[0])
    row = lax.broadcasted_iota(jnp.int32, (table_rows, rows.shape[1]), 0)
    return jnp.where(row == rows, 1.0, 0.0)


def density_kernel(places, *refs):
    piece_refs = refs[:len(places)]
    pick_ref, left_ref, values_ref, out_ref, table, dense = refs[len(places):]
    batches, points, columns = values_ref.shape
    groups = columns // GO
    owners = sum(len(blocks) for blocks in places)
    held = table.shape[0] // owners
    for ref, blocks in zip(piece_refs, places):
        table[blocks[0] * held:(blocks[-1] + 1) * held, :] = ref[...]
    pick = pick_ref[...]
    low = lax.broadcasted_iota(jnp.int32, (1, 1, 1, groups, 128), 4) < GO
    for chunk in range(table.shape[1] // 512):
        wide = split_dot(pick, table[:, chunk * 512:(chunk + 1) * 512])
        for j in range(4 * chunk, 4 * chunk + 4):
            got = wide[:, (j % 4) * 128:(j % 4 + 1) * 128].reshape(2, batches, groups // 4, 2, groups, 128)
            even, odd = got[:, :, :, 0], got[:, :, :, 1]
            first = jnp.where(low, even, pltpu.roll(odd, GO, 4))
            second = jnp.where(low, pltpu.roll(even, GO, 4), odd)
            for t in range(batches):
                for q in range(groups // 2):
                    at = (q // (groups // 4), t, q % (groups // 4))
                    both = jnp.concatenate([first[at], second[at]], axis=0)
                    dense[t, j * 2 * groups:(j + 1) * 2 * groups, q * 128:(q + 1) * 128] = both.astype(jnp.bfloat16)
    for t in range(batches):
        product = split_dot(left_ref[t], dense[t]) * values_ref[t].astype(jnp.float32)
        folded = product[:, :128]
        for q in range(1, columns // 128):
            folded = folded + product[:, q * 128:(q + 1) * 128]
        out_ref[t:t + 1, :] = jnp.sum(folded.T, axis=0, keepdims=True)


def scatter_kernel(places, *refs):
    mine_ref, far_ref, weight_ref, values_ref, left_t_ref, put_ref = refs[:6]
    out_refs = refs[6:-1]
    terms = refs[-1]
    target = {k: (ref, i) for ref, blocks in zip(out_refs, places) for i, k in enumerate(blocks)}
    pieces = len(target)
    held = out_refs[0].shape[0] // len(places[0])
    batches, points, columns = values_ref.shape
    groups = columns // GO
    kept = left_t_ref.shape[1]
    steps = kept // (2 * groups)
    entries = batches * groups * groups
    potential = weight_ref[...] * jnp.tanh(mine_ref[...] + far_ref[...])
    low = lax.broadcasted_iota(jnp.int32, (1, groups, 128), 2) < GO
    for t in range(batches):
        factor = jnp.broadcast_to(potential[t:t + 1, :], (128, points)).T
        factor = jnp.concatenate([factor] * (columns // 128), axis=1)
        weighted = (values_ref[t].astype(jnp.float32) * factor).astype(jnp.bfloat16)
        part = split_dot(left_t_ref[t], weighted)
        for q in range(groups // 2):
            cut = part[:, q * 128:(q + 1) * 128].reshape(steps, 2, groups, 128)
            first, second = cut[:, 0], cut[:, 1]
            even = jnp.where(low, first, pltpu.roll(second, GO, 2))
            odd = jnp.where(low, pltpu.roll(first, GO, 2), second)
            side, pair = q // (groups // 4), q % (groups // 4)
            at = ((side * batches + t) * (groups // 2) + 2 * pair) * groups
            for j in range(steps):
                both = jnp.concatenate([even[j], odd[j]], axis=0)
                top = both.astype(jnp.bfloat16)
                terms[at:at + 2 * groups, j * 128:(j + 1) * 128] = top
                left = (both - top.astype(jnp.float32)).astype(jnp.bfloat16)
                terms[entries + at:entries + at + 2 * groups, j * 128:(j + 1) * 128] = left
    step = max(1, min(pieces, 128 // held))
    for k in range(0, pieces, step):
        some = put_ref[k * held:(k + step) * held, :]
        total = split_dot(some, terms[...])
        for i in range(step):
            ref, at = target[k + i]
            ref[at * held:(at + 1) * held, :] = total[i * held:(i + 1) * held, :].astype(jnp.bfloat16)


def finish_kernel(half_ref, mine_ref, other_ref, core_ref, out_ref):
    wide = mine_ref.shape[1]
    own = pl.multiple_of(half_ref[0] * wide, wide)
    far = pl.multiple_of((1 - half_ref[0]) * wide, wide)
    out_ref[:, pl.ds(own, wide)] = core_ref[:, pl.ds(own, wide)].astype(jnp.float32) + mine_ref[...]
    out_ref[:, pl.ds(far, wide)] = core_ref[:, pl.ds(far, wide)].astype(jnp.float32) + other_ref[...]


def call(kernel, outs, count, scratch=(), scalars=0, flops=0, moved=0):
    specs = [pl.BlockSpec(memory_space=pltpu.VMEM)] * count
    specs = [pl.BlockSpec(memory_space=pltpu.SMEM)] * scalars + specs
    out_specs = jax.tree.map(lambda _: pl.BlockSpec(memory_space=pltpu.VMEM), outs)
    return pl.pallas_call(
        kernel,
        out_shape=outs,
        in_specs=specs,
        out_specs=out_specs,
        scratch_shapes=list(scratch),
        compiler_params=pltpu.CompilerParams(vmem_limit_bytes=VMEM_LIMIT),
        cost_estimate=pl.CostEstimate(flops=flops, bytes_accessed=moved, transcendentals=0),
    )


def swap(array, axis, count, step):
    return lax.ppermute(array, axis, [(i, i ^ step) for i in range(count)])


def per_device(basis_values, point_weights, slot_ids, fetch_rows, density_blocks, core_blocks):
    rows_z, rows_x = lax.axis_size("batch"), lax.axis_size("pair")
    z, x, half = lax.axis_index("batch"), lax.axis_index("pair"), lax.axis_index("orb")
    owners = rows_z * rows_x
    batches, points, columns = basis_values.shape
    groups, own_groups = slot_ids.shape[1], slot_ids.shape[2]
    held, square = density_blocks.shape
    capacity = fetch_rows.shape[3]
    wide = square // 2
    table_rows = owners * held
    entries = batches * groups * groups
    kept = columns // 2
    bf16, f32 = jnp.bfloat16, jnp.float32

    own_rows = call(
        functools.partial(index_kernel, held),
        jax.ShapeDtypeStruct((1, batches * own_groups * groups), jnp.int32),
        2,
    )(fetch_rows.reshape(owners, capacity), slot_ids.transpose(0, 2, 1).reshape(1, -1))
    other_rows = swap(own_rows, "orb", 2, 1)

    far = list(range(rows_z // 2, rows_z))
    near = list(range(1, rows_z // 2))
    side = list(range(1, rows_x))

    mine = lax.dynamic_slice_in_dim(density_blocks, half * wide, wide, 1)
    direct = {dz: swap(mine, "batch", rows_z, dz) for dz in far}
    beside = [swap(mine, "pair", rows_x, dx) for dx in side]
    *beside, own_rows = lax.optimization_barrier((*beside, own_rows))
    cluster = jnp.concatenate([mine, *beside], axis=0)
    arrays, places = [cluster], [list(range(rows_x))]
    for dz in near:
        arrays.append(swap(cluster, "batch", rows_z, dz))
        places.append(list(range(dz * rows_x, (dz + 1) * rows_x)))
    direct[far[0]], other_rows = lax.optimization_barrier((direct[far[0]], other_rows))
    for dz in far:
        arrays.append(direct[dz])
        places.append([dz * rows_x])
        for dx in side:
            arrays.append(swap(direct[dz], "pair", rows_x, dx))
            places.append([dz * rows_x + dx])

    half_at, _ = lax.optimization_barrier((half.reshape(1).astype(jnp.int32), direct[far[-1]]))
    place = ((z * rows_x + x) * held).reshape(1).astype(jnp.int32)
    left, left_t, pick, put = call(
        prepare_kernel,
        (
            jax.ShapeDtypeStruct((batches, points, kept), bf16),
            jax.ShapeDtypeStruct((batches, kept, points), bf16),
            jax.ShapeDtypeStruct((entries, table_rows), bf16),
            jax.ShapeDtypeStruct((table_rows, 2 * entries), bf16),
        ),
        3,
        scalars=2,
        flops=4 * batches * points * columns * kept,
        moved=3 * batches * points * columns * 2,
    )(place, half_at, basis_values, own_rows, other_rows)


    partial = call(
        functools.partial(density_kernel, places),
        jax.ShapeDtypeStruct((batches, points), f32),
        len(arrays) + 3,
        scratch=(pltpu.VMEM((table_rows, wide), bf16), pltpu.VMEM((batches, kept, columns), bf16)),
        flops=2 * batches * points * columns * kept,
        moved=2 * batches * points * columns * 2,
    )(*arrays, pick, left, basis_values)
    partial_other = swap(partial, "orb", 2, 1)

    out_places = [list(range(dz * rows_x, (dz + 1) * rows_x)) for dz in [0] + near]
    out_places += [[dz * rows_x + dx] for dz in far for dx in [0] + side]
    sums = call(
        functools.partial(scatter_kernel, out_places),
        [jax.ShapeDtypeStruct((held * len(blocks), wide), bf16) for blocks in out_places],
        6,
        scratch=(pltpu.VMEM((2 * entries, wide), bf16),),
        flops=2 * batches * points * columns * kept,
        moved=2 * batches * points * columns * 2,
    )(partial, partial_other, point_weights, basis_values, left_t, put)

    clusters, singles = sums[:len(near) + 1], sums[len(near) + 1:]
    landed = []
    for i, dz in enumerate(far):
        joined = singles[i * rows_x].astype(f32)
        for dx in side:
            joined = joined + swap(singles[i * rows_x + dx], "pair", rows_x, dx).astype(f32)
        landed.append(swap(joined.astype(bf16), "batch", rows_z, dz).astype(f32))
    cluster = clusters[0].astype(f32)
    for dz, array in zip(near, clusters[1:]):
        cluster = cluster + swap(array, "batch", rows_z, dz).astype(f32)
    total = cluster[:held]
    for dx in side:
        total = total + swap(cluster[dx * held:(dx + 1) * held].astype(bf16), "pair", rows_x, dx).astype(f32)
    for term in landed:
        total = total + term
    total_other = swap(total, "orb", 2, 1)
    return call(
        finish_kernel, jax.ShapeDtypeStruct((held, square), f32), 3, scalars=1, moved=held * square * 12
    )(half_at, total, total_other, core_blocks)


def solution(mesh):
    placed = (
        P(("groups", "batch", "pair"), None, None),
        P(("groups", "batch", "pair"), None),
        P(("groups", "batch", "pair"), None, "orb"),
        P(("groups", "batch", "pair"), "orb", None, None),
        P(("groups", "batch", "pair"), None),
        P(("groups", "batch", "pair"), None),
    )
    return jax.shard_map(
        per_device,
        mesh=mesh,
        in_specs=placed,
        out_specs=P(("groups", "batch", "pair"), None),
        check_vma=False,
    )
```

```python
import functools

import jax
import jax.numpy as jnp
from jax import lax
from jax.experimental import pallas as pl
from jax.experimental.pallas import tpu as pltpu
from jax.sharding import PartitionSpec as P

GO = 64
VMEM_LIMIT = 50 * 1024 * 1024
NT = (((1,), (1,)), ((), ()))


def split_dot(left, right, dims=None):
    if dims is None:
        return jnp.dot(left, right, preferred_element_type=jnp.float32)
    return lax.dot_general(left, right, dims, preferred_element_type=jnp.float32)


def prepare_kernel(place_ref, half_ref, values_ref, own_ref, other_ref, left_ref, left_t_ref, pick_ref, put_ref):
    batches, points, columns = values_ref.shape
    groups = columns // GO
    kept = left_ref.shape[2]
    first = half_ref[0] * (kept // groups)
    at = lax.broadcasted_iota(jnp.int32, (kept, columns), 0)
    lane = lax.broadcasted_iota(jnp.int32, (kept, columns), 1)
    wanted = (at % groups) * GO + first + at // groups
    select = jnp.where(lane == wanted, 1.0, 0.0).astype(jnp.bfloat16)
    for t in range(batches):
        left_ref[t] = split_dot(values_ref[t], select, NT).astype(jnp.bfloat16)
        left_t_ref[t] = split_dot(select, values_ref[t], NT).astype(jnp.bfloat16)
    hot = row_table(place_ref, half_ref, own_ref, other_ref, put_ref.shape[0])
    pick_ref[...] = hot.T.astype(jnp.bfloat16)
    hot = hot.astype(jnp.bfloat16)
    put_ref[...] = jnp.concatenate([hot, hot], axis=1)


def index_kernel(held, fetch_ref, slots_ref, rows_ref):
    owners, capacity = fetch_ref.shape
    slots = slots_ref[...]
    entries = slots.shape[1]
    owner = slots // capacity
    owner_hot = jnp.where(lax.broadcasted_iota(jnp.int32, (owners, entries), 0) == owner, 1.0, 0.0)
    stored = fetch_ref[...].astype(jnp.float32).T.astype(jnp.bfloat16)
    listed = split_dot(stored, owner_hot.astype(jnp.bfloat16)).astype(jnp.int32)
    at = lax.broadcasted_iota(jnp.int32, (capacity, entries), 0)
    chosen = jnp.where(at == slots - owner * capacity, listed, 0)
    rows_ref[...] = jnp.sum(chosen, axis=0, keepdims=True) + owner * held


def row_table(place_ref, core_ref, own_ref, other_ref, table_rows):
    low = core_ref[0] == 0
    rows = jnp.concatenate(
        [jnp.where(low, own_ref[...], other_ref[...]), jnp.where(low, other_ref[...], own_ref[...])], axis=1
    )
    rows = lax.bitwise_xor(rows, place_ref[0])
    row = lax.broadcasted_iota(jnp.int32, (table_rows, rows.shape[1]), 0)
    return jnp.where(row == rows, 1.0, 0.0)


def density_kernel(places, *refs):
    piece_refs = refs[:len(places)]
    pick_ref, left_ref, values_ref, out_ref, dense = refs[len(places):]
    batches, points, columns = values_ref.shape
    groups = columns // GO
    assert [k for blocks in places for k in blocks] == list(range(sum(len(blocks) for blocks in places)))
    pick = pick_ref[...]
    low = lax.broadcasted_iota(jnp.int32, (1, 1, 1, groups, 128), 4) < GO
    for chunk in range(piece_refs[0].shape[1] // 512):
        table = jnp.concatenate([ref[:, chunk * 512:(chunk + 1) * 512] for ref in piece_refs], axis=0)
        wide = split_dot(pick, table)
        for j in range(4 * chunk, 4 * chunk + 4):
            got = wide[:, (j % 4) * 128:(j % 4 + 1) * 128].reshape(2, batches, groups // 4, 2, groups, 128)
            even, odd = got[:, :, :, 0], got[:, :, :, 1]
            first = jnp.where(low, even, pltpu.roll(odd, GO, 4))
            second = jnp.where(low, pltpu.roll(even, GO, 4), odd)
            for t in range(batches):
                for q in range(groups // 2):
                    at = (q // (groups // 4), t, q % (groups // 4))
                    both = jnp.concatenate([first[at], second[at]], axis=0)
                    dense[t, j * 2 * groups:(j + 1) * 2 * groups, q * 128:(q + 1) * 128] = both.astype(jnp.bfloat16)
    for t in range(batches):
        product = split_dot(left_ref[t], dense[t]) * values_ref[t].astype(jnp.float32)
        folded = product[:, :128]
        for q in range(1, columns // 128):
            folded = folded + product[:, q * 128:(q + 1) * 128]
        out_ref[t:t + 1, :] = jnp.sum(folded.T, axis=0, keepdims=True)


def scatter_kernel(places, *refs):
    mine_ref, far_ref, weight_ref, values_ref, left_t_ref, put_ref = refs[:6]
    out_refs = refs[6:-1]
    terms = refs[-1]
    target = {k: (ref, i) for ref, blocks in zip(out_refs, places) for i, k in enumerate(blocks)}
    pieces = len(target)
    held = out_refs[0].shape[0] // len(places[0])
    batches, points, columns = values_ref.shape
    groups = columns // GO
    kept = left_t_ref.shape[1]
    steps = kept // (2 * groups)
    entries = batches * groups * groups
    potential = weight_ref[...] * jnp.tanh(mine_ref[...] + far_ref[...])
    low = lax.broadcasted_iota(jnp.int32, (1, groups, 128), 2) < GO
    for t in range(batches):
        factor = jnp.broadcast_to(potential[t:t + 1, :], (128, points)).T
        factor = jnp.concatenate([factor] * (columns // 128), axis=1)
        weighted = (values_ref[t].astype(jnp.float32) * factor).astype(jnp.bfloat16)
        part = split_dot(left_t_ref[t], weighted)
        for q in range(groups // 2):
            cut = part[:, q * 128:(q + 1) * 128].reshape(steps, 2, groups, 128)
            first, second = cut[:, 0], cut[:, 1]
            even = jnp.where(low, first, pltpu.roll(second, GO, 2))
            odd = jnp.where(low, pltpu.roll(first, GO, 2), second)
            side, pair = q // (groups // 4), q % (groups // 4)
            at = ((side * batches + t) * (groups // 2) + 2 * pair) * groups
            for j in range(steps):
                both = jnp.concatenate([even[j], odd[j]], axis=0)
                top = both.astype(jnp.bfloat16)
                terms[at:at + 2 * groups, j * 128:(j + 1) * 128] = top
                left = (both - top.astype(jnp.float32)).astype(jnp.bfloat16)
                terms[entries + at:entries + at + 2 * groups, j * 128:(j + 1) * 128] = left
    step = max(1, min(pieces, 128 // held))
    for k in range(0, pieces, step):
        some = put_ref[k * held:(k + step) * held, :]
        total = split_dot(some, terms[...])
        for i in range(step):
            ref, at = target[k + i]
            ref[at * held:(at + 1) * held, :] = total[i * held:(i + 1) * held, :].astype(jnp.bfloat16)


def finish_kernel(half_ref, mine_ref, other_ref, core_ref, out_ref):
    wide = mine_ref.shape[1]
    own = pl.multiple_of(half_ref[0] * wide, wide)
    far = pl.multiple_of((1 - half_ref[0]) * wide, wide)
    out_ref[:, pl.ds(own, wide)] = core_ref[:, pl.ds(own, wide)].astype(jnp.float32) + mine_ref[...]
    out_ref[:, pl.ds(far, wide)] = core_ref[:, pl.ds(far, wide)].astype(jnp.float32) + other_ref[...]


def call(kernel, outs, count, scratch=(), scalars=0, flops=0, moved=0):
    specs = [pl.BlockSpec(memory_space=pltpu.VMEM)] * count
    specs = [pl.BlockSpec(memory_space=pltpu.SMEM)] * scalars + specs
    out_specs = jax.tree.map(lambda _: pl.BlockSpec(memory_space=pltpu.VMEM), outs)
    return pl.pallas_call(
        kernel,
        out_shape=outs,
        in_specs=specs,
        out_specs=out_specs,
        scratch_shapes=list(scratch),
        compiler_params=pltpu.CompilerParams(vmem_limit_bytes=VMEM_LIMIT),
        cost_estimate=pl.CostEstimate(flops=flops, bytes_accessed=moved, transcendentals=0),
    )


def swap(array, axis, count, step):
    return lax.ppermute(array, axis, [(i, i ^ step) for i in range(count)])


def per_device(basis_values, point_weights, slot_ids, fetch_rows, density_blocks, core_blocks):
    rows_z, rows_x = lax.axis_size("batch"), lax.axis_size("pair")
    z, x, half = lax.axis_index("batch"), lax.axis_index("pair"), lax.axis_index("orb")
    owners = rows_z * rows_x
    batches, points, columns = basis_values.shape
    groups, own_groups = slot_ids.shape[1], slot_ids.shape[2]
    held, square = density_blocks.shape
    capacity = fetch_rows.shape[3]
    wide = square // 2
    table_rows = owners * held
    entries = batches * groups * groups
    kept = columns // 2
    bf16, f32 = jnp.bfloat16, jnp.float32

    own_rows = call(
        functools.partial(index_kernel, held),
        jax.ShapeDtypeStruct((1, batches * own_groups * groups), jnp.int32),
        2,
    )(fetch_rows.reshape(owners, capacity), slot_ids.transpose(0, 2, 1).reshape(1, -1))
    other_rows = swap(own_rows, "orb", 2, 1)

    far = list(range(rows_z // 2, rows_z))
    near = list(range(1, rows_z // 2))
    side = list(range(1, rows_x))

    mine = lax.dynamic_slice_in_dim(density_blocks, half * wide, wide, 1)
    direct = {dz: swap(mine, "batch", rows_z, dz) for dz in far}
    beside = [swap(mine, "pair", rows_x, dx) for dx in side]
    *beside, own_rows = lax.optimization_barrier((*beside, own_rows))
    cluster = jnp.concatenate([mine, *beside], axis=0)
    arrays, places = [cluster], [list(range(rows_x))]
    for dz in near:
        arrays.append(swap(cluster, "batch", rows_z, dz))
        places.append(list(range(dz * rows_x, (dz + 1) * rows_x)))
    direct[far[0]], other_rows = lax.optimization_barrier((direct[far[0]], other_rows))
    for dz in far:
        arrays.append(direct[dz])
        places.append([dz * rows_x])
        for dx in side:
            arrays.append(swap(direct[dz], "pair", rows_x, dx))
            places.append([dz * rows_x + dx])

    half_at, _ = lax.optimization_barrier((half.reshape(1).astype(jnp.int32), direct[far[-1]]))
    place = ((z * rows_x + x) * held).reshape(1).astype(jnp.int32)
    left, left_t, pick, put = call(
        prepare_kernel,
        (
            jax.ShapeDtypeStruct((batches, points, kept), bf16),
            jax.ShapeDtypeStruct((batches, kept, points), bf16),
            jax.ShapeDtypeStruct((entries, table_rows), bf16),
            jax.ShapeDtypeStruct((table_rows, 2 * entries), bf16),
        ),
        3,
        scalars=2,
        flops=4 * batches * points * columns * kept,
        moved=3 * batches * points * columns * 2,
    )(place, half_at, basis_values, own_rows, other_rows)


    partial = call(
        functools.partial(density_kernel, places),
        jax.ShapeDtypeStruct((batches, points), f32),
        len(arrays) + 3,
        scratch=(pltpu.VMEM((batches, kept, columns), bf16),),
        flops=2 * batches * points * columns * kept,
        moved=2 * batches * points * columns * 2,
    )(*arrays, pick, left, basis_values)
    partial_other = swap(partial, "orb", 2, 1)

    out_places = [list(range(dz * rows_x, (dz + 1) * rows_x)) for dz in [0] + near]
    out_places += [[dz * rows_x + dx] for dz in far for dx in [0] + side]
    sums = call(
        functools.partial(scatter_kernel, out_places),
        [jax.ShapeDtypeStruct((held * len(blocks), wide), bf16) for blocks in out_places],
        6,
        scratch=(pltpu.VMEM((2 * entries, wide), bf16),),
        flops=2 * batches * points * columns * kept,
        moved=2 * batches * points * columns * 2,
    )(partial, partial_other, point_weights, basis_values, left_t, put)

    clusters, singles = sums[:len(near) + 1], sums[len(near) + 1:]
    landed = []
    for i, dz in enumerate(far):
        joined = singles[i * rows_x].astype(f32)
        for dx in side:
            joined = joined + swap(singles[i * rows_x + dx], "pair", rows_x, dx).astype(f32)
        landed.append(swap(joined.astype(bf16), "batch", rows_z, dz).astype(f32))
    cluster = clusters[0].astype(f32)
    for dz, array in zip(near, clusters[1:]):
        cluster = cluster + swap(array, "batch", rows_z, dz).astype(f32)
    total = cluster[:held]
    for dx in side:
        total = total + swap(cluster[dx * held:(dx + 1) * held].astype(bf16), "pair", rows_x, dx).astype(f32)
    for term in landed:
        total = total + term
    total_other = swap(total, "orb", 2, 1)
    return call(
        finish_kernel, jax.ShapeDtypeStruct((held, square), f32), 3, scalars=1, moved=held * square * 12
    )(half_at, total, total_other, core_blocks)


def solution(mesh):
    placed = (
        P(("groups", "batch", "pair"), None, None),
        P(("groups", "batch", "pair"), None),
        P(("groups", "batch", "pair"), None, "orb"),
        P(("groups", "batch", "pair"), "orb", None, None),
        P(("groups", "batch", "pair"), None),
        P(("groups", "batch", "pair"), None),
    )
    return jax.shard_map(
        per_device,
        mesh=mesh,
        in_specs=placed,
        out_specs=P(("groups", "batch", "pair"), None),
        check_vma=False,
    )
```

```python
import functools

import jax
import jax.numpy as jnp
from jax import lax
from jax.experimental import pallas as pl
from jax.experimental.pallas import tpu as pltpu
from jax.sharding import PartitionSpec as P

GO = 64
VMEM_LIMIT = 50 * 1024 * 1024
NT = (((1,), (1,)), ((), ()))


def split_dot(left, right, dims=None):
    if dims is None:
        return jnp.dot(left, right, preferred_element_type=jnp.float32)
    return lax.dot_general(left, right, dims, preferred_element_type=jnp.float32)


def prepare_kernel(place_ref, half_ref, values_ref, own_ref, other_ref, left_ref, left_t_ref, pick_ref, put_ref):
    batches, points, columns = values_ref.shape
    groups = columns // GO
    kept = left_ref.shape[2]
    first = half_ref[0] * (kept // groups)
    at = lax.broadcasted_iota(jnp.int32, (kept, columns), 0)
    lane = lax.broadcasted_iota(jnp.int32, (kept, columns), 1)
    wanted = (at % groups) * GO + first + at // groups
    select = jnp.where(lane == wanted, 1.0, 0.0).astype(jnp.bfloat16)
    for t in range(batches):
        left_ref[t] = split_dot(values_ref[t], select, NT).astype(jnp.bfloat16)
        left_t_ref[t] = split_dot(select, values_ref[t], NT).astype(jnp.bfloat16)
    hot = row_table(place_ref, half_ref, own_ref, other_ref, put_ref.shape[0])
    pick_ref[...] = hot.T.astype(jnp.bfloat16)
    hot = hot.astype(jnp.bfloat16)
    put_ref[...] = jnp.concatenate([hot, hot], axis=1)


def index_kernel(held, fetch_ref, slots_ref, rows_ref):
    owners, capacity = fetch_ref.shape
    slots = slots_ref[...]
    entries = slots.shape[1]
    owner = slots // capacity
    owner_hot = jnp.where(lax.broadcasted_iota(jnp.int32, (owners, entries), 0) == owner, 1.0, 0.0)
    stored = fetch_ref[...].astype(jnp.float32).T.astype(jnp.bfloat16)
    listed = split_dot(stored, owner_hot.astype(jnp.bfloat16)).astype(jnp.int32)
    at = lax.broadcasted_iota(jnp.int32, (capacity, entries), 0)
    chosen = jnp.where(at == slots - owner * capacity, listed, 0)
    rows_ref[...] = jnp.sum(chosen, axis=0, keepdims=True) + owner * held


def row_table(place_ref, core_ref, own_ref, other_ref, table_rows):
    low = core_ref[0] == 0
    rows = jnp.concatenate(
        [jnp.where(low, own_ref[...], other_ref[...]), jnp.where(low, other_ref[...], own_ref[...])], axis=1
    )
    rows = lax.bitwise_xor(rows, place_ref[0])
    row = lax.broadcasted_iota(jnp.int32, (table_rows, rows.shape[1]), 0)
    return jnp.where(row == rows, 1.0, 0.0)


def density_kernel(places, *refs):
    piece_refs = refs[:len(places)]
    pick_ref, left_ref, values_ref, out_ref, table, dense = refs[len(places):]
    batches, points, columns = values_ref.shape
    groups = columns // GO
    owners = sum(len(blocks) for blocks in places)
    held = table.shape[0] // owners
    for ref, blocks in zip(piece_refs, places):
        table[blocks[0] * held:(blocks[-1] + 1) * held, :] = ref[...]
    pick = pick_ref[...]
    low = lax.broadcasted_iota(jnp.int32, (1, 1, 1, groups, 128), 4) < GO
    for chunk in range(table.shape[1] // 512):
        wide = split_dot(pick, table[:, chunk * 512:(chunk + 1) * 512])
        for j in range(4 * chunk, 4 * chunk + 4):
            got = wide[:, (j % 4) * 128:(j % 4 + 1) * 128].reshape(2, batches, groups // 4, 2, groups, 128)
            even, odd = got[:, :, :, 0], got[:, :, :, 1]
            first = jnp.where(low, even, pltpu.roll(odd, GO, 4))
            second = jnp.where(low, pltpu.roll(even, GO, 4), odd)
            for t in range(batches):
                for q in range(groups // 2):
                    at = (q // (groups // 4), t, q % (groups // 4))
                    both = jnp.concatenate([first[at], second[at]], axis=0)
                    dense[t, j * 2 * groups:(j + 1) * 2 * groups, q * 128:(q + 1) * 128] = both.astype(jnp.bfloat16)
    for t in range(batches):
        product = split_dot(left_ref[t], dense[t]) * values_ref[t].astype(jnp.float32)
        folded = product[:, :128]
        for q in range(1, columns // 128):
            folded = folded + product[:, q * 128:(q + 1) * 128]
        out_ref[t:t + 1, :] = jnp.sum(folded.T, axis=0, keepdims=True)


def scatter_kernel(places, *refs):
    mine_ref, far_ref, weight_ref, values_ref, left_t_ref, put_ref = refs[:6]
    out_refs = refs[6:-1]
    terms = refs[-1]
    target = {k: (ref, i) for ref, blocks in zip(out_refs, places) for i, k in enumerate(blocks)}
    pieces = len(target)
    held = out_refs[0].shape[0] // len(places[0])
    batches, points, columns = values_ref.shape
    groups = columns // GO
    kept = left_t_ref.shape[1]
    steps = kept // (2 * groups)
    entries = batches * groups * groups
    potential = weight_ref[...] * jnp.tanh(mine_ref[...] + far_ref[...])
    low = lax.broadcasted_iota(jnp.int32, (1, groups, 128), 2) < GO
    for t in range(batches):
        factor = jnp.broadcast_to(potential[t:t + 1, :], (128, points)).T
        factor = jnp.concatenate([factor] * (columns // 128), axis=1)
        weighted = (values_ref[t].astype(jnp.float32) * factor).astype(jnp.bfloat16)
        part = split_dot(left_t_ref[t], weighted)
        for q in range(groups // 2):
            cut = part[:, q * 128:(q + 1) * 128].reshape(steps, 2, groups, 128)
            first, second = cut[:, 0], cut[:, 1]
            even = jnp.where(low, first, pltpu.roll(second, GO, 2))
            odd = jnp.where(low, pltpu.roll(first, GO, 2), second)
            side, pair = q // (groups // 4), q % (groups // 4)
            at = ((side * batches + t) * (groups // 2) + 2 * pair) * groups
            for j in range(steps):
                both = jnp.concatenate([even[j], odd[j]], axis=0)
                top = both.astype(jnp.bfloat16)
                terms[at:at + 2 * groups, j * 128:(j + 1) * 128] = top
                left = (both - top.astype(jnp.float32)).astype(jnp.bfloat16)
                terms[entries + at:entries + at + 2 * groups, j * 128:(j + 1) * 128] = left
    step = max(1, min(pieces, 128 // held))
    for k in range(0, pieces, step):
        some = put_ref[k * held:(k + step) * held, :]
        total = split_dot(some, terms[...])
        for i in range(step):
            ref, at = target[k + i]
            ref[at * held:(at + 1) * held, :] = total[i * held:(i + 1) * held, :].astype(jnp.bfloat16)


def finish_kernel(half_ref, mine_ref, other_ref, core_ref, out_ref):
    wide = mine_ref.shape[1]
    own = pl.multiple_of(half_ref[0] * wide, wide)
    far = pl.multiple_of((1 - half_ref[0]) * wide, wide)
    out_ref[:, pl.ds(own, wide)] = core_ref[:, pl.ds(own, wide)].astype(jnp.float32) + mine_ref[...]
    out_ref[:, pl.ds(far, wide)] = core_ref[:, pl.ds(far, wide)].astype(jnp.float32) + other_ref[...]


def call(kernel, outs, count, scratch=(), scalars=0, flops=0, moved=0):
    specs = [pl.BlockSpec(memory_space=pltpu.VMEM)] * count
    specs = [pl.BlockSpec(memory_space=pltpu.SMEM)] * scalars + specs
    out_specs = jax.tree.map(lambda _: pl.BlockSpec(memory_space=pltpu.VMEM), outs)
    return pl.pallas_call(
        kernel,
        out_shape=outs,
        in_specs=specs,
        out_specs=out_specs,
        scratch_shapes=list(scratch),
        compiler_params=pltpu.CompilerParams(vmem_limit_bytes=VMEM_LIMIT),
        cost_estimate=pl.CostEstimate(flops=flops, bytes_accessed=moved, transcendentals=0),
    )


def swap(array, axis, count, step):
    return lax.ppermute(array, axis, [(i, i ^ step) for i in range(count)])


def per_device(basis_values, point_weights, slot_ids, fetch_rows, density_blocks, core_blocks):
    rows_z, rows_x = lax.axis_size("batch"), lax.axis_size("pair")
    z, x, half = lax.axis_index("batch"), lax.axis_index("pair"), lax.axis_index("orb")
    owners = rows_z * rows_x
    batches, points, columns = basis_values.shape
    groups, own_groups = slot_ids.shape[1], slot_ids.shape[2]
    held, square = density_blocks.shape
    capacity = fetch_rows.shape[3]
    wide = square // 2
    table_rows = owners * held
    entries = batches * groups * groups
    kept = columns // 2
    bf16, f32 = jnp.bfloat16, jnp.float32

    own_rows = call(
        functools.partial(index_kernel, held),
        jax.ShapeDtypeStruct((1, batches * own_groups * groups), jnp.int32),
        2,
    )(fetch_rows.reshape(owners, capacity), slot_ids.transpose(0, 2, 1).reshape(1, -1))
    other_rows = swap(own_rows, "orb", 2, 1)

    far = list(range(rows_z // 2, rows_z))
    near = list(range(1, rows_z // 2))
    side = list(range(1, rows_x))

    mine = lax.dynamic_slice_in_dim(density_blocks, half * wide, wide, 1)
    direct = {dz: swap(mine, "batch", rows_z, dz) for dz in far}
    beside = [
        lax.dynamic_slice_in_dim(swap(density_blocks, "pair", rows_x, dx), half * wide, wide, 1) for dx in side
    ]
    *beside, own_rows = lax.optimization_barrier((*beside, own_rows))
    cluster = jnp.concatenate([mine, *beside], axis=0)
    arrays, places = [cluster], [list(range(rows_x))]
    for dz in near:
        arrays.append(swap(cluster, "batch", rows_z, dz))
        places.append(list(range(dz * rows_x, (dz + 1) * rows_x)))
    direct[far[0]], other_rows = lax.optimization_barrier((direct[far[0]], other_rows))
    for dz in far:
        arrays.append(direct[dz])
        places.append([dz * rows_x])
        for dx in side:
            arrays.append(swap(direct[dz], "pair", rows_x, dx))
            places.append([dz * rows_x + dx])

    half_at, _ = lax.optimization_barrier((half.reshape(1).astype(jnp.int32), direct[far[-1]]))
    place = ((z * rows_x + x) * held).reshape(1).astype(jnp.int32)
    left, left_t, pick, put = call(
        prepare_kernel,
        (
            jax.ShapeDtypeStruct((batches, points, kept), bf16),
            jax.ShapeDtypeStruct((batches, kept, points), bf16),
            jax.ShapeDtypeStruct((entries, table_rows), bf16),
            jax.ShapeDtypeStruct((table_rows, 2 * entries), bf16),
        ),
        3,
        scalars=2,
        flops=4 * batches * points * columns * kept,
        moved=3 * batches * points * columns * 2,
    )(place, half_at, basis_values, own_rows, other_rows)


    partial = call(
        functools.partial(density_kernel, places),
        jax.ShapeDtypeStruct((batches, points), f32),
        len(arrays) + 3,
        scratch=(pltpu.VMEM((table_rows, wide), bf16), pltpu.VMEM((batches, kept, columns), bf16)),
        flops=2 * batches * points * columns * kept,
        moved=2 * batches * points * columns * 2,
    )(*arrays, pick, left, basis_values)
    partial_other = swap(partial, "orb", 2, 1)

    out_places = [list(range(dz * rows_x, (dz + 1) * rows_x)) for dz in [0] + near]
    out_places += [[dz * rows_x + dx] for dz in far for dx in [0] + side]
    sums = call(
        functools.partial(scatter_kernel, out_places),
        [jax.ShapeDtypeStruct((held * len(blocks), wide), bf16) for blocks in out_places],
        6,
        scratch=(pltpu.VMEM((2 * entries, wide), bf16),),
        flops=2 * batches * points * columns * kept,
        moved=2 * batches * points * columns * 2,
    )(partial, partial_other, point_weights, basis_values, left_t, put)

    clusters, singles = sums[:len(near) + 1], sums[len(near) + 1:]
    landed = []
    for i, dz in enumerate(far):
        joined = singles[i * rows_x].astype(f32)
        for dx in side:
            joined = joined + swap(singles[i * rows_x + dx], "pair", rows_x, dx).astype(f32)
        landed.append(swap(joined.astype(bf16), "batch", rows_z, dz).astype(f32))
    cluster = clusters[0].astype(f32)
    for dz, array in zip(near, clusters[1:]):
        cluster = cluster + swap(array, "batch", rows_z, dz).astype(f32)
    total = cluster[:held]
    for dx in side:
        total = total + swap(cluster[dx * held:(dx + 1) * held].astype(bf16), "pair", rows_x, dx).astype(f32)
    for term in reversed(landed):
        total = total + term
    total_other = swap(total, "orb", 2, 1)
    return call(
        finish_kernel, jax.ShapeDtypeStruct((held, square), f32), 3, scalars=1, moved=held * square * 12
    )(half_at, total, total_other, core_blocks)


def solution(mesh):
    placed = (
        P(("groups", "batch", "pair"), None, None),
        P(("groups", "batch", "pair"), None),
        P(("groups", "batch", "pair"), None, "orb"),
        P(("groups", "batch", "pair"), "orb", None, None),
        P(("groups", "batch", "pair"), None),
        P(("groups", "batch", "pair"), None),
    )
    return jax.shard_map(
        per_device,
        mesh=mesh,
        in_specs=placed,
        out_specs=P(("groups", "batch", "pair"), None),
        check_vma=False,
    )
```

```python
import functools

import jax
import jax.numpy as jnp
from jax import lax
from jax.experimental import pallas as pl
from jax.experimental.pallas import tpu as pltpu
from jax.sharding import PartitionSpec as P

GO = 64
VMEM_LIMIT = 50 * 1024 * 1024
NT = (((1,), (1,)), ((), ()))


def split_dot(left, right, dims=None):
    if dims is None:
        return jnp.dot(left, right, preferred_element_type=jnp.float32)
    return lax.dot_general(left, right, dims, preferred_element_type=jnp.float32)


def prepare_kernel(place_ref, half_ref, values_ref, own_ref, other_ref, left_ref, left_t_ref, pick_ref, put_ref):
    batches, points, columns = values_ref.shape
    groups = columns // GO
    kept = left_ref.shape[2]
    first = half_ref[0] * (kept // groups)
    at = lax.broadcasted_iota(jnp.int32, (kept, columns), 0)
    lane = lax.broadcasted_iota(jnp.int32, (kept, columns), 1)
    wanted = (at % groups) * GO + first + at // groups
    select = jnp.where(lane == wanted, 1.0, 0.0).astype(jnp.bfloat16)
    for t in range(batches):
        left_ref[t] = split_dot(values_ref[t], select, NT).astype(jnp.bfloat16)
        left_t_ref[t] = split_dot(select, values_ref[t], NT).astype(jnp.bfloat16)
    hot = row_table(place_ref, half_ref, own_ref, other_ref, put_ref.shape[0])
    pick_ref[...] = hot.T.astype(jnp.bfloat16)
    hot = hot.astype(jnp.bfloat16)
    put_ref[...] = jnp.concatenate([hot, hot], axis=1)


def index_kernel(held, fetch_ref, slots_ref, rows_ref):
    owners, capacity = fetch_ref.shape
    slots = slots_ref[...]
    entries = slots.shape[1]
    owner = slots // capacity
    owner_hot = jnp.where(lax.broadcasted_iota(jnp.int32, (owners, entries), 0) == owner, 1.0, 0.0)
    stored = fetch_ref[...].astype(jnp.float32).T.astype(jnp.bfloat16)
    listed = split_dot(stored, owner_hot.astype(jnp.bfloat16)).astype(jnp.int32)
    at = lax.broadcasted_iota(jnp.int32, (capacity, entries), 0)
    chosen = jnp.where(at == slots - owner * capacity, listed, 0)
    rows_ref[...] = jnp.sum(chosen, axis=0, keepdims=True) + owner * held


def row_table(place_ref, core_ref, own_ref, other_ref, table_rows):
    low = core_ref[0] == 0
    rows = jnp.concatenate(
        [jnp.where(low, own_ref[...], other_ref[...]), jnp.where(low, other_ref[...], own_ref[...])], axis=1
    )
    rows = lax.bitwise_xor(rows, place_ref[0])
    row = lax.broadcasted_iota(jnp.int32, (table_rows, rows.shape[1]), 0)
    return jnp.where(row == rows, 1.0, 0.0)


def density_kernel(places, *refs):
    piece_refs = refs[:len(places)]
    pick_ref, left_ref, values_ref, out_ref, table, dense = refs[len(places):]
    batches, points, columns = values_ref.shape
    groups = columns // GO
    owners = sum(len(blocks) for blocks in places)
    held = table.shape[0] // owners
    for ref, blocks in zip(piece_refs, places):
        table[blocks[0] * held:(blocks[-1] + 1) * held, :] = ref[...]
    pick = pick_ref[...]
    low = lax.broadcasted_iota(jnp.int32, (1, 1, 1, groups, 128), 4) < GO
    for chunk in range(table.shape[1] // 512):
        wide = split_dot(pick, table[:, chunk * 512:(chunk + 1) * 512])
        for j in range(4 * chunk, 4 * chunk + 4):
            got = wide[:, (j % 4) * 128:(j % 4 + 1) * 128].reshape(2, batches, groups // 4, 2, groups, 128)
            even, odd = got[:, :, :, 0], got[:, :, :, 1]
            first = jnp.where(low, even, pltpu.roll(odd, GO, 4))
            second = jnp.where(low, pltpu.roll(even, GO, 4), odd)
            for t in range(batches):
                for q in range(groups // 2):
                    at = (q // (groups // 4), t, q % (groups // 4))
                    both = jnp.concatenate([first[at], second[at]], axis=0)
                    dense[t, j * 2 * groups:(j + 1) * 2 * groups, q * 128:(q + 1) * 128] = both.astype(jnp.bfloat16)
    for t in range(batches):
        product = split_dot(left_ref[t], dense[t]) * values_ref[t].astype(jnp.float32)
        folded = product[:, :128]
        for q in range(1, columns // 128):
            folded = folded + product[:, q * 128:(q + 1) * 128]
        out_ref[t:t + 1, :] = jnp.sum(folded.T, axis=0, keepdims=True)


def scatter_kernel(places, *refs):
    mine_ref, far_ref, weight_ref, values_ref, left_t_ref, put_ref = refs[:6]
    out_refs = refs[6:-1]
    terms = refs[-1]
    target = {k: (ref, i) for ref, blocks in zip(out_refs, places) for i, k in enumerate(blocks)}
    pieces = len(target)
    held = out_refs[0].shape[0] // len(places[0])
    batches, points, columns = values_ref.shape
    groups = columns // GO
    kept = left_t_ref.shape[1]
    steps = kept // (2 * groups)
    entries = batches * groups * groups
    potential = weight_ref[...] * jnp.tanh(mine_ref[...] + far_ref[...])
    low = lax.broadcasted_iota(jnp.int32, (1, groups, 128), 2) < GO
    for t in range(batches):
        factor = jnp.broadcast_to(potential[t:t + 1, :], (128, points)).T
        factor = jnp.concatenate([factor] * (columns // 128), axis=1)
        weighted = (values_ref[t].astype(jnp.float32) * factor).astype(jnp.bfloat16)
        part = split_dot(left_t_ref[t], weighted)
        for q in range(groups // 2):
            cut = part[:, q * 128:(q + 1) * 128].reshape(steps, 2, groups, 128)
            first, second = cut[:, 0], cut[:, 1]
            even = jnp.where(low, first, pltpu.roll(second, GO, 2))
            odd = jnp.where(low, pltpu.roll(first, GO, 2), second)
            side, pair = q // (groups // 4), q % (groups // 4)
            at = ((side * batches + t) * (groups // 2) + 2 * pair) * groups
            for j in range(steps):
                both = jnp.concatenate([even[j], odd[j]], axis=0)
                top = both.astype(jnp.bfloat16)
                terms[at:at + 2 * groups, j * 128:(j + 1) * 128] = top
                left = (both - top.astype(jnp.float32)).astype(jnp.bfloat16)
                terms[entries + at:entries + at + 2 * groups, j * 128:(j + 1) * 128] = left
    step = max(1, min(pieces, 128 // held))
    for k in range(0, pieces, step):
        some = put_ref[k * held:(k + step) * held, :]
        total = split_dot(some, terms[...])
        for i in range(step):
            ref, at = target[k + i]
            ref[at * held:(at + 1) * held, :] = total[i * held:(i + 1) * held, :].astype(jnp.bfloat16)


def finish_kernel(half_ref, mine_ref, other_ref, core_ref, out_ref):
    wide = mine_ref.shape[1]
    own = pl.multiple_of(half_ref[0] * wide, wide)
    far = pl.multiple_of((1 - half_ref[0]) * wide, wide)
    out_ref[:, pl.ds(own, wide)] = core_ref[:, pl.ds(own, wide)].astype(jnp.float32) + mine_ref[...]
    out_ref[:, pl.ds(far, wide)] = core_ref[:, pl.ds(far, wide)].astype(jnp.float32) + other_ref[...]


def call(kernel, outs, count, scratch=(), scalars=0, flops=0, moved=0):
    specs = [pl.BlockSpec(memory_space=pltpu.VMEM)] * count
    specs = [pl.BlockSpec(memory_space=pltpu.SMEM)] * scalars + specs
    out_specs = jax.tree.map(lambda _: pl.BlockSpec(memory_space=pltpu.VMEM), outs)
    return pl.pallas_call(
        kernel,
        out_shape=outs,
        in_specs=specs,
        out_specs=out_specs,
        scratch_shapes=list(scratch),
        compiler_params=pltpu.CompilerParams(vmem_limit_bytes=VMEM_LIMIT),
        cost_estimate=pl.CostEstimate(flops=flops, bytes_accessed=moved, transcendentals=0),
    )


def swap(array, axis, count, step):
    return lax.ppermute(array, axis, [(i, i ^ step) for i in range(count)])


def per_device(basis_values, point_weights, slot_ids, fetch_rows, density_blocks, core_blocks):
    rows_z, rows_x = lax.axis_size("batch"), lax.axis_size("pair")
    z, x, half = lax.axis_index("batch"), lax.axis_index("pair"), lax.axis_index("orb")
    owners = rows_z * rows_x
    batches, points, columns = basis_values.shape
    groups, own_groups = slot_ids.shape[1], slot_ids.shape[2]
    held, square = density_blocks.shape
    capacity = fetch_rows.shape[3]
    wide = square // 2
    table_rows = owners * held
    entries = batches * groups * groups
    kept = columns // 2
    bf16, f32 = jnp.bfloat16, jnp.float32

    own_rows = call(
        functools.partial(index_kernel, held),
        jax.ShapeDtypeStruct((1, batches * own_groups * groups), jnp.int32),
        2,
    )(fetch_rows.reshape(owners, capacity), slot_ids.transpose(0, 2, 1).reshape(1, -1))
    other_rows = swap(own_rows, "orb", 2, 1)

    far = list(range(rows_z // 2, rows_z))
    near = list(range(1, rows_z // 2))
    side = list(range(1, rows_x))

    mine = lax.dynamic_slice_in_dim(density_blocks, half * wide, wide, 1)
    direct = {dz: swap(mine, "batch", rows_z, dz) for dz in far}
    beside = [
        lax.dynamic_slice_in_dim(swap(density_blocks, "pair", rows_x, dx), half * wide, wide, 1) for dx in side
    ]
    *beside, own_rows = lax.optimization_barrier((*beside, own_rows))
    cluster = jnp.concatenate([mine, *beside], axis=0)
    arrays, places = [cluster], [list(range(rows_x))]
    for dz in near:
        arrays.append(swap(cluster, "batch", rows_z, dz))
        places.append(list(range(dz * rows_x, (dz + 1) * rows_x)))
    direct[far[-1]], other_rows = lax.optimization_barrier((direct[far[-1]], other_rows))
    for dz in far:
        arrays.append(direct[dz])
        places.append([dz * rows_x])
        for dx in side:
            arrays.append(swap(direct[dz], "pair", rows_x, dx))
            places.append([dz * rows_x + dx])

    half_at, _ = lax.optimization_barrier((half.reshape(1).astype(jnp.int32), direct[far[-1]]))
    place = ((z * rows_x + x) * held).reshape(1).astype(jnp.int32)
    left, left_t, pick, put = call(
        prepare_kernel,
        (
            jax.ShapeDtypeStruct((batches, points, kept), bf16),
            jax.ShapeDtypeStruct((batches, kept, points), bf16),
            jax.ShapeDtypeStruct((entries, table_rows), bf16),
            jax.ShapeDtypeStruct((table_rows, 2 * entries), bf16),
        ),
        3,
        scalars=2,
        flops=4 * batches * points * columns * kept,
        moved=3 * batches * points * columns * 2,
    )(place, half_at, basis_values, own_rows, other_rows)


    partial = call(
        functools.partial(density_kernel, places),
        jax.ShapeDtypeStruct((batches, points), f32),
        len(arrays) + 3,
        scratch=(pltpu.VMEM((table_rows, wide), bf16), pltpu.VMEM((batches, kept, columns), bf16)),
        flops=2 * batches * points * columns * kept,
        moved=2 * batches * points * columns * 2,
    )(*arrays, pick, left, basis_values)
    partial_other = swap(partial, "orb", 2, 1)

    out_places = [list(range(dz * rows_x, (dz + 1) * rows_x)) for dz in [0] + near]
    out_places += [[dz * rows_x + dx] for dz in far for dx in [0] + side]
    sums = call(
        functools.partial(scatter_kernel, out_places),
        [jax.ShapeDtypeStruct((held * len(blocks), wide), bf16) for blocks in out_places],
        6,
        scratch=(pltpu.VMEM((2 * entries, wide), bf16),),
        flops=2 * batches * points * columns * kept,
        moved=2 * batches * points * columns * 2,
    )(partial, partial_other, point_weights, basis_values, left_t, put)

    clusters, singles = sums[:len(near) + 1], sums[len(near) + 1:]
    landed = []
    for i, dz in enumerate(far):
        joined = singles[i * rows_x].astype(f32)
        for dx in side:
            joined = joined + swap(singles[i * rows_x + dx], "pair", rows_x, dx).astype(f32)
        landed.append(swap(joined.astype(bf16), "batch", rows_z, dz).astype(f32))
    cluster = clusters[0].astype(f32)
    for dz, array in zip(near, clusters[1:]):
        cluster = cluster + swap(array, "batch", rows_z, dz).astype(f32)
    total = cluster[:held]
    for dx in side:
        total = total + swap(cluster[dx * held:(dx + 1) * held].astype(bf16), "pair", rows_x, dx).astype(f32)
    for term in reversed(landed):
        total = total + term
    total_other = swap(total, "orb", 2, 1)
    return call(
        finish_kernel, jax.ShapeDtypeStruct((held, square), f32), 3, scalars=1, moved=held * square * 12
    )(half_at, total, total_other, core_blocks)


def solution(mesh):
    placed = (
        P(("groups", "batch", "pair"), None, None),
        P(("groups", "batch", "pair"), None),
        P(("groups", "batch", "pair"), None, "orb"),
        P(("groups", "batch", "pair"), "orb", None, None),
        P(("groups", "batch", "pair"), None),
        P(("groups", "batch", "pair"), None),
    )
    return jax.shard_map(
        per_device,
        mesh=mesh,
        in_specs=placed,
        out_specs=P(("groups", "batch", "pair"), None),
        check_vma=False,
    )
```
